128 devices in a mesh: section: 4 (over x), seq: 32 (over y, z, core).
Axes of the slice: x: 4, y: 4, z: 4, core: 2. Of those that a mesh axis runs over, the one named last changes fastest.
Arguments:
- dna_embed: bfloat16 [3, 8192, 768], P(None, 'seq'), may hold values from -6 to 6
- conv_weight: bfloat16 [4, 768, 5, 768], P('section'), may hold values from -0.125 to 0.125
- interval_starts: int32 [3, 16], replicated, may hold values from 0 to 8191, as said below
- cotangent: bfloat16 [3, 1024, 768], P(None, 'seq'), may hold values from -6 to 6
Outputs:
- weight_grad: float32 [4, 768, 5, 768], P('section', 'seq')
- input_grads: bfloat16 [4, 3, 8192, 768], P('section', None, 'seq')
The draws below stay inside these ranges and needn't reach their ends.
Inputs may be any that keep to these rules, and one draw needn't show every extreme that they name: `interval_starts`: each row begins with 0, rises strictly and ends with 8191; interval j of a window runs from its start up to the next start, the last one to the window's end.
All inputs are finite; a program needn't handle non-finite values.
Results may differ from the reference program's by a relative error of at most 0.023.
Values may be sent and summed in bfloat16 or wider, within the bound.
No kernel may reach another device: no remote copies, remote signals or barrier semaphores. Data moves between devices by JAX's collectives and lax.ppermute only.
A program may use at most 192 MiB of HBM per device.

```python
import jax
import jax.numpy as jnp
from jax import lax

C = 768
ROWS_DEV = 256
WINDOWS = 3
NSEG = 16
LENGTH = 8192
N_SECTION = 4
N_SEQ = 32


def draw_interval_starts(key, part):
    key = jax.random.fold_in(key, 7)
    window_keys = jax.random.split(key, WINDOWS)

    def one_window(window_key):
        shuffled = jax.random.permutation(window_key, LENGTH - 2)[:NSEG - 2] + 1
        ordered = jnp.sort(shuffled.astype(jnp.int32))
        return jnp.concatenate([jnp.zeros((1,), jnp.int32), ordered, jnp.full((1,), LENGTH - 1, jnp.int32)])
    return jax.vmap(one_window)(window_keys).astype(jnp.int32)


def spiked(entries, key, source, target, shards_of, factor):
    owner, partner = [(jnp.arange(entries.shape[axis_at]) // (entries.shape[axis_at] // shards_of)).reshape([-1 if axis == axis_at else 1 for axis in range(entries.ndim)]) for axis_at in (source, target)]
    chosen = jax.random.permutation(key, shards_of)[partner]
    strong = (owner == chosen) | (owner == (partner + shards_of // 2) % shards_of)
    return jnp.where(strong, factor * entries, entries)


def level_of(own_key, shape, cuts, least, top_value):
    loudness = 1.0
    for axis_at, parts in cuts:
        steps = jax.random.uniform(jax.random.fold_in(jax.random.fold_in(own_key, 6), axis_at), (parts,), jnp.float32, least / len(cuts), top_value / len(cuts))
        loudness = loudness * jnp.repeat(jnp.exp(steps), shape[axis_at] // parts).reshape((-1,) + (1,) * (len(shape) - 1 - axis_at))
    return loudness


def normal_values(rng, extent, spread, reach, pieces=(), kind=jnp.bfloat16):
    loudness = level_of(rng, extent, pieces, -0.22, 0.18) if pieces else 1.0
    values = jax.random.normal(rng, extent, jnp.float32) * spread * loudness
    return jnp.minimum(jnp.maximum(values, -reach), reach).astype(kind)


def bell_draw_with(key, shape, deviation, limit, pieces, heavy, held_as=jnp.bfloat16):
    result = deviation * jax.random.normal(key, shape, jnp.float32)
    if pieces:
        result = result * level_of(key, shape, pieces, -0.22, 0.18)
    return jnp.clip(spiked(result, jax.random.fold_in(key, 3), *heavy), -limit, limit).astype(held_as)


def setup_inputs(seed: int = 0) -> dict:
    seeds = jax.random.split(jax.random.key(seed), 5)
    return {
        "dna_embed": bell_draw_with(seeds[0], (WINDOWS, LENGTH, C), 1.0, 6.0, ((1, 32),), (1, 2, 32, 2.75)),
        "conv_weight": normal_values(seeds[1], (N_SECTION, C, 5, C), (5 * C // 2) ** -0.5, 0.125, ((0, 4),)),
        "interval_starts": draw_interval_starts(jax.random.fold_in(seeds[4], 71), 0),
        "cotangent": normal_values(seeds[3], (WINDOWS, LENGTH // 8, C), 1.0, 6.0, ((1, 32),)),
    }


def interval_ids(starts, positions):
    return lax.optimization_barrier(jnp.sum((starts[None, :] <= positions[:, None]).astype(jnp.int32), axis=1))

def tap_masks(starts, first_row, row_total, level_total, stride_scale, inside_rows):
    positions = first_row + jnp.arange(row_total, dtype=jnp.int32)
    base_ids = interval_ids(starts, positions * stride_scale)
    columns = []
    for tap_index in range(5):
        neighbor = positions + (tap_index - 2)
        inside = (neighbor >= 0) & (neighbor < level_total) & inside_rows
        same_interval = interval_ids(starts, jnp.clip(neighbor, 0, level_total - 1) * stride_scale) == base_ids
        columns.append((inside & same_interval).astype(jnp.float32))
    return jnp.stack(columns, axis=1)

def level_forward(extended, weights, tap_mask):
    row_total = tap_mask.shape[0]
    channels = extended.shape[1]
    projected = jnp.dot(extended, weights, preferred_element_type=jnp.float32)
    summed = jnp.zeros((row_total, channels), jnp.float32)
    for tap_index in range(5):
        summed = summed + tap_mask[:, tap_index:tap_index + 1] * projected[tap_index:tap_index + row_total, tap_index * channels:(tap_index + 1) * channels]
    return summed

def tap_rows(pre_grad, tap_mask):
    columns = []
    for tap_index in range(5):
        masked = (pre_grad.astype(jnp.float32) * tap_mask[:, tap_index:tap_index + 1]).astype(jnp.bfloat16)
        columns.append(jnp.pad(masked, ((tap_index, 4 - tap_index), (0, 0))))
    return jnp.concatenate(columns, axis=1)

def reference(dna_embed, conv_weight, interval_starts, cotangent):
    channels = C
    weight_list = [conv_weight[level_index].reshape(channels, 5 * channels) for level_index in range(N_SECTION)]
    weight_sums = [jnp.zeros((channels, 5 * channels), jnp.float32) for level_index in range(N_SECTION)]
    grad_blocks = [[] for level_index in range(N_SECTION)]
    for window in range(WINDOWS):
        starts = interval_starts[window]
        current = dna_embed[window]
        saved = []
        for level_index in range(N_SECTION):
            row_total = current.shape[0]
            tap_mask = tap_masks(starts, 0, row_total, row_total, 2 ** level_index, True)
            extended = jnp.pad(current, ((2, 2), (0, 0)))
            preact = level_forward(extended, weight_list[level_index], tap_mask)
            saved.append((extended, tap_mask, preact))
            if level_index < N_SECTION - 1:
                activation = jax.nn.gelu(preact)
                current = (0.5 * (activation[0::2] + activation[1::2])).astype(jnp.bfloat16)
        upper_grad = None
        for level_index in reversed(range(N_SECTION)):
            extended, tap_mask, preact = saved[level_index]
            row_total = tap_mask.shape[0]
            if level_index == N_SECTION - 1:
                upstream = cotangent[window].astype(jnp.float32)
            else:
                upstream = 0.5 * jnp.repeat(upper_grad.astype(jnp.float32), 2, axis=0)
            pre_grad = jax.vjp(jax.nn.gelu, preact)[1](upstream)[0].astype(jnp.bfloat16)
            stacked = tap_rows(pre_grad, tap_mask)
            weight_sums[level_index] = weight_sums[level_index] + lax.dot_general(extended, stacked, (((0,), (0,)), ((), ())), preferred_element_type=jnp.float32)
            back_ext = lax.dot_general(stacked, weight_list[level_index], (((1,), (1,)), ((), ())), preferred_element_type=jnp.float32)
            upper_grad = back_ext[2:2 + row_total].astype(jnp.bfloat16)
            blocks = upper_grad.reshape(N_SEQ, row_total // N_SEQ, channels)
            padded = jnp.pad(blocks, ((0, 0), (0, ROWS_DEV - row_total // N_SEQ), (0, 0)))
            grad_blocks[level_index].append(padded.reshape(LENGTH, channels))
    weight_grad = jnp.stack([weight_sums[level_index].reshape(channels, 5, channels) for level_index in range(N_SECTION)], axis=0)
    input_grads = jnp.stack([jnp.stack(grad_blocks[level_index], axis=0) for level_index in range(N_SECTION)], axis=0)
    return (weight_grad, input_grads)
```

```python
import functools

import jax
import jax.numpy as jnp
from jax import lax
from jax.experimental import pallas as pl
from jax.experimental.pallas import tpu as pltpu
from jax.sharding import PartitionSpec as P

C = 768
TAPS = 5
AXES = ("section", "seq")
OWN = (256, 128, 64, 32)
HALO = (64, 32, 16, 8)
ROWS = (384, 192, 96, 48)
BACK_HALO = (16, 16, 16, 8)
BACK_ROWS = (288, 160, 96, 48)
SEND_ROWS = (0, 144, 80, 48)
EDGE = 80
CHUNK = 24
LIMIT = 40 * 1024 * 1024
F32 = jnp.float32
BF16 = jnp.bfloat16
ANY = pl.BlockSpec(memory_space=pl.ANY)
SMEM = pl.BlockSpec(memory_space=pltpu.SMEM)


def no_cut(starts, window, positions, level, length):
    cut = positions == length
    for entry in range(starts.shape[1]):
        first = (starts[window, entry] + ((1 << level) - 1)) >> level
        cut = cut | (positions == first)
    return jnp.where(cut, 0.0, 1.0)


def roll_rows(value, by):
    return pltpu.roll(value, by % value.shape[0], 0)


def fill_masks(mask_ref, starts, window, seq, level, halo, rows):
    own = OWN[level]
    length = own * 32
    row = lax.broadcasted_iota(jnp.int32, (rows, 128), 0)
    positions = row + (seq * own - halo)
    inside = jnp.where((positions >= 0) & (positions < length), 1.0, 0.0)
    free = no_cut(starts, window, positions, level, length)
    before = inside * free
    after_free = roll_rows(free, -1)
    after = inside * after_free
    mask_ref[0, 0:rows] = before * roll_rows(free, 1)
    mask_ref[1, 0:rows] = before
    mask_ref[2, 0:rows] = inside
    mask_ref[3, 0:rows] = after
    mask_ref[4, 0:rows] = after * roll_rows(free, -2)


def lanes(index, width):
    return pl.ds(pl.multiple_of(index * width, width), width)


def gelu_and_slope(u):
    scale = 0.7978845608028654
    square = u * u
    bend = jnp.tanh(scale * (u + 0.044715 * square * u))
    half = 0.5 * (1.0 + bend)
    slope = half + 0.5 * u * (1.0 - bend * bend) * (scale * (1.0 + 0.134145 * square))
    return u * half, slope


def stack_inputs(value_ref, mask_ref, stacked_ref, rows):
    def column(index, _):
        tile = value_ref[0:rows, lanes(index, 128)].astype(F32)
        for tap in range(TAPS):
            moved = roll_rows(tile, 2 - tap) if tap != 2 else tile
            stacked_ref[0:rows, pl.ds(pl.multiple_of(tap * C + index * 128, 128), 128)] = (
                moved * mask_ref[tap, 0:rows]
            ).astype(BF16)
        return 0

    lax.fori_loop(0, C // 128, column, 0)


def stack_grads(value_ref, mask_ref, stacked_ref, rows):
    def column(index, _):
        tile = value_ref[0:rows, lanes(index, 128)].astype(F32)
        for tap in range(TAPS):
            moved = tile * mask_ref[tap, 0:rows]
            moved = roll_rows(moved, tap - 2) if tap != 2 else moved
            stacked_ref[0:rows, pl.ds(pl.multiple_of(tap * C + index * 128, 128), 128)] = (
                moved.astype(BF16)
            )
        return 0

    lax.fori_loop(0, C // 128, column, 0)


def conv_columns(stacked_ref, weight_ref, index):
    total = None
    for tap in range(TAPS):
        part = jnp.dot(
            stacked_ref[:, tap * C : (tap + 1) * C],
            weight_ref[:, pl.ds(pl.multiple_of(tap * C + index * 256, 256), 256)],
            preferred_element_type=F32,
        )
        total = part if total is None else total + part
    return total


def back_columns(stacked_ref, weight_ref, index):
    return lax.dot_general(
        stacked_ref[...],
        weight_ref[lanes(index, 256), :],
        (((1,), (1,)), ((), ())),
        preferred_element_type=F32,
    )


def copy_all(pairs, sems, first=0):
    copies = [
        pltpu.make_async_copy(source, target, sems.at[first + place])
        for place, (source, target) in enumerate(pairs)
    ]
    for copy in copies:
        copy.start()
    return copies


def wait_all(copies):
    for copy in copies:
        copy.wait()


def forward_kernel(level, window, info, starts, *refs):
    rows, back = ROWS[level], BACK_ROWS[level]
    skip = HALO[level] - BACK_HALO[level]
    if level == 0:
        x_in, up, down, weight, pooled_out, slope_out = refs[:6]
        rest = refs[6:]
    else:
        x_in, weight, pooled_out, slope_out = refs[:4]
        rest = refs[4:]
    x_v, mask_v, stacked_v, weight_v, act_v, slope_v, pooled_v, sems = rest

    @pl.when(info[0] == level)
    def _():
        if level == 0:
            pairs = [
                (x_in.at[window], x_v.at[pl.ds(64, 256)]),
                (up.at[window, pl.ds(0, 64)], x_v.at[pl.ds(0, 64)]),
                (down.at[window, pl.ds(0, 64)], x_v.at[pl.ds(320, 64)]),
            ]
        else:
            pairs = [(x_in, x_v)]
        arriving = copy_all(pairs, sems)
        loading = copy_all([(weight, weight_v)], sems, 3)
        fill_masks(mask_v, starts, window, info[1], level, HALO[level], rows)
        wait_all(arriving)
        stack_inputs(x_v, mask_v, stacked_v, rows)
        wait_all(loading)

        def block(index, _):
            u = conv_columns(stacked_v, weight_v, index)
            act, slope = gelu_and_slope(u)
            cols = lanes(index, 256)
            slope_v[:, cols] = slope[skip : skip + back]
            for half in range(2):
                act_v[...] = act[:, half * 128 : (half + 1) * 128]
                even = act_v[pl.ds(0, rows // 2, stride=2), :]
                odd = act_v[pl.ds(1, rows // 2, stride=2), :]
                pooled_v[:, pl.ds(pl.multiple_of(index * 256 + half * 128, 128), 128)] = (
                    0.5 * (even + odd)
                ).astype(BF16)
            return 0

        lax.fori_loop(0, C // 256, block, 0)
        wait_all(copy_all([(pooled_v, pooled_out), (slope_v, slope_out)], sems))


def cost(flops, nbytes):
    return pl.CostEstimate(flops=int(flops), bytes_accessed=int(nbytes), transcendentals=0)


def params():
    return pltpu.CompilerParams(vmem_limit_bytes=LIMIT)


def forward_call(level, window, info, starts, weight, *xs):
    rows, back = ROWS[level], BACK_ROWS[level]
    return pl.pallas_call(
        functools.partial(forward_kernel, level, window),
        out_shape=(
            jax.ShapeDtypeStruct((rows // 2, C), BF16),
            jax.ShapeDtypeStruct((back, C), F32),
        ),
        in_specs=[SMEM, SMEM] + [ANY] * (len(xs) + 1),
        out_specs=(ANY, ANY),
        scratch_shapes=[
            pltpu.VMEM((rows, C), BF16),
            pltpu.VMEM((TAPS, rows, 128), F32),
            pltpu.VMEM((rows, TAPS * C), BF16),
            pltpu.VMEM((C, TAPS * C), BF16),
            pltpu.VMEM((rows, 128), F32),
            pltpu.VMEM((back, C), F32),
            pltpu.VMEM((rows // 2, C), BF16),
            pltpu.SemaphoreType.DMA((4,)),
        ],
        compiler_params=params(),
        cost_estimate=cost(2 * rows * C * C * TAPS, 6e6),
        name=f"forward{level}",
    )(info, starts, *xs, weight)


def finish_backward(level, du_v, mask_v, stacked_v, weight_v, full_v, send_v, grad_v):
    rows, own, halo = BACK_ROWS[level], OWN[level], BACK_HALO[level]
    send = SEND_ROWS[level]
    stack_grads(du_v, mask_v, stacked_v, rows)

    def block(index, _):
        full_v[...] = back_columns(stacked_v, weight_v, index)
        cols = lanes(index, 256)
        trim = (rows - send) // 2
        send_v[:, cols] = full_v[trim : trim + send].astype(BF16)
        grad_v[0:own, cols] = full_v[halo : halo + own].astype(BF16)
        return 0

    lax.fori_loop(0, C // 256, block, 0)
    grad_v[own:, :] = jnp.zeros((256 - own, C), BF16)


def own_grads(level, du_v, own_v):
    own, halo = OWN[level], BACK_HALO[level]
    own_v[0:own, :] = du_v[halo : halo + own, :].astype(BF16)
    if own < 256:
        own_v[own:, :] = jnp.zeros((256 - own, C), BF16)


def last_kernel(window, info, starts, x_in, cot, up, down, weight, send_out, grad_out, du_out, *rest):
    x_v, cot_v, mask_v, stacked_v, weight_v, du_v, full_v, send_v, grad_v, own_v, sems = rest
    level, rows = 3, ROWS[3]

    @pl.when(info[0] == level)
    def _():
        arriving = copy_all(
            [
                (x_in, x_v),
                (cot.at[window], cot_v.at[pl.ds(16, 32)]),
                (up.at[window, pl.ds(64, 16)], cot_v.at[pl.ds(0, 16)]),
                (down.at[window, pl.ds(64, 16)], cot_v.at[pl.ds(48, 16)]),
            ],
            sems,
        )
        loading = copy_all([(weight, weight_v)], sems, 4)
        fill_masks(mask_v, starts, window, info[1], level, HALO[level], rows)
        wait_all(arriving)
        stack_inputs(x_v, mask_v, stacked_v, rows)
        wait_all(loading)

        def block(index, _):
            u = conv_columns(stacked_v, weight_v, index)
            _, slope = gelu_and_slope(u)
            cols = lanes(index, 256)
            g = cot_v[:, cols].astype(F32)[8:56]
            du_v[:, cols] = (g * slope).astype(BF16).astype(F32)
            return 0

        lax.fori_loop(0, C // 256, block, 0)
        finish_backward(level, du_v, mask_v, stacked_v, weight_v, full_v, send_v, grad_v)
        own_grads(level, du_v, own_v)
        wait_all(
            copy_all([(send_v, send_out), (grad_v, grad_out), (own_v, du_out)], sems)
        )


def last_call(window, info, starts, weight, x, cot, up, down):
    rows = ROWS[3]
    return pl.pallas_call(
        functools.partial(last_kernel, window),
        out_shape=(
            jax.ShapeDtypeStruct((rows, C), BF16),
            jax.ShapeDtypeStruct((256, C), BF16),
            jax.ShapeDtypeStruct((256, C), BF16),
        ),
        in_specs=[SMEM, SMEM] + [ANY] * 5,
        out_specs=(ANY,) * 3,
        scratch_shapes=[
            pltpu.VMEM((rows, C), BF16),
            pltpu.VMEM((64, C), BF16),
            pltpu.VMEM((TAPS, rows, 128), F32),
            pltpu.VMEM((rows, TAPS * C), BF16),
            pltpu.VMEM((C, TAPS * C), BF16),
            pltpu.VMEM((rows, C), F32),
            pltpu.VMEM((rows, 256), F32),
            pltpu.VMEM((rows, C), BF16),
            pltpu.VMEM((256, C), BF16),
            pltpu.VMEM((256, C), BF16),
            pltpu.SemaphoreType.DMA((5,)),
        ],
        compiler_params=params(),
        cost_estimate=cost(4 * rows * C * C * TAPS, 6e6),
        name="last",
    )(info, starts, x, cot, up, down, weight)


def spread_grads(arrived_v, wide_v, slope_v, du_v, rows):
    def column(index, _):
        cols = lanes(index, 128)
        half = 0.5 * arrived_v[:, cols].astype(F32)
        wide_v[pl.ds(0, rows // 2, stride=2), :] = half
        wide_v[pl.ds(1, rows // 2, stride=2), :] = half
        du_v[:, cols] = (wide_v[...] * slope_v[:, cols]).astype(BF16).astype(F32)
        return 0

    lax.fori_loop(0, C // 128, column, 0)


def backward_kernel(level, window, info, starts, arrived, slope, weight, send_out, grad_out, du_out, *rest):
    (arrived_v, slope_v, wide_v, mask_v, stacked_v, weight_v, du_v, full_v, send_v, grad_v, own_v,
     sems) = rest
    rows = BACK_ROWS[level]

    @pl.when(info[0] == level)
    def _():
        arriving = copy_all([(arrived, arrived_v), (slope, slope_v)], sems)
        loading = copy_all([(weight, weight_v)], sems, 2)
        fill_masks(mask_v, starts, window, info[1], level, BACK_HALO[level], rows)
        wait_all(arriving)
        spread_grads(arrived_v, wide_v, slope_v, du_v, rows)
        wait_all(loading)
        finish_backward(level, du_v, mask_v, stacked_v, weight_v, full_v, send_v, grad_v)
        own_grads(level, du_v, own_v)
        wait_all(
            copy_all([(send_v, send_out), (grad_v, grad_out), (own_v, du_out)], sems)
        )


def backward_call(level, window, info, starts, weight, arrived, slope):
    rows = BACK_ROWS[level]
    return pl.pallas_call(
        functools.partial(backward_kernel, level, window),
        out_shape=(
            jax.ShapeDtypeStruct((SEND_ROWS[level], C), BF16),
            jax.ShapeDtypeStruct((256, C), BF16),
            jax.ShapeDtypeStruct((256, C), BF16),
        ),
        in_specs=[SMEM, SMEM] + [ANY] * 3,
        out_specs=(ANY,) * 3,
        scratch_shapes=[
            pltpu.VMEM((rows // 2, C), BF16),
            pltpu.VMEM((rows, C), F32),
            pltpu.VMEM((rows, 128), F32),
            pltpu.VMEM((TAPS, rows, 128), F32),
            pltpu.VMEM((rows, TAPS * C), BF16),
            pltpu.VMEM((C, TAPS * C), BF16),
            pltpu.VMEM((rows, C), F32),
            pltpu.VMEM((rows, 256), F32),
            pltpu.VMEM((SEND_ROWS[level], C), BF16),
            pltpu.VMEM((256, C), BF16),
            pltpu.VMEM((256, C), BF16),
            pltpu.SemaphoreType.DMA((3,)),
        ],
        compiler_params=params(),
        cost_estimate=cost(2 * rows * C * C * TAPS, 6e6),
        name=f"backward{level}",
    )(info, starts, arrived, slope, weight)


def first_du_kernel(info, arrived, slope, du_out, own_out, arrived_v, slope_v, wide_v, du_v, all_v, own_v, sems):
    rows = BACK_ROWS[0]

    @pl.when(info[0] == 0)
    def _():
        wait_all(copy_all([(arrived, arrived_v), (slope, slope_v)], sems))
        spread_grads(arrived_v, wide_v, slope_v, du_v, rows)
        own_grads(0, du_v, own_v)
        all_v[...] = du_v[...].astype(BF16)
        wait_all(copy_all([(own_v, own_out), (all_v, du_out)], sems))


def first_du_call(info, arrived, slope):
    rows = BACK_ROWS[0]
    return pl.pallas_call(
        first_du_kernel,
        out_shape=(
            jax.ShapeDtypeStruct((rows, C), BF16),
            jax.ShapeDtypeStruct((256, C), BF16),
        ),
        in_specs=[SMEM] + [ANY] * 2,
        out_specs=(ANY,) * 2,
        scratch_shapes=[
            pltpu.VMEM((rows // 2, C), BF16),
            pltpu.VMEM((rows, C), F32),
            pltpu.VMEM((rows, 128), F32),
            pltpu.VMEM((rows, C), F32),
            pltpu.VMEM((rows, C), BF16),
            pltpu.VMEM((256, C), BF16),
            pltpu.SemaphoreType.DMA((2,)),
        ],
        compiler_params=params(),
        cost_estimate=cost(rows * C * 4, 2e6),
        name="first_du",
    )(info, arrived, slope)


def first_grad_kernel(windows, info, starts, *refs):
    du_in = refs[:windows]
    weight, grad_out = refs[windows : windows + 2]
    du_v, mask_v, stacked_v, weight_v, grad_v, sems = refs[windows + 2 :]
    rows = BACK_ROWS[0]

    @pl.when(info[0] == 0)
    def _():
        loading = copy_all([(weight, weight_v)], sems, 0)
        leaving = []
        for window in range(windows):
            wait_all(copy_all([(du_in[window], du_v)], sems, 1))
            fill_masks(mask_v, starts, window, info[1], 0, BACK_HALO[0], rows)
            stack_grads(du_v, mask_v, stacked_v, rows)
            if window == 0:
                wait_all(loading)

            def block(index, _):
                found = back_columns(stacked_v, weight_v, index)
                grad_v[window, :, lanes(index, 256)] = found[16:272].astype(BF16)
                return 0

            lax.fori_loop(0, C // 256, block, 0)
        wait_all(copy_all([(grad_v, grad_out)], sems, 2))


def first_grad_call(info, starts, weight, *du):
    rows = BACK_ROWS[0]
    windows = len(du)
    return pl.pallas_call(
        functools.partial(first_grad_kernel, windows),
        out_shape=jax.ShapeDtypeStruct((windows, 256, C), BF16),
        in_specs=[SMEM, SMEM] + [ANY] * (windows + 1),
        out_specs=ANY,
        scratch_shapes=[
            pltpu.VMEM((rows, C), BF16),
            pltpu.VMEM((TAPS, rows, 128), F32),
            pltpu.VMEM((rows, TAPS * C), BF16),
            pltpu.VMEM((C, TAPS * C), BF16),
            pltpu.VMEM((windows, 256, C), BF16),
            pltpu.SemaphoreType.DMA((3,)),
        ],
        compiler_params=params(),
        cost_estimate=cost(2 * windows * rows * C * C * TAPS, 9e6),
        name="first_grad",
    )(info, starts, *du, weight)


def fill_order(seq, order_ref):
    row = lax.broadcasted_iota(jnp.int32, (C, 128), 0)
    place = (row * 2731) >> 16
    apart = ((place & 15) << 1) | (place >> 4)
    source = CHUNK * (seq ^ apart) + (row - CHUNK * place)
    lane = lax.broadcasted_iota(jnp.int32, (C, 128), 1)
    for index in range(C // 128):
        order_ref[:, index * 128 : (index + 1) * 128] = jnp.where(
            source == lane + index * 128, 1.0, 0.0
        ).astype(BF16)


def side_level(level, window, x_pairs, info, starts, x_v, mask_v, stacked_v, order_v, side_v, sems):
    rows, halo, own = BACK_ROWS[level], BACK_HALO[level], OWN[level]
    wait_all(copy_all(x_pairs, sems))
    fill_masks(mask_v, starts, window, info[1], level, halo, rows)
    stack_inputs(x_v, mask_v, stacked_v, rows)
    width = max(own, 128)

    def tap_block(tap, _):
        part = stacked_v[halo : halo + own, lanes(tap, C)]
        if own < width:
            part = jnp.concatenate([part, jnp.zeros((width - own, C), BF16)], axis=0)
        found = lax.dot_general(
            order_v[...], part, (((1,), (1,)), ((), ())), preferred_element_type=F32
        )
        side_v[pl.ds(pl.multiple_of(tap * C, C), C), window * 256 : window * 256 + width] = (
            found.astype(BF16)
        )
        if width < 256:
            side_v[
                pl.ds(pl.multiple_of(tap * C, C), C), window * 256 + width : (window + 1) * 256
            ] = jnp.zeros((C, 256 - width), BF16)
        return 0

    lax.fori_loop(0, TAPS, tap_block, 0)


def side_kernel(levels, windows, info, starts, *refs):
    count = 3 if levels == (0,) else windows * len(levels)
    inputs = refs[:count]
    side_out = refs[count]
    x_v, mask_v, stacked_v, order_v, side_v, sems = refs[count + 1 :]
    for slot, level in enumerate(levels):
        rows = BACK_ROWS[level]

        @pl.when(info[0] == level)
        def _():
            fill_order(info[1], order_v)
            for window in range(windows):
                if level == 0:
                    x_in, up, down = inputs
                    pairs = [
                        (x_in.at[window], x_v.at[pl.ds(16, 256)]),
                        (up.at[window, pl.ds(48, 16)], x_v.at[pl.ds(0, 16)]),
                        (down.at[window, pl.ds(0, 16)], x_v.at[pl.ds(272, 16)]),
                    ]
                else:
                    skip = HALO[level] - BACK_HALO[level]
                    x_in = inputs[slot * windows + window]
                    pairs = [(x_in.at[pl.ds(skip, rows)], x_v.at[pl.ds(0, rows)])]
                side_level(
                    level, window, pairs, info, starts, x_v, mask_v, stacked_v, order_v, side_v, sems
                )
            wait_all(copy_all([(side_v, side_out)], sems, 3))


def side_call(levels, windows, info, starts, *xs):
    rows = BACK_ROWS[levels[0]]
    return pl.pallas_call(
        functools.partial(side_kernel, levels, windows),
        out_shape=jax.ShapeDtypeStruct((TAPS * C, windows * 256), BF16),
        in_specs=[SMEM, SMEM] + [ANY] * len(xs),
        out_specs=ANY,
        scratch_shapes=[
            pltpu.VMEM((rows, C), BF16),
            pltpu.VMEM((TAPS, rows, 128), F32),
            pltpu.VMEM((rows, TAPS * C), BF16),
            pltpu.VMEM((C, C), BF16),
            pltpu.VMEM((TAPS * C, windows * 256), BF16),
            pltpu.SemaphoreType.DMA((4,)),
        ],
        compiler_params=params(),
        cost_estimate=cost(2 * windows * 256 * C * C * TAPS, 8e6),
        name=f"side{levels[0]}",
    )(info, starts, *xs)


PIECES = (4, 4, 4, 3)


def weight_kernel(quarter, windows, info, *refs):
    count = 4 * windows
    dus = refs[:count]
    side_first, side_other = refs[count : count + 2]
    send_out, keep_out = refs[count + 2 : count + 4]
    du_v, side_v, sems = refs[count + 4 :]
    first = sum(PIECES[:quarter])
    low = first // 3
    high = (first + PIECES[quarter] - 1) // 3 + 1
    rows = pl.ds(low * C, (high - low) * C)

    def fetch(level):
        pairs = [
            (dus[level * windows + window], du_v.at[pl.ds(window * 256, 256)])
            for window in range(windows)
        ]
        source = side_first if level == 0 else side_other
        pairs.append((source.at[rows], side_v))
        wait_all(copy_all(pairs, sems))

    for level in range(4):
        pl.when(info[0] == level)(functools.partial(fetch, level))
    for piece in range(PIECES[quarter]):
        tap, part = divmod(first + piece, 3)
        found = jnp.dot(
            side_v[(tap - low) * C : (tap - low + 1) * C, :],
            du_v[:, part * 256 : (part + 1) * 256],
            preferred_element_type=F32,
        )
        found = found.reshape(2, 16, CHUNK, 256)
        cols = slice(piece * 256, (piece + 1) * 256)
        keep_out[:, :, cols] = found[0].astype(BF16)
        send_out[:, :, cols] = found[1].astype(BF16)


def weight_call(quarter, windows, info, dus, side_first, side_other):
    width = PIECES[quarter] * 256
    first = sum(PIECES[:quarter])
    taps = (first + PIECES[quarter] - 1) // 3 + 1 - first // 3
    whole = pl.BlockSpec(memory_space=pltpu.VMEM)
    shape = jax.ShapeDtypeStruct((16, CHUNK, width), BF16)
    return pl.pallas_call(
        functools.partial(weight_kernel, quarter, windows),
        out_shape=(shape, shape),
        in_specs=[SMEM] + [ANY] * (len(dus) + 2),
        out_specs=(whole, whole),
        scratch_shapes=[
            pltpu.VMEM((windows * 256, C), BF16),
            pltpu.VMEM((taps * C, windows * 256), BF16),
            pltpu.SemaphoreType.DMA((windows + 1,)),
        ],
        compiler_params=params(),
        cost_estimate=cost(2 * C * 768 * width, 5e6),
        name=f"weight{quarter}",
    )(info, *dus, side_first, side_other)


def section_pairs(source, target, shards):
    return [(source * shards + place, target * shards + place) for place in range(shards)]


def apart_pairs(sections, shards, apart):
    return [
        (section * shards + place, section * shards + (place ^ apart))
        for section in range(sections)
        for place in range(shards)
    ]


def add(left, right):
    return (left.astype(F32) + right.astype(F32)).astype(BF16)


def reduce_quarter(send, keep, order, sections, shards):
    def exchange(value, apart):
        return lax.ppermute(value, AXES, apart_pairs(sections, shards, apart))

    width = keep.shape[-1]
    total = add(keep, exchange(send, 1)).reshape(4, 4, CHUNK, width)
    for axis, steps in order:
        unit = 8 if axis == 0 else 2
        one, two = steps

        def pick(place):
            return lax.index_in_dim(total, place, axis, keepdims=True)

        leaving = jnp.concatenate([pick(one), pick(2)], axis=axis)
        staying = jnp.concatenate([pick(0), pick(two)], axis=axis)
        total = add(staying, exchange(leaving, one * unit))
        near = lax.index_in_dim(total, 0, axis, keepdims=True)
        far = lax.index_in_dim(total, 1, axis, keepdims=True)
        total = add(near, exchange(far, two * unit))
    return total.reshape(CHUNK, width)


ORDERS = (
    ((1, (1, 3)), (0, (1, 3))),
    ((1, (3, 1)), (0, (3, 1))),
    ((0, (1, 3)), (1, (1, 3))),
    ((0, (3, 1)), (1, (3, 1))),
)


def body(dna_embed, conv_weight, interval_starts, cotangent):
    windows = dna_embed.shape[0]
    sections = lax.axis_size("section")
    shards = lax.axis_size("seq")
    section_index = lax.axis_index("section")
    seq_index = lax.axis_index("seq")
    info = jnp.stack([section_index, seq_index]).astype(jnp.int32)
    weight = conv_weight[0].reshape(C, TAPS * C)
    starts = interval_starts

    up_pairs = [
        (section * shards + place, section * shards + place + 1)
        for section in range(sections)
        for place in range(shards - 1)
    ]
    down_pairs = [(target, source) for source, target in up_pairs]
    up = lax.ppermute(
        jnp.concatenate([dna_embed[:, 192:], cotangent[:, 16:]], axis=1), AXES, up_pairs
    )
    down = lax.ppermute(
        jnp.concatenate([dna_embed[:, :64], cotangent[:, :16]], axis=1), AXES, down_pairs
    )

    def relay(value, source, target):
        return lax.ppermute(value, AXES, section_pairs(source, target, shards))

    inputs = [[None] * windows for _ in range(4)]
    slopes = [[None] * windows for _ in range(4)]
    grads = [[None] * windows for _ in range(4)]
    dus = [[None] * windows for _ in range(4)]
    wide_du = [None] * windows
    for window in range(windows):
        pooled, slopes[0][window] = forward_call(
            0, window, info, starts, weight, dna_embed, up, down
        )
        inputs[1][window] = relay(pooled, 0, 1)
    tied = lax.optimization_barrier((dna_embed, up, down, pooled))
    side_first = side_call((0,), windows, info, starts, *tied[:3])
    for window in range(windows):
        for level in (1, 2):
            pooled, slopes[level][window] = forward_call(
                level, window, info, starts, weight, inputs[level][window]
            )
            inputs[level + 1][window] = relay(pooled, level, level + 1)
        send, grads[3][window], dus[3][window] = last_call(
            window, info, starts, weight, inputs[3][window], cotangent, up, down
        )
        for level in (2, 1):
            arrived = relay(send, level + 1, level)
            send, grads[level][window], dus[level][window] = backward_call(
                level, window, info, starts, weight, arrived, slopes[level][window]
            )
        arrived = relay(send, 1, 0)
        wide_du[window], dus[0][window] = first_du_call(info, arrived, slopes[0][window])
    others = [inputs[level][window] for level in (1, 2, 3) for window in range(windows)]
    tied = lax.optimization_barrier((*others, send))
    side_other = side_call((1, 2, 3), windows, info, starts, *tied[:-1])
    all_du = [dus[level][window] for level in range(4) for window in range(windows)]
    quarters = []
    for quarter in range(4):
        send, keep = weight_call(quarter, windows, info, all_du, side_first, side_other)
        quarters.append((send, keep))
    tied = lax.optimization_barrier((*wide_du, quarters[-1][0]))
    quarters[-1] = (tied[-1], quarters[-1][1])
    first_grads = first_grad_call(info, starts, weight, *tied[:-1])
    reduced = [
        reduce_quarter(send, keep, order, sections, shards)
        for (send, keep), order in zip(quarters, ORDERS)
    ]
    weight_grad = jnp.concatenate(reduced, axis=1).astype(F32).reshape(1, CHUNK, TAPS, C)
    chosen = first_grads
    for level in (1, 2, 3):
        chosen = jnp.where(section_index == level, jnp.stack(grads[level]), chosen)
    return (weight_grad, chosen[None])


def solution(mesh):
    placed = (P(None, "seq", None), P("section", None, None, None), P(), P(None, "seq", None))
    return jax.shard_map(
        body,
        mesh=mesh,
        in_specs=placed,
        out_specs=(P("section", "seq", None, None), P("section", None, "seq", None)),
        check_vma=False,
    )
```

```python
import functools

import jax
import jax.numpy as jnp
from jax import lax
from jax.experimental import pallas as pl
from jax.experimental.pallas import tpu as pltpu
from jax.sharding import PartitionSpec as P

C = 768
TAPS = 5
AXES = ("section", "seq")
OWN = (256, 128, 64, 32)
HALO = (64, 32, 16, 8)
ROWS = (384, 192, 96, 48)
BACK_HALO = (16, 16, 16, 8)
BACK_ROWS = (288, 160, 96, 48)
SEND_ROWS = (0, 144, 80, 48)
CHUNK = 24
LIMIT = 24 * 1024 * 1024
F32 = jnp.float32
BF16 = jnp.bfloat16
ANY = pl.BlockSpec(memory_space=pl.ANY)
SMEM = pl.BlockSpec(memory_space=pltpu.SMEM)
VMEM = pl.BlockSpec(memory_space=pltpu.VMEM)
PIECES = (4, 4, 4, 3)


def shape_of(*dims, dtype=BF16):
    return jax.ShapeDtypeStruct(dims, dtype)


def call(kernel, name, flops, smem, vmem, outs, token, scratch, aliases=()):
    operands = (*smem, *vmem, token)
    count = len(operands)
    pairs = {len(smem) + place: out for place, out in aliases}
    pairs[count - 1] = len(outs)
    return pl.pallas_call(
        kernel,
        out_shape=(*outs, jax.ShapeDtypeStruct(token.shape, token.dtype)),
        in_specs=[SMEM] * len(smem) + [VMEM] * len(vmem) + [ANY],
        out_specs=(*[VMEM] * len(outs), ANY),
        scratch_shapes=scratch,
        input_output_aliases=pairs,
        compiler_params=pltpu.CompilerParams(vmem_limit_bytes=LIMIT),
        cost_estimate=pl.CostEstimate(flops=int(flops), bytes_accessed=1000000, transcendentals=0),
        name=name,
    )(*operands)


def no_cut(starts, window, positions, level, length):
    cut = positions == length
    for entry in range(starts.shape[1]):
        first = (starts[window, entry] + ((1 << level) - 1)) >> level
        cut = cut | (positions == first)
    return jnp.where(cut, 0.0, 1.0)


def roll_rows(value, by):
    return pltpu.roll(value, by % value.shape[0], 0)


def fill_masks(mask_ref, starts, window, seq, level, halo, rows):
    own = OWN[level]
    length = own * 32
    row = lax.broadcasted_iota(jnp.int32, (rows, 128), 0)
    positions = row + (seq * own - halo)
    inside = jnp.where((positions >= 0) & (positions < length), 1.0, 0.0)
    free = no_cut(starts, window, positions, level, length)
    before = inside * free
    after = inside * roll_rows(free, -1)
    mask_ref[0, 0:rows] = before * roll_rows(free, 1)
    mask_ref[1, 0:rows] = before
    mask_ref[2, 0:rows] = inside
    mask_ref[3, 0:rows] = after
    mask_ref[4, 0:rows] = after * roll_rows(free, -2)


def stack_inputs(read, mask_ref, stacked_ref, rows):
    for index in range(C // 128):
        tile = read(index).astype(F32)
        for tap in range(TAPS):
            moved = roll_rows(tile, 2 - tap) if tap != 2 else tile
            first = tap * C + index * 128
            stacked_ref[0:rows, first : first + 128] = (moved * mask_ref[tap, 0:rows]).astype(BF16)


def stack_grads(value_ref, mask_ref, stacked_ref, rows):
    for index in range(C // 128):
        tile = value_ref[0:rows, index * 128 : (index + 1) * 128].astype(F32)
        for tap in range(TAPS):
            moved = tile * mask_ref[tap, 0:rows]
            moved = roll_rows(moved, tap - 2) if tap != 2 else moved
            first = tap * C + index * 128
            stacked_ref[0:rows, first : first + 128] = moved.astype(BF16)


def conv_columns(stacked_ref, weight_ref, index):
    return jnp.dot(
        stacked_ref[...], weight_ref[:, index * 256 : (index + 1) * 256], preferred_element_type=F32
    )


def back_columns(stacked_ref, weight_ref, index):
    total = None
    for tap in range(TAPS):
        first = tap * C + index * 256
        part = lax.dot_general(
            stacked_ref[:, tap * C : (tap + 1) * C],
            weight_ref[first : first + 256, :],
            (((1,), (1,)), ((), ())),
            preferred_element_type=F32,
        )
        total = part if total is None else total + part
    return total


def gelu_and_slope(u):
    scale = 0.7978845608028654
    square = u * u
    bend = jnp.tanh(scale * (u + 0.044715 * square * u))
    half = 0.5 * (1.0 + bend)
    slope = half + 0.5 * u * (1.0 - bend * bend) * (scale * (1.0 + 0.134145 * square))
    return u * half, slope


def forward_kernel(level, window, info, starts, *refs):
    rows, back = ROWS[level], BACK_ROWS[level]
    skip = HALO[level] - BACK_HALO[level]
    inputs = 3 if level == 0 else 1
    xs = refs[:inputs]
    weight, _, pooled_out, slope_out, _, mask_v, stacked_v, act_v = refs[inputs:]

    def read(index):
        cols = slice(index * 128, (index + 1) * 128)
        if level == 0:
            x_in, up, down = xs
            return jnp.concatenate(
                [up[window, 0:64, cols], x_in[window, :, cols], down[window, 0:64, cols]], axis=0
            )
        return xs[0][:, cols]

    @pl.when(info[0] == level)
    def _():
        fill_masks(mask_v, starts, window, info[1], level, HALO[level], rows)
        stack_inputs(read, mask_v, stacked_v, rows)
        for index in range(C // 256):
            act, slope = gelu_and_slope(conv_columns(stacked_v, weight, index))
            slope_out[:, index * 256 : (index + 1) * 256] = slope[skip : skip + back]
            for half in range(2):
                place = index * 2 + half
                act_v[place] = act[:, half * 128 : (half + 1) * 128]
                even = act_v[place, pl.ds(0, rows // 2, stride=2), :]
                odd = act_v[place, pl.ds(1, rows // 2, stride=2), :]
                pooled_out[:, place * 128 : (place + 1) * 128] = (0.5 * (even + odd)).astype(BF16)


def forward_call(level, window, info, starts, weight, token, *xs):
    rows, back = ROWS[level], BACK_ROWS[level]
    return call(
        functools.partial(forward_kernel, level, window),
        f"forward{level}",
        2 * rows * C * C * TAPS,
        (info, starts),
        (*xs, weight),
        (shape_of(rows // 2, C), shape_of(back, C, dtype=F32)),
        token,
        [
            pltpu.VMEM((TAPS, rows, 128), F32),
            pltpu.VMEM((rows, TAPS * C), BF16),
            pltpu.VMEM((C // 128, rows, 128), F32),
        ],
    )


def finish_backward(level, du_v, mask_v, stacked_v, weight, send_out, grad_out):
    rows, own, halo = BACK_ROWS[level], OWN[level], BACK_HALO[level]
    send = SEND_ROWS[level]
    trim = (rows - send) // 2
    stack_grads(du_v, mask_v, stacked_v, rows)
    for index in range(C // 256):
        found = back_columns(stacked_v, weight, index)
        cols = slice(index * 256, (index + 1) * 256)
        if send:
            send_out[:, cols] = found[trim : trim + send].astype(BF16)
        grad_out[0:own, cols] = found[halo : halo + own].astype(BF16)
    if own < 256:
        grad_out[own:, :] = jnp.zeros((256 - own, C), BF16)


def own_grads(level, du_v, du_out):
    own, halo = OWN[level], BACK_HALO[level]
    du_out[0:own, :] = du_v[halo : halo + own, :].astype(BF16)
    if own < 256:
        du_out[own:, :] = jnp.zeros((256 - own, C), BF16)


def last_kernel(window, info, starts, x_in, cot, up, down, weight, _, send_out, grad_out, du_out,
                _out, mask_v, stacked_v, du_v):
    level, rows = 3, ROWS[3]

    @pl.when(info[0] == level)
    def _():
        fill_masks(mask_v, starts, window, info[1], level, HALO[level], rows)
        stack_inputs(
            lambda index: x_in[:, index * 128 : (index + 1) * 128], mask_v, stacked_v, rows
        )
        for index in range(C // 256):
            _, slope = gelu_and_slope(conv_columns(stacked_v, weight, index))
            cols = slice(index * 256, (index + 1) * 256)
            g = jnp.concatenate(
                [
                    up[window, 64:80, cols].astype(F32)[8:16],
                    cot[window, :, cols].astype(F32),
                    down[window, 64:80, cols].astype(F32)[0:8],
                ],
                axis=0,
            )
            du_v[:, cols] = (g * slope).astype(BF16).astype(F32)
        finish_backward(level, du_v, mask_v, stacked_v, weight, send_out, grad_out)
        own_grads(level, du_v, du_out)


def last_call(window, info, starts, weight, token, x, cot, up, down):
    rows = ROWS[3]
    return call(
        functools.partial(last_kernel, window),
        "last",
        4 * rows * C * C * TAPS,
        (info, starts),
        (x, cot, up, down, weight),
        (shape_of(rows, C), shape_of(256, C), shape_of(256, C)),
        token,
        [
            pltpu.VMEM((TAPS, rows, 128), F32),
            pltpu.VMEM((rows, TAPS * C), BF16),
            pltpu.VMEM((rows, C), F32),
        ],
    )


def spread_grads(arrived, wide_v, slope, du_v, rows):
    for index in range(C // 128):
        cols = slice(index * 128, (index + 1) * 128)
        half = 0.5 * arrived[:, cols].astype(F32)
        wide_v[index, pl.ds(0, rows // 2, stride=2), :] = half
        wide_v[index, pl.ds(1, rows // 2, stride=2), :] = half
        du_v[:, cols] = (wide_v[index] * slope[:, cols]).astype(BF16).astype(F32)


def backward_kernel(level, window, info, starts, arrived, slope, weight, _grad, _du, _token,
                    send_out, grad_out, du_out, _out, wide_v, mask_v, stacked_v, du_v):
    rows = BACK_ROWS[level]

    @pl.when(info[0] == level)
    def _():
        fill_masks(mask_v, starts, window, info[1], level, BACK_HALO[level], rows)
        spread_grads(arrived, wide_v, slope, du_v, rows)
        finish_backward(level, du_v, mask_v, stacked_v, weight, send_out, grad_out)
        own_grads(level, du_v, du_out)


def backward_call(level, window, info, starts, weight, token, arrived, slope, grad, du):
    rows = BACK_ROWS[level]
    return call(
        functools.partial(backward_kernel, level, window),
        f"backward{level}",
        2 * rows * C * C * TAPS,
        (info, starts),
        (arrived, slope, weight, grad, du),
        (shape_of(SEND_ROWS[level], C), shape_of(256, C), shape_of(256, C)),
        token,
        [
            pltpu.VMEM((C // 128, rows, 128), F32),
            pltpu.VMEM((TAPS, rows, 128), F32),
            pltpu.VMEM((rows, TAPS * C), BF16),
            pltpu.VMEM((rows, C), F32),
        ],
        aliases=((3, 1), (4, 2)),
    )


def first_du_kernel(info, arrived, slope, _du, _token, all_out, du_out, _out, wide_v, du_v):
    rows = BACK_ROWS[0]

    @pl.when(info[0] == 0)
    def _():
        spread_grads(arrived, wide_v, slope, du_v, rows)
        own_grads(0, du_v, du_out)
        all_out[...] = du_v[...].astype(BF16)


def first_du_call(info, token, arrived, slope, du):
    rows = BACK_ROWS[0]
    return call(
        first_du_kernel,
        "first_du",
        rows * C * 8,
        (info,),
        (arrived, slope, du),
        (shape_of(rows, C), shape_of(256, C)),
        token,
        [pltpu.VMEM((C // 128, rows, 128), F32), pltpu.VMEM((rows, C), F32)],
        aliases=((2, 1),),
    )


def first_grad_kernel(window, info, starts, du, weight, _grad, _token, grad_out, _out, mask_v,
                      stacked_v):
    rows = BACK_ROWS[0]

    @pl.when(info[0] == 0)
    def _():
        fill_masks(mask_v, starts, window, info[1], 0, BACK_HALO[0], rows)
        finish_backward(0, du, mask_v, stacked_v, weight, None, grad_out)


def first_grad_call(window, info, starts, weight, token, du, grad):
    rows = BACK_ROWS[0]
    return call(
        functools.partial(first_grad_kernel, window),
        "first_grad",
        2 * rows * C * C * TAPS,
        (info, starts),
        (du, weight, grad),
        (shape_of(256, C),),
        token,
        [pltpu.VMEM((TAPS, rows, 128), F32), pltpu.VMEM((rows, TAPS * C), BF16)],
        aliases=((2, 0),),
    )


def fill_order(seq, order_ref):
    row = lax.broadcasted_iota(jnp.int32, (C, 128), 0)
    place = (row * 2731) >> 16
    apart = ((place & 15) << 1) | (place >> 4)
    source = CHUNK * (seq ^ apart) + (row - CHUNK * place)
    lane = lax.broadcasted_iota(jnp.int32, (C, 128), 1)
    for index in range(C // 128):
        order_ref[:, index * 128 : (index + 1) * 128] = jnp.where(
            source == lane + index * 128, 1.0, 0.0
        ).astype(BF16)


def side_kernel(level, windows, info, starts, *refs):
    rows, halo, own = BACK_ROWS[level], BACK_HALO[level], OWN[level]
    inputs = 3 if level == 0 else windows
    xs = refs[:inputs]
    rest = refs[inputs + (1 if level == 0 else 2) :]
    side_out, _, mask_v, stacked_v, order_v = rest
    width = max(own, 128)
    skip = HALO[level] - halo

    @pl.when(info[0] == level)
    def _():
        fill_order(info[1], order_v)
        for window in range(windows):

            def read(index):
                cols = slice(index * 128, (index + 1) * 128)
                if level == 0:
                    x_in, up, down = xs
                    return jnp.concatenate(
                        [up[window, 48:64, cols], x_in[window, :, cols], down[window, 0:16, cols]],
                        axis=0,
                    )
                return xs[window][skip : skip + rows, cols]

            fill_masks(mask_v, starts, window, info[1], level, halo, rows)
            stack_inputs(read, mask_v, stacked_v, rows)
            for tap in range(TAPS):
                part = stacked_v[halo : halo + own, tap * C : (tap + 1) * C]
                if own < width:
                    part = jnp.concatenate([part, jnp.zeros((width - own, C), BF16)], axis=0)
                found = lax.dot_general(
                    order_v[...], part, (((1,), (1,)), ((), ())), preferred_element_type=F32
                )
                lines = slice(tap * C, (tap + 1) * C)
                side_out[lines, window * 256 : window * 256 + width] = found.astype(BF16)
                if width < 256:
                    side_out[lines, window * 256 + width : (window + 1) * 256] = jnp.zeros(
                        (C, 256 - width), BF16
                    )


def side_call(level, windows, info, starts, token, side, *xs):
    rows = BACK_ROWS[level]
    held = () if side is None else (side,)
    return call(
        functools.partial(side_kernel, level, windows),
        f"side{level}",
        2 * windows * 256 * C * C * TAPS,
        (info, starts),
        (*xs, *held),
        (shape_of(TAPS * C, windows * 256),),
        token,
        [
            pltpu.VMEM((TAPS, rows, 128), F32),
            pltpu.VMEM((rows, TAPS * C), BF16),
            pltpu.VMEM((C, C), BF16),
        ],
        aliases=() if side is None else ((len(xs), 0),),
    )


def weight_kernel(quarter, side, *refs):
    dus = refs[:-4]
    _, send_out, keep_out, _ = refs[-4:]
    first = sum(PIECES[:quarter])
    for piece in range(PIECES[quarter]):
        tap, part = divmod(first + piece, 3)
        found = None
        for window, du in enumerate(dus):
            term = jnp.dot(
                side[tap * C : (tap + 1) * C, window * 256 : (window + 1) * 256],
                du[:, part * 256 : (part + 1) * 256],
                preferred_element_type=F32,
            )
            found = term if found is None else found + term
        found = found.reshape(2, 16, CHUNK, 256)
        cols = slice(piece * 256, (piece + 1) * 256)
        keep_out[:, :, cols] = found[0].astype(BF16)
        send_out[:, :, cols] = found[1].astype(BF16)


def weight_call(quarter, token, side, dus):
    width = PIECES[quarter] * 256
    shape = shape_of(16, CHUNK, width)
    return call(
        functools.partial(weight_kernel, quarter),
        f"weight{quarter}",
        2 * C * 768 * width,
        (),
        (side, *dus),
        (shape, shape),
        token,
        [],
    )


def quarter_plan(first_axis, steps):
    one, two = steps
    held = [(y, z) for y in range(4) for z in range(4)]
    plan = []
    for axis in (first_axis, 1 - first_axis):
        unit = (8, 2)[axis]
        for apart, gone in ((one, (one, 2)), (two, (two,))):
            leaving = [place for place in held if place[axis] in gone]
            leaving.sort(key=lambda place: (place[1 - axis], gone.index(place[axis])))
            staying = []
            for place in leaving:
                moved = list(place)
                moved[axis] ^= apart
                staying.append(tuple(moved))
            plan.append(
                (
                    apart * unit,
                    [held.index(place) for place in leaving],
                    [held.index(place) for place in staying],
                )
            )
            held = staying
    return plan


PLANS = (
    quarter_plan(1, (1, 3)),
    quarter_plan(1, (3, 1)),
    quarter_plan(0, (1, 3)),
    quarter_plan(0, (3, 1)),
)


def add_kernel(step, *refs):
    keeps, arriveds = refs[0:4], refs[4:8]
    stays, leaves = refs[9:13], refs[13:17]
    for quarter in range(4):
        _, leaving, staying = PLANS[quarter][step]
        for place, source in enumerate(staying):
            stays[quarter][place] = (
                keeps[quarter][source].astype(F32) + arriveds[quarter][source].astype(F32)
            ).astype(BF16)
        for place, source in enumerate(leaving):
            leaves[quarter][place] = (
                keeps[quarter][source].astype(F32) + arriveds[quarter][source].astype(F32)
            ).astype(BF16)


def add_call(step, token, keeps, arriveds):
    half = len(PLANS[0][step][1])
    shapes = tuple(shape_of(half, CHUNK, keep.shape[-1]) for keep in keeps)
    return call(
        functools.partial(add_kernel, step),
        f"add{step}",
        4000000 // (1 << step),
        (),
        (*keeps, *arriveds),
        shapes + shapes,
        token,
        [],
    )


def final_kernel(*refs):
    keeps, arriveds, out = refs[0:4], refs[4:8], refs[9]
    for quarter in range(4):
        first = sum(PIECES[:quarter])
        total = keeps[quarter][0].astype(F32) + arriveds[quarter][0].astype(F32)
        total = total.astype(BF16).astype(F32)
        for piece in range(PIECES[quarter]):
            tap, part = divmod(first + piece, 3)
            out[tap, :, part * 256 : (part + 1) * 256] = total[:, piece * 256 : (piece + 1) * 256]


def section_pairs(source, target, shards):
    return [(source * shards + place, target * shards + place) for place in range(shards)]


def apart_pairs(sections, shards, apart):
    return [
        (section * shards + place, section * shards + (place ^ apart))
        for section in range(sections)
        for place in range(shards)
    ]


def body(dna_embed, conv_weight, interval_starts, cotangent):
    windows = dna_embed.shape[0]
    sections = lax.axis_size("section")
    shards = lax.axis_size("seq")
    section_index = lax.axis_index("section")
    seq_index = lax.axis_index("seq")
    info = jnp.stack([section_index, seq_index]).astype(jnp.int32)
    weight = jnp.transpose(conv_weight[0], (1, 0, 2)).reshape(TAPS * C, C)
    starts = interval_starts
    token = jnp.zeros((8, 128), F32)

    up_pairs = [
        (section * shards + place, section * shards + place + 1)
        for section in range(sections)
        for place in range(shards - 1)
    ]
    down_pairs = [(target, source) for source, target in up_pairs]
    up = lax.ppermute(
        jnp.concatenate([dna_embed[:, 192:], cotangent[:, 16:]], axis=1), AXES, up_pairs
    )
    down = lax.ppermute(
        jnp.concatenate([dna_embed[:, :64], cotangent[:, :16]], axis=1), AXES, down_pairs
    )

    def relay(value, source, target):
        return lax.ppermute(value, AXES, section_pairs(source, target, shards))

    inputs = [[None] * windows for _ in range(4)]
    slopes = [[None] * windows for _ in range(4)]
    grads = [None] * windows
    dus = [None] * windows
    wide_du = [None] * windows
    arrived = [None] * windows
    side = None

    def forward(level, window):
        nonlocal token
        xs = (dna_embed, up, down) if level == 0 else (inputs[level][window],)
        pooled, slopes[level][window], token = forward_call(
            level, window, info, starts, weight, token, *xs
        )
        inputs[level + 1][window] = relay(pooled, level, level + 1)

    def turn(window):
        nonlocal token
        send, grads[window], dus[window], token = last_call(
            window, info, starts, weight, token, inputs[3][window], cotangent, up, down
        )
        arrived[window] = relay(send, 3, 2)

    def backward(level, window):
        nonlocal token
        send, grads[window], dus[window], token = backward_call(
            level, window, info, starts, weight, token, arrived[window], slopes[level][window],
            grads[window], dus[window],
        )
        arrived[window] = relay(send, level, level - 1)

    def arrive(window):
        nonlocal token
        wide_du[window], dus[window], token = first_du_call(
            info, token, arrived[window], slopes[0][window], dus[window]
        )

    def first_grad(window):
        nonlocal token
        grads[window], token = first_grad_call(
            window, info, starts, weight, token, wide_du[window], grads[window]
        )

    def sideways(level):
        nonlocal side, token
        xs = (dna_embed, up, down) if level == 0 else inputs[level]
        side, token = side_call(level, windows, info, starts, token, side, *xs)

    forward(0, 0)
    forward(0, 1)
    forward(0, 2)
    sideways(0)
    forward(1, 0)
    forward(1, 1)
    forward(2, 0)
    forward(1, 2)
    sideways(1)
    forward(2, 1)
    turn(0)
    forward(2, 2)
    turn(1)
    backward(2, 0)
    turn(2)
    sideways(3)
    backward(2, 1)
    backward(1, 0)
    backward(2, 2)
    sideways(2)
    backward(1, 1)
    arrive(0)
    first_grad(0)
    backward(1, 2)
    arrive(1)
    first_grad(1)
    arrive(2)

    keeps, arriveds = [], []
    for quarter in range(4):
        send, keep, token = weight_call(quarter, token, side, dus)
        keeps.append(keep)
        arriveds.append(lax.ppermute(send, AXES, apart_pairs(sections, shards, 1)))
    for step in range(4):
        *parts, token = add_call(step, token, keeps, arriveds)
        keeps = parts[:4]
        arriveds = [
            lax.ppermute(leaving, AXES, apart_pairs(sections, shards, PLANS[quarter][step][0]))
            for quarter, leaving in enumerate(parts[4:])
        ]
        if step == 0:
            first_grad(2)
    weight_grad, token = call(
        final_kernel, "final", 1000000, (), (*keeps, *arriveds),
        (shape_of(TAPS, CHUNK, C, dtype=F32),), token, [],
    )
    weight_grad = jnp.transpose(weight_grad, (1, 0, 2))[None]
    return (weight_grad, jnp.stack(grads)[None])


def solution(mesh):
    placed = (P(None, "seq", None), P("section", None, None, None), P(), P(None, "seq", None))
    return jax.shard_map(
        body,
        mesh=mesh,
        in_specs=placed,
        out_specs=(P("section", "seq", None, None), P("section", None, "seq", None)),
        check_vma=False,
    )
```

```python
import functools

import jax
import jax.numpy as jnp
from jax import lax
from jax.experimental import pallas as pl
from jax.experimental.pallas import tpu as pltpu
from jax.sharding import PartitionSpec as P

C = 768
TAPS = 5
AXES = ("section", "seq")
OWN = (256, 128, 64, 32)
HALO = (64, 32, 16, 8)
ROWS = (384, 192, 96, 48)
BACK_HALO = (16, 16, 16, 8)
BACK_ROWS = (288, 160, 96, 48)
SEND_ROWS = (0, 144, 80, 48)
CHUNK = 24
LIMIT = 24 * 1024 * 1024
F32 = jnp.float32
BF16 = jnp.bfloat16
ANY = pl.BlockSpec(memory_space=pl.ANY)
SMEM = pl.BlockSpec(memory_space=pltpu.SMEM)
VMEM = pl.BlockSpec(memory_space=pltpu.VMEM)
PIECES = (4, 4, 4, 3)


def shape_of(*dims, dtype=BF16):
    return jax.ShapeDtypeStruct(dims, dtype)


def call(kernel, name, flops, smem, vmem, outs, token, scratch, aliases=()):
    operands = (*smem, *vmem, token)
    count = len(operands)
    pairs = {len(smem) + place: out for place, out in aliases}
    pairs[count - 1] = len(outs)
    return pl.pallas_call(
        kernel,
        out_shape=(*outs, jax.ShapeDtypeStruct(token.shape, token.dtype)),
        in_specs=[SMEM] * len(smem) + [VMEM] * len(vmem) + [ANY],
        out_specs=(*[VMEM] * len(outs), ANY),
        scratch_shapes=scratch,
        input_output_aliases=pairs,
        compiler_params=pltpu.CompilerParams(vmem_limit_bytes=LIMIT),
        cost_estimate=pl.CostEstimate(flops=1, bytes_accessed=1, transcendentals=0),
        name=name,
    )(*operands)


def no_cut(starts, window, positions, level, length):
    cut = positions == length
    for entry in range(starts.shape[1]):
        first = (starts[window, entry] + ((1 << level) - 1)) >> level
        cut = cut | (positions == first)
    return jnp.where(cut, 0.0, 1.0)


def roll_rows(value, by):
    return pltpu.roll(value, by % value.shape[0], 0)


def fill_masks(mask_ref, starts, window, seq, level, halo, rows):
    own = OWN[level]
    length = own * 32
    row = lax.broadcasted_iota(jnp.int32, (rows, 128), 0)
    positions = row + (seq * own - halo)
    inside = jnp.where((positions >= 0) & (positions < length), 1.0, 0.0)
    free = no_cut(starts, window, positions, level, length)
    before = inside * free
    after = inside * roll_rows(free, -1)
    mask_ref[0, 0:rows] = before * roll_rows(free, 1)
    mask_ref[1, 0:rows] = before
    mask_ref[2, 0:rows] = inside
    mask_ref[3, 0:rows] = after
    mask_ref[4, 0:rows] = after * roll_rows(free, -2)


def stack_inputs(read, mask_ref, stacked_ref, rows):
    for index in range(C // 128):
        tile = read(index).astype(F32)
        for tap in range(TAPS):
            moved = roll_rows(tile, 2 - tap) if tap != 2 else tile
            first = tap * C + index * 128
            stacked_ref[0:rows, first : first + 128] = (moved * mask_ref[tap, 0:rows]).astype(BF16)


def stack_grads(value_ref, mask_ref, stacked_ref, rows):
    for index in range(C // 128):
        tile = value_ref[0:rows, index * 128 : (index + 1) * 128].astype(F32)
        for tap in range(TAPS):
            moved = tile * mask_ref[tap, 0:rows]
            moved = roll_rows(moved, tap - 2) if tap != 2 else moved
            first = tap * C + index * 128
            stacked_ref[0:rows, first : first + 128] = moved.astype(BF16)


def conv_columns(stacked_ref, weight_ref, index):
    return jnp.dot(
        stacked_ref[...], weight_ref[:, index * 256 : (index + 1) * 256], preferred_element_type=F32
    )


def back_columns(stacked_ref, weight_ref, index):
    total = None
    for tap in range(TAPS):
        first = tap * C + index * 256
        part = lax.dot_general(
            stacked_ref[:, tap * C : (tap + 1) * C],
            weight_ref[first : first + 256, :],
            (((1,), (1,)), ((), ())),
            preferred_element_type=F32,
        )
        total = part if total is None else total + part
    return total


def gelu_and_slope(u):
    scale = 0.7978845608028654
    square = u * u
    bend = jnp.tanh(scale * (u + 0.044715 * square * u))
    half = 0.5 * (1.0 + bend)
    slope = half + 0.5 * u * (1.0 - bend * bend) * (scale * (1.0 + 0.134145 * square))
    return u * half, slope


def first_edges_kernel(info, dna, _, up0, down0, _out):
    @pl.when(info[0] == 0)
    def _():
        up0[...] = dna[0, OWN[0] - 64 :, :]
        down0[...] = dna[0, 0:64, :]


def rest_edges_kernel(windows, info, dna, cot, _, up_rest, down_rest, _out):
    @pl.when(info[0] == 0)
    def _():
        for window in range(1, windows):
            rows = slice((window - 1) * 64, window * 64)
            up_rest[rows, :] = dna[window, OWN[0] - 64 :, :]
            down_rest[rows, :] = dna[window, 0:64, :]

    @pl.when(info[0] == 3)
    def _():
        for window in range(windows):
            rows = slice(window * 16, window * 16 + 16)
            up_rest[rows, :] = cot[window, 16:32, :]
            down_rest[rows, :] = cot[window, 0:16, :]


def first_edges_call(info, token, dna):
    edge = shape_of(64, C)
    return call(first_edges_kernel, "first_edges", 1, (info,), (dna,), (edge, edge), token, [])


def rest_edges_call(info, token, dna, cot):
    windows = dna.shape[0]
    rest = shape_of((windows - 1) * 64, C)
    return call(
        functools.partial(rest_edges_kernel, windows),
        "rest_edges",
        1,
        (info,),
        (dna, cot),
        (rest, rest),
        token,
        [],
    )


def halo_rows(window):
    return 0 if window == 0 else (window - 1) * 64


def forward_kernel(level, window, info, starts, *refs):
    rows, back = ROWS[level], BACK_ROWS[level]
    skip = HALO[level] - BACK_HALO[level]
    inputs = 3 if level == 0 else 1
    xs = refs[:inputs]
    weight, _, pooled_out, slope_out, _, mask_v, stacked_v, act_v = refs[inputs:]

    def read(index):
        cols = slice(index * 128, (index + 1) * 128)
        if level == 0:
            x_in, up, down = xs
            first = halo_rows(window)
            return jnp.concatenate(
                [up[first : first + 64, cols], x_in[window, :, cols], down[first : first + 64, cols]],
                axis=0,
            )
        return xs[0][:, cols]

    @pl.when(info[0] == level)
    def _():
        fill_masks(mask_v, starts, window, info[1], level, HALO[level], rows)
        stack_inputs(read, mask_v, stacked_v, rows)
        for index in range(C // 256):
            act, slope = gelu_and_slope(conv_columns(stacked_v, weight, index))
            slope_out[:, index * 256 : (index + 1) * 256] = slope[skip : skip + back]
            for half in range(2):
                place = index * 2 + half
                act_v[place] = act[:, half * 128 : (half + 1) * 128]
                even = act_v[place, pl.ds(0, rows // 2, stride=2), :]
                odd = act_v[place, pl.ds(1, rows // 2, stride=2), :]
                pooled_out[:, place * 128 : (place + 1) * 128] = (0.5 * (even + odd)).astype(BF16)


def forward_call(level, window, info, starts, weight, token, *xs):
    rows, back = ROWS[level], BACK_ROWS[level]
    return call(
        functools.partial(forward_kernel, level, window),
        f"forward{level}",
        2 * rows * C * C * TAPS,
        (info, starts),
        (*xs, weight),
        (shape_of(rows // 2, C), shape_of(back, C, dtype=F32)),
        token,
        [
            pltpu.VMEM((TAPS, rows, 128), F32),
            pltpu.VMEM((rows, TAPS * C), BF16),
            pltpu.VMEM((C // 128, rows, 128), F32),
        ],
    )


def finish_backward(level, du_v, mask_v, stacked_v, weight, send_out, grad_out):
    rows, own, halo = BACK_ROWS[level], OWN[level], BACK_HALO[level]
    send = SEND_ROWS[level]
    trim = (rows - send) // 2
    stack_grads(du_v, mask_v, stacked_v, rows)
    for index in range(C // 256):
        found = back_columns(stacked_v, weight, index)
        cols = slice(index * 256, (index + 1) * 256)
        if send:
            send_out[:, cols] = found[trim : trim + send].astype(BF16)
        grad_out[0:own, cols] = found[halo : halo + own].astype(BF16)
    if own < 256:
        grad_out[own:, :] = jnp.zeros((256 - own, C), BF16)


def own_grads(level, du_v, du_out):
    own, halo = OWN[level], BACK_HALO[level]
    du_out[0:own, :] = du_v[halo : halo + own, :].astype(BF16)
    if own < 256:
        du_out[own:, :] = jnp.zeros((256 - own, C), BF16)


def last_kernel(window, info, starts, x_in, cot, up, down, weight, _, send_out, grad_out, du_out,
                _out, mask_v, stacked_v, du_v):
    level, rows = 3, ROWS[3]

    @pl.when(info[0] == level)
    def _():
        fill_masks(mask_v, starts, window, info[1], level, HALO[level], rows)
        stack_inputs(
            lambda index: x_in[:, index * 128 : (index + 1) * 128], mask_v, stacked_v, rows
        )
        for index in range(C // 256):
            _, slope = gelu_and_slope(conv_columns(stacked_v, weight, index))
            cols = slice(index * 256, (index + 1) * 256)
            g = jnp.concatenate(
                [
                    up[window * 16 : window * 16 + 16, cols].astype(F32)[8:16],
                    cot[window, :, cols].astype(F32),
                    down[window * 16 : window * 16 + 16, cols].astype(F32)[0:8],
                ],
                axis=0,
            )
            du_v[:, cols] = (g * slope).astype(BF16).astype(F32)
        finish_backward(level, du_v, mask_v, stacked_v, weight, send_out, grad_out)
        own_grads(level, du_v, du_out)


def last_call(window, info, starts, weight, token, x, cot, up, down):
    rows = ROWS[3]
    return call(
        functools.partial(last_kernel, window),
        "last",
        4 * rows * C * C * TAPS,
        (info, starts),
        (x, cot, up, down, weight),
        (shape_of(rows, C), shape_of(256, C), shape_of(256, C)),
        token,
        [
            pltpu.VMEM((TAPS, rows, 128), F32),
            pltpu.VMEM((rows, TAPS * C), BF16),
            pltpu.VMEM((rows, C), F32),
        ],
    )


def spread_grads(arrived, wide_v, slope, du_v, rows):
    for index in range(C // 128):
        cols = slice(index * 128, (index + 1) * 128)
        half = 0.5 * arrived[:, cols].astype(F32)
        wide_v[index, pl.ds(0, rows // 2, stride=2), :] = half
        wide_v[index, pl.ds(1, rows // 2, stride=2), :] = half
        du_v[:, cols] = (wide_v[index] * slope[:, cols]).astype(BF16).astype(F32)


def backward_kernel(level, window, info, starts, arrived, slope, weight, _grad, _du, _token,
                    send_out, grad_out, du_out, _out, wide_v, mask_v, stacked_v, du_v):
    rows = BACK_ROWS[level]

    @pl.when(info[0] == level)
    def _():
        fill_masks(mask_v, starts, window, info[1], level, BACK_HALO[level], rows)
        spread_grads(arrived, wide_v, slope, du_v, rows)
        finish_backward(level, du_v, mask_v, stacked_v, weight, send_out, grad_out)
        own_grads(level, du_v, du_out)


def backward_call(level, window, info, starts, weight, token, arrived, slope, grad, du):
    rows = BACK_ROWS[level]
    return call(
        functools.partial(backward_kernel, level, window),
        f"backward{level}",
        2 * rows * C * C * TAPS,
        (info, starts),
        (arrived, slope, weight, grad, du),
        (shape_of(SEND_ROWS[level], C), shape_of(256, C), shape_of(256, C)),
        token,
        [
            pltpu.VMEM((C // 128, rows, 128), F32),
            pltpu.VMEM((TAPS, rows, 128), F32),
            pltpu.VMEM((rows, TAPS * C), BF16),
            pltpu.VMEM((rows, C), F32),
        ],
        aliases=((3, 1), (4, 2)),
    )


def first_du_kernel(info, arrived, slope, _du, _token, all_out, du_out, _out, wide_v, du_v):
    rows = BACK_ROWS[0]

    @pl.when(info[0] == 0)
    def _():
        spread_grads(arrived, wide_v, slope, du_v, rows)
        own_grads(0, du_v, du_out)
        all_out[...] = du_v[...].astype(BF16)


def first_du_call(info, token, arrived, slope, du):
    rows = BACK_ROWS[0]
    return call(
        first_du_kernel,
        "first_du",
        rows * C * 8,
        (info,),
        (arrived, slope, du),
        (shape_of(rows, C), shape_of(256, C)),
        token,
        [pltpu.VMEM((C // 128, rows, 128), F32), pltpu.VMEM((rows, C), F32)],
        aliases=((2, 1),),
    )


def first_grad_kernel(window, info, starts, du, weight, _grad, _token, grad_out, _out, mask_v,
                      stacked_v):
    rows = BACK_ROWS[0]

    @pl.when(info[0] == 0)
    def _():
        fill_masks(mask_v, starts, window, info[1], 0, BACK_HALO[0], rows)
        finish_backward(0, du, mask_v, stacked_v, weight, None, grad_out)


def first_grad_call(window, info, starts, weight, token, du, grad):
    rows = BACK_ROWS[0]
    return call(
        functools.partial(first_grad_kernel, window),
        "first_grad",
        2 * rows * C * C * TAPS,
        (info, starts),
        (du, weight, grad),
        (shape_of(256, C),),
        token,
        [pltpu.VMEM((TAPS, rows, 128), F32), pltpu.VMEM((rows, TAPS * C), BF16)],
        aliases=((2, 0),),
    )


def fill_order(seq, order_ref):
    row = lax.broadcasted_iota(jnp.int32, (C, 128), 0)
    place = (row * 2731) >> 16
    apart = ((place & 15) << 1) | (place >> 4)
    source = CHUNK * (seq ^ apart) + (row - CHUNK * place)
    lane = lax.broadcasted_iota(jnp.int32, (C, 128), 1)
    for index in range(C // 128):
        order_ref[:, index * 128 : (index + 1) * 128] = jnp.where(
            source == lane + index * 128, 1.0, 0.0
        ).astype(BF16)


def side_kernel(level, windows, info, starts, *refs):
    rows, halo, own = BACK_ROWS[level], BACK_HALO[level], OWN[level]
    inputs = 5 if level == 0 else windows
    xs = refs[:inputs]
    rest = refs[inputs + (1 if level == 0 else 2) :]
    side_out, _, mask_v, stacked_v, order_v = rest
    width = max(own, 128)
    skip = HALO[level] - halo

    @pl.when(info[0] == level)
    def _():
        fill_order(info[1], order_v)
        for window in range(windows):

            def read(index):
                cols = slice(index * 128, (index + 1) * 128)
                if level == 0:
                    up, down = xs[1:3] if window == 0 else xs[3:5]
                    first = halo_rows(window)
                    return jnp.concatenate(
                        [
                            up[first + 48 : first + 64, cols],
                            xs[0][window, :, cols],
                            down[first : first + 16, cols],
                        ],
                        axis=0,
                    )
                return xs[window][skip : skip + rows, cols]

            fill_masks(mask_v, starts, window, info[1], level, halo, rows)
            stack_inputs(read, mask_v, stacked_v, rows)
            for tap in range(TAPS):
                part = stacked_v[halo : halo + own, tap * C : (tap + 1) * C]
                if own < width:
                    part = jnp.concatenate([part, jnp.zeros((width - own, C), BF16)], axis=0)
                found = lax.dot_general(
                    order_v[...], part, (((1,), (1,)), ((), ())), preferred_element_type=F32
                )
                lines = slice(tap * C, (tap + 1) * C)
                side_out[lines, window * 256 : window * 256 + width] = found.astype(BF16)
                if width < 256:
                    side_out[lines, window * 256 + width : (window + 1) * 256] = jnp.zeros(
                        (C, 256 - width), BF16
                    )


def side_call(level, windows, info, starts, token, side, *xs):
    rows = BACK_ROWS[level]
    held = () if side is None else (side,)
    return call(
        functools.partial(side_kernel, level, windows),
        f"side{level}",
        2 * windows * 256 * C * C * TAPS,
        (info, starts),
        (*xs, *held),
        (shape_of(TAPS * C, windows * 256),),
        token,
        [
            pltpu.VMEM((TAPS, rows, 128), F32),
            pltpu.VMEM((rows, TAPS * C), BF16),
            pltpu.VMEM((C, C), BF16),
        ],
        aliases=() if side is None else ((len(xs), 0),),
    )


def weight_kernel(quarter, side, *refs):
    dus = refs[:-4]
    _, send_out, keep_out, _ = refs[-4:]
    first = sum(PIECES[:quarter])
    for piece in range(PIECES[quarter]):
        tap, part = divmod(first + piece, 3)
        found = None
        for window, du in enumerate(dus):
            term = jnp.dot(
                side[tap * C : (tap + 1) * C, window * 256 : (window + 1) * 256],
                du[:, part * 256 : (part + 1) * 256],
                preferred_element_type=F32,
            )
            found = term if found is None else found + term
        found = found.reshape(2, 16, CHUNK, 256)
        cols = slice(piece * 256, (piece + 1) * 256)
        keep_out[:, :, cols] = found[0].astype(BF16)
        send_out[:, :, cols] = found[1].astype(BF16)


def weight_call(quarter, token, side, dus):
    width = PIECES[quarter] * 256
    shape = shape_of(16, CHUNK, width)
    return call(
        functools.partial(weight_kernel, quarter),
        f"weight{quarter}",
        2 * C * 768 * width,
        (),
        (side, *dus),
        (shape, shape),
        token,
        [],
    )


def quarter_plan(first_axis, *orders):
    held = [(y, z) for y in range(4) for z in range(4)]
    plan = []
    for axis, (one, two) in zip((first_axis, 1 - first_axis), orders):
        unit = (8, 2)[axis]
        for apart, gone in ((one, (one, 2)), (two, (two,))):
            leaving = [place for place in held if place[axis] in gone]
            leaving.sort(key=lambda place: (place[1 - axis], gone.index(place[axis])))
            staying = []
            for place in leaving:
                moved = list(place)
                moved[axis] ^= apart
                staying.append(tuple(moved))
            plan.append(
                (
                    apart * unit,
                    [held.index(place) for place in leaving],
                    [held.index(place) for place in staying],
                )
            )
            held = staying
    return plan


PLANS = (
    quarter_plan(1, (1, 3), (1, 3)),
    quarter_plan(1, (3, 1), (1, 3)),
    quarter_plan(0, (1, 3), (1, 3)),
    quarter_plan(0, (3, 1), (1, 3)),
)
GROUPS = ((0, 1), (2, 3))


def added(keep, arrived, source):
    return keep[source].astype(F32) + arrived[source].astype(F32)


def add_kernel(group, step, *refs):
    parts = GROUPS[group] if step < 3 else (GROUPS[group][0],)
    count = len(parts)
    keeps, arriveds = refs[:count], refs[count : 2 * count]
    outs = refs[2 * count + 1 : -1]
    merged = step >= 2
    half = len(outs) // 2
    stays, leaves = outs[:half], outs[half:]
    first = 0
    for place, quarter in enumerate(parts):
        width = keeps[place].shape[-1]
        _, leaving, staying = PLANS[quarter][step]
        for target, sources in ((stays, staying), (leaves, leaving)):
            for row, source in enumerate(sources):
                total = added(keeps[place], arriveds[place], source).astype(BF16)
                if merged:
                    target[0][row, :, first : first + width] = total
                else:
                    target[place][row] = total
        first += width


def add_call(group, step, token, keeps, arriveds):
    half = len(PLANS[0][step][1])
    widths = [keep.shape[-1] for keep in keeps]
    if step >= 2:
        widths = [sum(widths)]
    shapes = tuple(shape_of(half, CHUNK, width) for width in widths)
    *outs, token = call(
        functools.partial(add_kernel, group, step),
        f"add{step}",
        4000000 // (1 << step),
        (),
        (*keeps, *arriveds),
        shapes + shapes,
        token,
        [],
    )
    return outs[: len(shapes)], outs[len(shapes) :], token


def final_kernel(*refs):
    keeps, arriveds, out = refs[0:2], refs[2:4], refs[5]
    for group, quarters in enumerate(GROUPS):
        total = added(keeps[group], arriveds[group], 0).astype(BF16).astype(F32)
        piece = sum(PIECES[: quarters[0]])
        for place in range(total.shape[1] // 256):
            tap, part = divmod(piece + place, 3)
            out[tap, :, part * 256 : (part + 1) * 256] = total[:, place * 256 : (place + 1) * 256]


def section_pairs(source, target, shards):
    return [(source * shards + place, target * shards + place) for place in range(shards)]


def apart_pairs(sections, shards, apart):
    return [
        (section * shards + place, section * shards + (place ^ apart))
        for section in range(sections)
        for place in range(shards)
    ]


def body(dna_embed, conv_weight, interval_starts, cotangent):
    windows = dna_embed.shape[0]
    sections = lax.axis_size("section")
    shards = lax.axis_size("seq")
    section_index = lax.axis_index("section")
    seq_index = lax.axis_index("seq")
    info = jnp.stack([section_index, seq_index]).astype(jnp.int32)
    weight = jnp.transpose(conv_weight[0], (1, 0, 2)).reshape(TAPS * C, C)
    starts = interval_starts
    token = jnp.zeros((8, 128), F32)

    up_pairs = [
        (section * shards + place, section * shards + place + 1)
        for section in (0, sections - 1)
        for place in range(shards - 1)
    ]
    down_pairs = [(target, source) for source, target in up_pairs]
    first_pairs = [pair for pair in up_pairs if pair[0] < shards]
    first_down = [(target, source) for source, target in first_pairs]
    up0, down0, token = first_edges_call(info, token, dna_embed)
    up0 = lax.ppermute(up0, AXES, first_pairs)
    down0 = lax.ppermute(down0, AXES, first_down)
    up_rest, down_rest, token = rest_edges_call(info, token, dna_embed, cotangent)
    up_rest = lax.ppermute(up_rest, AXES, up_pairs)
    down_rest = lax.ppermute(down_rest, AXES, down_pairs)

    def relay(value, source, target):
        return lax.ppermute(value, AXES, section_pairs(source, target, shards))

    inputs = [[None] * windows for _ in range(4)]
    slopes = [[None] * windows for _ in range(4)]
    grads = [None] * windows
    dus = [None] * windows
    wide_du = [None] * windows
    arrived = [None] * windows
    side = None

    def forward(level, window):
        nonlocal token
        xs = (inputs[level][window],)
        if level == 0:
            xs = (dna_embed, up0, down0) if window == 0 else (dna_embed, up_rest, down_rest)
        pooled, slopes[level][window], token = forward_call(
            level, window, info, starts, weight, token, *xs
        )
        inputs[level + 1][window] = relay(pooled, level, level + 1)

    def turn(window):
        nonlocal token
        send, grads[window], dus[window], token = last_call(
            window, info, starts, weight, token, inputs[3][window], cotangent, up_rest,
            down_rest,
        )
        arrived[window] = relay(send, 3, 2)

    def backward(level, window):
        nonlocal token
        send, grads[window], dus[window], token = backward_call(
            level, window, info, starts, weight, token, arrived[window], slopes[level][window],
            grads[window], dus[window],
        )
        arrived[window] = relay(send, level, level - 1)

    def arrive(window):
        nonlocal token
        wide_du[window], dus[window], token = first_du_call(
            info, token, arrived[window], slopes[0][window], dus[window]
        )

    def first_grad(window):
        nonlocal token
        grads[window], token = first_grad_call(
            window, info, starts, weight, token, wide_du[window], grads[window]
        )

    def sideways(level):
        nonlocal side, token
        xs = (dna_embed, up0, down0, up_rest, down_rest) if level == 0 else inputs[level]
        side, token = side_call(level, windows, info, starts, token, side, *xs)

    forward(0, 0)
    forward(0, 1)
    forward(0, 2)
    sideways(0)
    forward(1, 0)
    forward(1, 1)
    forward(2, 0)
    forward(1, 2)
    sideways(1)
    forward(2, 1)
    turn(0)
    forward(2, 2)
    turn(1)
    backward(2, 0)
    turn(2)
    sideways(3)
    backward(2, 1)
    backward(1, 0)
    backward(2, 2)
    sideways(2)
    backward(1, 1)
    backward(1, 2)
    arrive(0)
    first_grad(0)
    arrive(1)
    first_grad(1)
    arrive(2)

    keeps, arriveds = [[], []], [[], []]

    def weigh(group):
        nonlocal token
        for quarter in GROUPS[group]:
            send, keep, token = weight_call(quarter, token, side, dus)
            keeps[group].append(keep)
            arriveds[group].append(lax.ppermute(send, AXES, apart_pairs(sections, shards, 1)))

    def pass_on(group, step):
        nonlocal token
        keeps[group], leaves, token = add_call(group, step, token, keeps[group], arriveds[group])
        arriveds[group] = [
            lax.ppermute(leaving, AXES, apart_pairs(sections, shards, PLANS[quarter][step][0]))
            for quarter, leaving in zip(GROUPS[group], leaves)
        ]

    weigh(0)
    weigh(1)
    pass_on(0, 0)
    pass_on(1, 0)
    pass_on(0, 1)
    first_grad(2)
    pass_on(1, 1)
    pass_on(0, 2)
    pass_on(1, 2)
    pass_on(0, 3)
    pass_on(1, 3)
    weight_grad, token = call(
        final_kernel, "final", 1000000, (), (*keeps[0], *keeps[1], *arriveds[0], *arriveds[1]),
        (shape_of(TAPS, CHUNK, C, dtype=F32),), token, [],
    )
    weight_grad = jnp.transpose(weight_grad, (1, 0, 2))[None]
    return (weight_grad, jnp.stack(grads)[None])


def solution(mesh):
    placed = (P(None, "seq", None), P("section", None, None, None), P(), P(None, "seq", None))
    return jax.shard_map(
        body,
        mesh=mesh,
        in_specs=placed,
        out_specs=(P("section", "seq", None, None), P("section", None, "seq", None)),
        check_vma=False,
    )
```

```python
import functools

import jax
import jax.numpy as jnp
from jax import lax
from jax.experimental import pallas as pl
from jax.experimental.pallas import tpu as pltpu
from jax.sharding import PartitionSpec as P

C = 768
TAPS = 5
AXES = ("section", "seq")
OWN = (256, 128, 64, 32)
HALO = (64, 32, 16, 8)
ROWS = (384, 192, 96, 48)
BACK_HALO = (16, 16, 16, 8)
BACK_ROWS = (288, 160, 96, 48)
SEND_ROWS = (0, 144, 80, 48)
CHUNK = 24
LIMIT = 24 * 1024 * 1024
F32 = jnp.float32
BF16 = jnp.bfloat16
ANY = pl.BlockSpec(memory_space=pl.ANY)
SMEM = pl.BlockSpec(memory_space=pltpu.SMEM)
VMEM = pl.BlockSpec(memory_space=pltpu.VMEM)
PIECES = (4, 4, 4, 3)


def shape_of(*dims, dtype=BF16):
    return jax.ShapeDtypeStruct(dims, dtype)


def call(kernel, name, flops, smem, vmem, outs, token, scratch, aliases=()):
    operands = (*smem, *vmem, token)
    count = len(operands)
    pairs = {len(smem) + place: out for place, out in aliases}
    pairs[count - 1] = len(outs)
    return pl.pallas_call(
        kernel,
        out_shape=(*outs, jax.ShapeDtypeStruct(token.shape, token.dtype)),
        in_specs=[SMEM] * len(smem) + [VMEM] * len(vmem) + [ANY],
        out_specs=(*[VMEM] * len(outs), ANY),
        scratch_shapes=scratch,
        input_output_aliases=pairs,
        compiler_params=pltpu.CompilerParams(vmem_limit_bytes=LIMIT),
        cost_estimate=pl.CostEstimate(flops=int(flops), bytes_accessed=1000000, transcendentals=0),
        name=name,
    )(*operands)


def no_cut(starts, window, positions, level, length):
    cut = positions == length
    for entry in range(starts.shape[1]):
        first = (starts[window, entry] + ((1 << level) - 1)) >> level
        cut = cut | (positions == first)
    return jnp.where(cut, 0.0, 1.0)


def roll_rows(value, by):
    return pltpu.roll(value, by % value.shape[0], 0)


def fill_masks(mask_ref, starts, window, seq, level, halo, rows):
    own = OWN[level]
    length = own * 32
    row = lax.broadcasted_iota(jnp.int32, (rows, 128), 0)
    positions = row + (seq * own - halo)
    inside = jnp.where((positions >= 0) & (positions < length), 1.0, 0.0)
    free = no_cut(starts, window, positions, level, length)
    before = inside * free
    after = inside * roll_rows(free, -1)
    mask_ref[0, 0:rows] = before * roll_rows(free, 1)
    mask_ref[1, 0:rows] = before
    mask_ref[2, 0:rows] = inside
    mask_ref[3, 0:rows] = after
    mask_ref[4, 0:rows] = after * roll_rows(free, -2)


def stack_inputs(read, mask_ref, stacked_ref, rows):
    for index in range(C // 128):
        tile = read(index).astype(F32)
        for tap in range(TAPS):
            moved = roll_rows(tile, 2 - tap) if tap != 2 else tile
            first = tap * C + index * 128
            stacked_ref[0:rows, first : first + 128] = (moved * mask_ref[tap, 0:rows]).astype(BF16)


def stack_grads(value_ref, mask_ref, stacked_ref, rows):
    for index in range(C // 128):
        tile = value_ref[0:rows, index * 128 : (index + 1) * 128].astype(F32)
        for tap in range(TAPS):
            moved = tile * mask_ref[tap, 0:rows]
            moved = roll_rows(moved, tap - 2) if tap != 2 else moved
            first = tap * C + index * 128
            stacked_ref[0:rows, first : first + 128] = moved.astype(BF16)


def conv_columns(stacked_ref, weight_ref, index):
    return jnp.dot(
        stacked_ref[...], weight_ref[:, index * 256 : (index + 1) * 256], preferred_element_type=F32
    )


def back_columns(stacked_ref, weight_ref, index):
    total = None
    for tap in range(TAPS):
        first = tap * C + index * 256
        part = lax.dot_general(
            stacked_ref[:, tap * C : (tap + 1) * C],
            weight_ref[first : first + 256, :],
            (((1,), (1,)), ((), ())),
            preferred_element_type=F32,
        )
        total = part if total is None else total + part
    return total


def gelu_and_slope(u):
    scale = 0.7978845608028654
    square = u * u
    bend = jnp.tanh(scale * (u + 0.044715 * square * u))
    half = 0.5 * (1.0 + bend)
    slope = half + 0.5 * u * (1.0 - bend * bend) * (scale * (1.0 + 0.134145 * square))
    return u * half, slope


def edges_kernel(windows, info, dna, cot, _, near, first, rest, _out):
    own, part = OWN[0], cot.shape[1]
    odd = info[1] % 2 == 1

    def fill(leading_to_near):
        near_x, far_x = (0, own - 64) if leading_to_near else (own - 64, 0)
        near_c, far_c = (0, part - 16) if leading_to_near else (part - 16, 0)
        for window in range(windows):
            rows = slice(window * 64, window * 64 + 64)

            @pl.when(info[0] == 0)
            def _():
                near[rows, :] = dna[window, near_x : near_x + 64, :]
                if window == 0:
                    first[...] = dna[0, far_x : far_x + 64, :]
                else:
                    rest[(window - 1) * 64 : window * 64, :] = dna[window, far_x : far_x + 64, :]

            lines = slice(window * 16, window * 16 + 16)

            @pl.when(info[0] == 3)
            def _():
                near[lines, :] = cot[window, near_c : near_c + 16, :]
                rest[lines, :] = cot[window, far_c : far_c + 16, :]

    pl.when(odd)(functools.partial(fill, True))
    pl.when(jnp.logical_not(odd))(functools.partial(fill, False))


def edges_call(info, token, dna, cot):
    windows = dna.shape[0]
    return call(
        functools.partial(edges_kernel, windows),
        "edges",
        2e10,
        (info,),
        (dna, cot),
        (shape_of(windows * 64, C), shape_of(64, C), shape_of((windows - 1) * 64, C)),
        token,
        [],
    )


def sides(odd, near, far):
    near, far = near.astype(F32), far.astype(F32)
    return jnp.where(odd, near, far), jnp.where(odd, far, near)


def with_edges(own, near, far, odd, low, high):
    ahead, behind = sides(odd, near, far)
    return jnp.concatenate([ahead[low:], own.astype(F32), behind[:high]], axis=0)


def forward_kernel(level, window, info, starts, *refs):
    rows, back = ROWS[level], BACK_ROWS[level]
    skip = HALO[level] - BACK_HALO[level]
    inputs = 3 if level == 0 else 1
    xs = refs[:inputs]
    weight, _, pooled_out, slope_out, _, mask_v, stacked_v, act_v = refs[inputs:]

    def read(index):
        cols = slice(index * 128, (index + 1) * 128)
        if level == 0:
            x_in, near, far = xs
            first = max(window - 1, 0) * 64
            return with_edges(
                x_in[window, :, cols],
                near[window * 64 : window * 64 + 64, cols],
                far[first : first + 64, cols],
                info[1] % 2 == 1,
                0,
                64,
            )
        return xs[0][:, cols]

    @pl.when(info[0] == level)
    def _():
        fill_masks(mask_v, starts, window, info[1], level, HALO[level], rows)
        stack_inputs(read, mask_v, stacked_v, rows)
        for index in range(C // 256):
            act, slope = gelu_and_slope(conv_columns(stacked_v, weight, index))
            slope_out[:, index * 256 : (index + 1) * 256] = slope[skip : skip + back]
            for half in range(2):
                place = index * 2 + half
                act_v[place] = act[:, half * 128 : (half + 1) * 128]
                even = act_v[place, pl.ds(0, rows // 2, stride=2), :]
                odd = act_v[place, pl.ds(1, rows // 2, stride=2), :]
                pooled_out[:, place * 128 : (place + 1) * 128] = (0.5 * (even + odd)).astype(BF16)


def forward_call(level, window, info, starts, weight, token, *xs):
    rows, back = ROWS[level], BACK_ROWS[level]
    return call(
        functools.partial(forward_kernel, level, window),
        f"forward{level}",
        2 * rows * C * C * TAPS,
        (info, starts),
        (*xs, weight),
        (shape_of(rows // 2, C), shape_of(back, C, dtype=F32)),
        token,
        [
            pltpu.VMEM((TAPS, rows, 128), F32),
            pltpu.VMEM((rows, TAPS * C), BF16),
            pltpu.VMEM((C // 128, rows, 128), F32),
        ],
    )


def finish_backward(level, du_v, mask_v, stacked_v, weight, send_out, grad_out):
    rows, own, halo = BACK_ROWS[level], OWN[level], BACK_HALO[level]
    send = SEND_ROWS[level]
    trim = (rows - send) // 2
    stack_grads(du_v, mask_v, stacked_v, rows)
    for index in range(C // 256):
        found = back_columns(stacked_v, weight, index)
        cols = slice(index * 256, (index + 1) * 256)
        if send:
            send_out[:, cols] = found[trim : trim + send].astype(BF16)
        grad_out[0:own, cols] = found[halo : halo + own].astype(BF16)
    if own < 256:
        grad_out[own:, :] = jnp.zeros((256 - own, C), BF16)


def own_grads(level, du_v, du_out):
    own, halo = OWN[level], BACK_HALO[level]
    du_out[0:own, :] = du_v[halo : halo + own, :].astype(BF16)
    if own < 256:
        du_out[own:, :] = jnp.zeros((256 - own, C), BF16)


def last_kernel(window, info, starts, x_in, cot, near, far, weight, _, send_out, grad_out, du_out,
                _out, mask_v, stacked_v, du_v):
    level, rows = 3, ROWS[3]

    @pl.when(info[0] == level)
    def _():
        fill_masks(mask_v, starts, window, info[1], level, HALO[level], rows)
        stack_inputs(
            lambda index: x_in[:, index * 128 : (index + 1) * 128], mask_v, stacked_v, rows
        )
        for index in range(C // 256):
            _, slope = gelu_and_slope(conv_columns(stacked_v, weight, index))
            cols = slice(index * 256, (index + 1) * 256)
            lines = slice(window * 16, window * 16 + 16)
            g = with_edges(
                cot[window, :, cols], near[lines, cols], far[lines, cols], info[1] % 2 == 1, 8, 8
            )
            du_v[:, cols] = (g * slope).astype(BF16).astype(F32)
        finish_backward(level, du_v, mask_v, stacked_v, weight, send_out, grad_out)
        own_grads(level, du_v, du_out)


def last_call(window, info, starts, weight, token, x, cot, near, far):
    rows = ROWS[3]
    return call(
        functools.partial(last_kernel, window),
        "last",
        4 * rows * C * C * TAPS,
        (info, starts),
        (x, cot, near, far, weight),
        (shape_of(rows, C), shape_of(256, C), shape_of(256, C)),
        token,
        [
            pltpu.VMEM((TAPS, rows, 128), F32),
            pltpu.VMEM((rows, TAPS * C), BF16),
            pltpu.VMEM((rows, C), F32),
        ],
    )


def spread_grads(arrived, wide_v, slope, du_v, rows):
    for index in range(C // 128):
        cols = slice(index * 128, (index + 1) * 128)
        half = 0.5 * arrived[:, cols].astype(F32)
        wide_v[index, pl.ds(0, rows // 2, stride=2), :] = half
        wide_v[index, pl.ds(1, rows // 2, stride=2), :] = half
        du_v[:, cols] = (wide_v[index] * slope[:, cols]).astype(BF16).astype(F32)


def backward_kernel(level, window, info, starts, arrived, slope, weight, _grad, _du, _token,
                    send_out, grad_out, du_out, _out, wide_v, mask_v, stacked_v, du_v):
    rows = BACK_ROWS[level]

    @pl.when(info[0] == level)
    def _():
        fill_masks(mask_v, starts, window, info[1], level, BACK_HALO[level], rows)
        spread_grads(arrived, wide_v, slope, du_v, rows)
        finish_backward(level, du_v, mask_v, stacked_v, weight, send_out, grad_out)
        own_grads(level, du_v, du_out)


def backward_call(level, window, info, starts, weight, token, arrived, slope, grad, du):
    rows = BACK_ROWS[level]
    return call(
        functools.partial(backward_kernel, level, window),
        f"backward{level}",
        2 * rows * C * C * TAPS,
        (info, starts),
        (arrived, slope, weight, grad, du),
        (shape_of(SEND_ROWS[level], C), shape_of(256, C), shape_of(256, C)),
        token,
        [
            pltpu.VMEM((C // 128, rows, 128), F32),
            pltpu.VMEM((TAPS, rows, 128), F32),
            pltpu.VMEM((rows, TAPS * C), BF16),
            pltpu.VMEM((rows, C), F32),
        ],
        aliases=((3, 1), (4, 2)),
    )


def first_du_kernel(info, arrived, slope, _du, _token, all_out, du_out, _out, wide_v, du_v):
    rows = BACK_ROWS[0]

    @pl.when(info[0] == 0)
    def _():
        spread_grads(arrived, wide_v, slope, du_v, rows)
        own_grads(0, du_v, du_out)
        all_out[...] = du_v[...].astype(BF16)


def first_du_call(info, token, arrived, slope, du):
    rows = BACK_ROWS[0]
    return call(
        first_du_kernel,
        "first_du",
        rows * C * 8,
        (info,),
        (arrived, slope, du),
        (shape_of(rows, C), shape_of(256, C)),
        token,
        [pltpu.VMEM((C // 128, rows, 128), F32), pltpu.VMEM((rows, C), F32)],
        aliases=((2, 1),),
    )


def first_grad_kernel(window, info, starts, du, weight, _grad, _token, grad_out, _out, mask_v,
                      stacked_v):
    rows = BACK_ROWS[0]

    @pl.when(info[0] == 0)
    def _():
        fill_masks(mask_v, starts, window, info[1], 0, BACK_HALO[0], rows)
        finish_backward(0, du, mask_v, stacked_v, weight, None, grad_out)


def first_grad_call(window, info, starts, weight, token, du, grad):
    rows = BACK_ROWS[0]
    return call(
        functools.partial(first_grad_kernel, window),
        "first_grad",
        2 * rows * C * C * TAPS,
        (info, starts),
        (du, weight, grad),
        (shape_of(256, C),),
        token,
        [pltpu.VMEM((TAPS, rows, 128), F32), pltpu.VMEM((rows, TAPS * C), BF16)],
        aliases=((2, 0),),
    )


def fill_order(seq, order_ref):
    row = lax.broadcasted_iota(jnp.int32, (C, 128), 0)
    place = (row * 2731) >> 16
    apart = ((place & 15) << 1) | (place >> 4)
    source = CHUNK * (seq ^ apart) + (row - CHUNK * place)
    lane = lax.broadcasted_iota(jnp.int32, (C, 128), 1)
    for index in range(C // 128):
        order_ref[:, index * 128 : (index + 1) * 128] = jnp.where(
            source == lane + index * 128, 1.0, 0.0
        ).astype(BF16)


def side_kernel(level, windows, info, starts, *refs):
    rows, halo, own = BACK_ROWS[level], BACK_HALO[level], OWN[level]
    inputs = 4 if level == 0 else windows
    xs = refs[:inputs]
    rest = refs[inputs + (1 if level == 0 else 2) :]
    side_out, _, mask_v, stacked_v, order_v = rest
    width = max(own, 128)
    skip = HALO[level] - halo

    @pl.when(info[0] == level)
    def _():
        fill_order(info[1], order_v)
        for window in range(windows):

            def read(index):
                cols = slice(index * 128, (index + 1) * 128)
                if level == 0:
                    x_in, near, far, rest = xs
                    first = max(window - 1, 0) * 64
                    far = rest if window else far
                    return with_edges(
                        x_in[window, :, cols],
                        near[window * 64 : window * 64 + 64, cols],
                        far[first : first + 64, cols],
                        info[1] % 2 == 1,
                        48,
                        16,
                    )
                return xs[window][skip : skip + rows, cols]

            fill_masks(mask_v, starts, window, info[1], level, halo, rows)
            stack_inputs(read, mask_v, stacked_v, rows)
            for tap in range(TAPS):
                part = stacked_v[halo : halo + own, tap * C : (tap + 1) * C]
                if own < width:
                    part = jnp.concatenate([part, jnp.zeros((width - own, C), BF16)], axis=0)
                found = lax.dot_general(
                    order_v[...], part, (((1,), (1,)), ((), ())), preferred_element_type=F32
                )
                lines = slice(tap * C, (tap + 1) * C)
                side_out[lines, window * 256 : window * 256 + width] = found.astype(BF16)
                if width < 256:
                    side_out[lines, window * 256 + width : (window + 1) * 256] = jnp.zeros(
                        (C, 256 - width), BF16
                    )


def side_call(level, windows, info, starts, token, side, *xs):
    rows = BACK_ROWS[level]
    held = () if side is None else (side,)
    return call(
        functools.partial(side_kernel, level, windows),
        f"side{level}",
        2 * windows * 256 * C * C * TAPS,
        (info, starts),
        (*xs, *held),
        (shape_of(TAPS * C, windows * 256),),
        token,
        [
            pltpu.VMEM((TAPS, rows, 128), F32),
            pltpu.VMEM((rows, TAPS * C), BF16),
            pltpu.VMEM((C, C), BF16),
        ],
        aliases=() if side is None else ((len(xs), 0),),
    )


def weight_kernel(quarter, side, *refs):
    dus = refs[:-4]
    _, send_out, keep_out, _ = refs[-4:]
    first = sum(PIECES[:quarter])
    for piece in range(PIECES[quarter]):
        tap, part = divmod(first + piece, 3)
        found = None
        for window, du in enumerate(dus):
            term = jnp.dot(
                side[tap * C : (tap + 1) * C, window * 256 : (window + 1) * 256],
                du[:, part * 256 : (part + 1) * 256],
                preferred_element_type=F32,
            )
            found = term if found is None else found + term
        found = found.reshape(2, 16, CHUNK, 256)
        cols = slice(piece * 256, (piece + 1) * 256)
        keep_out[:, :, cols] = found[0].astype(BF16)
        send_out[:, :, cols] = found[1].astype(BF16)


def weight_call(quarter, token, side, dus):
    width = PIECES[quarter] * 256
    shape = shape_of(16, CHUNK, width)
    return call(
        functools.partial(weight_kernel, quarter),
        f"weight{quarter}",
        2 * C * 768 * width,
        (),
        (side, *dus),
        (shape, shape),
        token,
        [],
    )


def quarter_plan(first_axis, *orders):
    held = [(y, z) for y in range(4) for z in range(4)]
    plan = []
    for axis, (one, two) in zip((first_axis, 1 - first_axis), orders):
        unit = (8, 2)[axis]
        for apart, gone in ((one, (one, 2)), (two, (two,))):
            leaving = [place for place in held if place[axis] in gone]
            leaving.sort(key=lambda place: (place[1 - axis], gone.index(place[axis])))
            staying = []
            for place in leaving:
                moved = list(place)
                moved[axis] ^= apart
                staying.append(tuple(moved))
            plan.append(
                (
                    apart * unit,
                    [held.index(place) for place in leaving],
                    [held.index(place) for place in staying],
                )
            )
            held = staying
    return plan


PLANS = (
    quarter_plan(1, (1, 3), (1, 3)),
    quarter_plan(1, (3, 1), (1, 3)),
    quarter_plan(0, (1, 3), (1, 3)),
    quarter_plan(0, (3, 1), (1, 3)),
)
GROUPS = ((0, 1), (2, 3))


def added(keep, arrived, source):
    return keep[source].astype(F32) + arrived[source].astype(F32)


def add_kernel(group, step, *refs):
    parts = GROUPS[group] if step < 3 else (GROUPS[group][0],)
    count = len(parts)
    keeps, arriveds = refs[:count], refs[count : 2 * count]
    outs = refs[2 * count + 1 : -1]
    merged = step >= 2
    half = len(outs) // 2
    stays, leaves = outs[:half], outs[half:]
    first = 0
    for place, quarter in enumerate(parts):
        width = keeps[place].shape[-1]
        _, leaving, staying = PLANS[quarter][step]
        for target, sources in ((stays, staying), (leaves, leaving)):
            for row, source in enumerate(sources):
                total = added(keeps[place], arriveds[place], source).astype(BF16)
                if merged:
                    target[0][row, :, first : first + width] = total
                else:
                    target[place][row] = total
        first += width


def add_call(group, step, token, keeps, arriveds):
    half = len(PLANS[0][step][1])
    widths = [keep.shape[-1] for keep in keeps]
    if step >= 2:
        widths = [sum(widths)]
    shapes = tuple(shape_of(half, CHUNK, width) for width in widths)
    *outs, token = call(
        functools.partial(add_kernel, group, step),
        f"add{step}",
        4000000 // (1 << step),
        (),
        (*keeps, *arriveds),
        shapes + shapes,
        token,
        [],
    )
    return outs[: len(shapes)], outs[len(shapes) :], token


def final_kernel(*refs):
    keeps, arriveds, out = refs[0:2], refs[2:4], refs[5]
    for group, quarters in enumerate(GROUPS):
        total = added(keeps[group], arriveds[group], 0).astype(BF16).astype(F32)
        piece = sum(PIECES[: quarters[0]])
        for place in range(total.shape[1] // 256):
            tap, part = divmod(piece + place, 3)
            out[tap, :, part * 256 : (part + 1) * 256] = total[:, place * 256 : (place + 1) * 256]


def section_pairs(source, target, shards):
    return [(source * shards + place, target * shards + place) for place in range(shards)]


def apart_pairs(sections, shards, apart):
    return [
        (section * shards + place, section * shards + (place ^ apart))
        for section in range(sections)
        for place in range(shards)
    ]


def body(dna_embed, conv_weight, interval_starts, cotangent):
    windows = dna_embed.shape[0]
    sections = lax.axis_size("section")
    shards = lax.axis_size("seq")
    section_index = lax.axis_index("section")
    seq_index = lax.axis_index("seq")
    info = jnp.stack([section_index, seq_index]).astype(jnp.int32)
    weight = jnp.transpose(conv_weight[0], (1, 0, 2)).reshape(TAPS * C, C)
    starts = interval_starts
    token = jnp.zeros((8, 128), F32)

    ends = (0, sections - 1)
    near_pairs = [
        pair for pair in apart_pairs(sections, shards, 1) if pair[0] // shards in ends
    ]
    far_pairs = [
        (section * shards + place, section * shards + place + by)
        for section in ends
        for place in range(shards)
        for by in (1 if place % 2 else -1,)
        if 0 <= place + by < shards
    ]
    near, far, rest, token = edges_call(info, token, dna_embed, cotangent)
    near = lax.ppermute(near, AXES, near_pairs)
    far = lax.ppermute(far, AXES, [pair for pair in far_pairs if pair[0] < shards])
    rest = lax.ppermute(rest, AXES, far_pairs)

    def relay(value, source, target):
        return lax.ppermute(value, AXES, section_pairs(source, target, shards))

    inputs = [[None] * windows for _ in range(4)]
    slopes = [[None] * windows for _ in range(4)]
    grads = [None] * windows
    dus = [None] * windows
    wide_du = [None] * windows
    arrived = [None] * windows
    side = None

    def forward(level, window):
        nonlocal token
        xs = (inputs[level][window],)
        if level == 0:
            xs = (dna_embed, near, rest if window else far)
        pooled, slopes[level][window], token = forward_call(
            level, window, info, starts, weight, token, *xs
        )
        inputs[level + 1][window] = relay(pooled, level, level + 1)

    def turn(window):
        nonlocal token
        send, grads[window], dus[window], token = last_call(
            window, info, starts, weight, token, inputs[3][window], cotangent, near, rest
        )
        arrived[window] = relay(send, 3, 2)

    def backward(level, window):
        nonlocal token
        send, grads[window], dus[window], token = backward_call(
            level, window, info, starts, weight, token, arrived[window], slopes[level][window],
            grads[window], dus[window],
        )
        arrived[window] = relay(send, level, level - 1)

    def arrive(window):
        nonlocal token
        wide_du[window], dus[window], token = first_du_call(
            info, token, arrived[window], slopes[0][window], dus[window]
        )

    def first_grad(window):
        nonlocal token
        grads[window], token = first_grad_call(
            window, info, starts, weight, token, wide_du[window], grads[window]
        )

    def sideways(level):
        nonlocal side, token
        xs = (dna_embed, near, far, rest) if level == 0 else inputs[level]
        side, token = side_call(level, windows, info, starts, token, side, *xs)

    forward(0, 0)
    forward(0, 1)
    forward(0, 2)
    sideways(0)
    forward(1, 0)
    forward(1, 1)
    forward(2, 0)
    forward(1, 2)
    sideways(1)
    forward(2, 1)
    turn(0)
    forward(2, 2)
    turn(1)
    backward(2, 0)
    turn(2)
    sideways(3)
    backward(2, 1)
    backward(1, 0)
    backward(2, 2)
    sideways(2)
    backward(1, 1)
    backward(1, 2)
    arrive(0)
    first_grad(0)
    arrive(1)
    first_grad(1)
    arrive(2)

    keeps, arriveds = [[], []], [[], []]

    def weigh(group):
        nonlocal token
        for quarter in GROUPS[group]:
            send, keep, token = weight_call(quarter, token, side, dus)
            keeps[group].append(keep)
            arriveds[group].append(lax.ppermute(send, AXES, apart_pairs(sections, shards, 1)))

    def pass_on(group, step):
        nonlocal token
        keeps[group], leaves, token = add_call(group, step, token, keeps[group], arriveds[group])
        arriveds[group] = [
            lax.ppermute(leaving, AXES, apart_pairs(sections, shards, PLANS[quarter][step][0]))
            for quarter, leaving in zip(GROUPS[group], leaves)
        ]

    weigh(0)
    weigh(1)
    pass_on(0, 0)
    pass_on(1, 0)
    first_grad(2)
    pass_on(0, 1)
    pass_on(1, 1)
    pass_on(0, 2)
    pass_on(1, 2)
    pass_on(0, 3)
    pass_on(1, 3)
    weight_grad, token = call(
        final_kernel, "final", 1000000, (), (*keeps[0], *keeps[1], *arriveds[0], *arriveds[1]),
        (shape_of(TAPS, CHUNK, C, dtype=F32),), token, [],
    )
    weight_grad = jnp.transpose(weight_grad, (1, 0, 2))[None]
    return (weight_grad, jnp.stack(grads)[None])


def solution(mesh):
    placed = (P(None, "seq", None), P("section", None, None, None), P(), P(None, "seq", None))
    return jax.shard_map(
        body,
        mesh=mesh,
        in_specs=placed,
        out_specs=(P("section", "seq", None, None), P("section", None, "seq", None)),
        check_vma=False,
    )
```

```python
import functools

import jax
import jax.numpy as jnp
from jax import lax
from jax.experimental import pallas as pl
from jax.experimental.pallas import tpu as pltpu
from jax.sharding import PartitionSpec as P

C = 768
TAPS = 5
AXES = ("section", "seq")
OWN = (256, 128, 64, 32)
HALO = (64, 32, 16, 8)
ROWS = (384, 192, 96, 48)
BACK_HALO = (16, 16, 16, 8)
BACK_ROWS = (288, 160, 96, 48)
SEND_ROWS = (0, 144, 80, 48)
CHUNK = 24
LIMIT = 24 * 1024 * 1024
F32 = jnp.float32
BF16 = jnp.bfloat16
ANY = pl.BlockSpec(memory_space=pl.ANY)
SMEM = pl.BlockSpec(memory_space=pltpu.SMEM)
VMEM = pl.BlockSpec(memory_space=pltpu.VMEM)
PIECES = (4, 4, 4, 3)


def shape_of(*dims, dtype=BF16):
    return jax.ShapeDtypeStruct(dims, dtype)


def call(kernel, name, flops, smem, vmem, outs, token, scratch, aliases=()):
    operands = (*smem, *vmem, token)
    count = len(operands)
    pairs = {len(smem) + place: out for place, out in aliases}
    pairs[count - 1] = len(outs)
    return pl.pallas_call(
        kernel,
        out_shape=(*outs, jax.ShapeDtypeStruct(token.shape, token.dtype)),
        in_specs=[SMEM] * len(smem) + [VMEM] * len(vmem) + [ANY],
        out_specs=(*[VMEM] * len(outs), ANY),
        scratch_shapes=scratch,
        input_output_aliases=pairs,
        compiler_params=pltpu.CompilerParams(vmem_limit_bytes=LIMIT),
        cost_estimate=pl.CostEstimate(flops=int(flops), bytes_accessed=1000000, transcendentals=0),
        name=name,
    )(*operands)


def no_cut(starts, window, positions, level, length):
    cut = positions == length
    for entry in range(starts.shape[1]):
        first = (starts[window, entry] + ((1 << level) - 1)) >> level
        cut = cut | (positions == first)
    return jnp.where(cut, 0.0, 1.0)


def roll_rows(value, by):
    return pltpu.roll(value, by % value.shape[0], 0)


def fill_masks(mask_ref, starts, window, seq, level, halo, rows):
    own = OWN[level]
    length = own * 32
    row = lax.broadcasted_iota(jnp.int32, (rows, 128), 0)
    positions = row + (seq * own - halo)
    inside = jnp.where((positions >= 0) & (positions < length), 1.0, 0.0)
    free = no_cut(starts, window, positions, level, length)
    before = inside * free
    after = inside * roll_rows(free, -1)
    mask_ref[0, 0:rows] = before * roll_rows(free, 1)
    mask_ref[1, 0:rows] = before
    mask_ref[2, 0:rows] = inside
    mask_ref[3, 0:rows] = after
    mask_ref[4, 0:rows] = after * roll_rows(free, -2)


def stack_inputs(read, mask_ref, stacked_ref, rows):
    for index in range(C // 128):
        tile = read(index).astype(F32)
        for tap in range(TAPS):
            moved = roll_rows(tile, 2 - tap) if tap != 2 else tile
            first = tap * C + index * 128
            stacked_ref[0:rows, first : first + 128] = (moved * mask_ref[tap, 0:rows]).astype(BF16)


def stack_grads(value_ref, mask_ref, stacked_ref, rows):
    for index in range(C // 128):
        tile = value_ref[0:rows, index * 128 : (index + 1) * 128].astype(F32)
        for tap in range(TAPS):
            moved = tile * mask_ref[tap, 0:rows]
            moved = roll_rows(moved, tap - 2) if tap != 2 else moved
            first = tap * C + index * 128
            stacked_ref[0:rows, first : first + 128] = moved.astype(BF16)


def conv_columns(stacked_ref, weight_ref, index):
    return jnp.dot(
        stacked_ref[...], weight_ref[:, index * 256 : (index + 1) * 256], preferred_element_type=F32
    )


def back_columns(stacked_ref, weight_ref, index, turned):
    if turned:
        return conv_columns(stacked_ref, weight_ref, index)
    total = None
    for tap in range(TAPS):
        first = tap * C + index * 256
        part = lax.dot_general(
            stacked_ref[:, tap * C : (tap + 1) * C],
            weight_ref[first : first + 256, :],
            (((1,), (1,)), ((), ())),
            preferred_element_type=F32,
        )
        total = part if total is None else total + part
    return total


def turn_kernel(info, weight, _, turned_out, _out, unit_v):
    @pl.when(info[0] > 0)
    def _():
        row = lax.broadcasted_iota(jnp.int32, (C, 128), 0)
        lane = lax.broadcasted_iota(jnp.int32, (C, 128), 1)
        for index in range(C // 128):
            unit_v[:, index * 128 : (index + 1) * 128] = jnp.where(
                row == lane + index * 128, 1.0, 0.0
            ).astype(BF16)
        for tap in range(TAPS):
            lines = slice(tap * C, (tap + 1) * C)
            for index in range(C // 256):
                first = tap * C + index * 256
                turned_out[lines, index * 256 : (index + 1) * 256] = lax.dot_general(
                    unit_v[...],
                    weight[first : first + 256, :],
                    (((1,), (1,)), ((), ())),
                    preferred_element_type=F32,
                ).astype(BF16)


def turn_call(info, token, weight):
    return call(
        turn_kernel, "turn", 2 * C * C * C * TAPS, (info,), (weight,), (shape_of(TAPS * C, C),),
        token, [pltpu.VMEM((C, C), BF16)],
    )


def gelu_and_slope(u):
    scale = 0.7978845608028654
    square = u * u
    bend = jnp.tanh(scale * (u + 0.044715 * square * u))
    half = 0.5 * (1.0 + bend)
    slope = half + 0.5 * u * (1.0 - bend * bend) * (scale * (1.0 + 0.134145 * square))
    return u * half, slope


def edges_kernel(windows, info, dna, cot, _, near, first, rest, _out):
    own, part = OWN[0], cot.shape[1]
    odd = info[1] % 2 == 1

    def fill(leading_to_near):
        near_x, far_x = (0, own - 64) if leading_to_near else (own - 64, 0)
        near_c, far_c = (0, part - 16) if leading_to_near else (part - 16, 0)
        for window in range(windows):
            rows = slice(window * 64, window * 64 + 64)

            @pl.when(info[0] == 0)
            def _():
                near[rows, :] = dna[window, near_x : near_x + 64, :]
                if window == 0:
                    first[...] = dna[0, far_x : far_x + 64, :]
                else:
                    rest[(window - 1) * 64 : window * 64, :] = dna[window, far_x : far_x + 64, :]

            lines = slice(window * 16, window * 16 + 16)

            @pl.when(info[0] == 3)
            def _():
                near[lines, :] = cot[window, near_c : near_c + 16, :]
                rest[lines, :] = cot[window, far_c : far_c + 16, :]

    pl.when(odd)(functools.partial(fill, True))
    pl.when(jnp.logical_not(odd))(functools.partial(fill, False))


def edges_call(info, token, dna, cot):
    windows = dna.shape[0]
    return call(
        functools.partial(edges_kernel, windows),
        "edges",
        2e10,
        (info,),
        (dna, cot),
        (shape_of(windows * 64, C), shape_of(64, C), shape_of((windows - 1) * 64, C)),
        token,
        [],
    )


def sides(odd, near, far):
    near, far = near.astype(F32), far.astype(F32)
    return jnp.where(odd, near, far), jnp.where(odd, far, near)


def with_edges(own, near, far, odd, low, high):
    ahead, behind = sides(odd, near, far)
    return jnp.concatenate([ahead[low:], own.astype(F32), behind[:high]], axis=0)


def forward_kernel(level, window, info, starts, *refs):
    rows, back = ROWS[level], BACK_ROWS[level]
    skip = HALO[level] - BACK_HALO[level]
    inputs = 3 if level == 0 else 1
    xs = refs[:inputs]
    weight, _, pooled_out, slope_out, _, mask_v, stacked_v, act_v = refs[inputs:]

    def read(index):
        cols = slice(index * 128, (index + 1) * 128)
        if level == 0:
            x_in, near, far = xs
            first = max(window - 1, 0) * 64
            return with_edges(
                x_in[window, :, cols],
                near[window * 64 : window * 64 + 64, cols],
                far[first : first + 64, cols],
                info[1] % 2 == 1,
                0,
                64,
            )
        return xs[0][:, cols]

    @pl.when(info[0] == level)
    def _():
        fill_masks(mask_v, starts, window, info[1], level, HALO[level], rows)
        stack_inputs(read, mask_v, stacked_v, rows)
        for index in range(C // 256):
            act, slope = gelu_and_slope(conv_columns(stacked_v, weight, index))
            slope_out[:, index * 256 : (index + 1) * 256] = slope[skip : skip + back]
            for half in range(2):
                place = index * 2 + half
                act_v[place] = act[:, half * 128 : (half + 1) * 128]
                even = act_v[place, pl.ds(0, rows // 2, stride=2), :]
                odd = act_v[place, pl.ds(1, rows // 2, stride=2), :]
                pooled_out[:, place * 128 : (place + 1) * 128] = (0.5 * (even + odd)).astype(BF16)


def forward_call(level, window, info, starts, weight, token, *xs):
    rows, back = ROWS[level], BACK_ROWS[level]
    return call(
        functools.partial(forward_kernel, level, window),
        f"forward{level}",
        2 * rows * C * C * TAPS,
        (info, starts),
        (*xs, weight),
        (shape_of(rows // 2, C), shape_of(back, C, dtype=F32)),
        token,
        [
            pltpu.VMEM((TAPS, rows, 128), F32),
            pltpu.VMEM((rows, TAPS * C), BF16),
            pltpu.VMEM((C // 128, rows, 128), F32),
        ],
    )


def finish_backward(level, du_v, mask_v, stacked_v, weight, send_out, grad_out):
    rows, own, halo = BACK_ROWS[level], OWN[level], BACK_HALO[level]
    send = SEND_ROWS[level]
    trim = (rows - send) // 2
    stack_grads(du_v, mask_v, stacked_v, rows)
    for index in range(C // 256):
        found = back_columns(stacked_v, weight, index, level > 0)
        cols = slice(index * 256, (index + 1) * 256)
        if send:
            send_out[:, cols] = found[trim : trim + send].astype(BF16)
        grad_out[0:own, cols] = found[halo : halo + own].astype(BF16)
    if own < 256:
        grad_out[own:, :] = jnp.zeros((256 - own, C), BF16)


def own_grads(level, du_v, du_out):
    own, halo = OWN[level], BACK_HALO[level]
    du_out[0:own, :] = du_v[halo : halo + own, :].astype(BF16)
    if own < 256:
        du_out[own:, :] = jnp.zeros((256 - own, C), BF16)


def last_kernel(window, info, starts, x_in, cot, near, far, weight, turned, *refs):
    send_out, grad_out, du_out, _, mask_v, stacked_v, du_v = refs[-7:]
    level, rows = 3, ROWS[3]

    @pl.when(info[0] == level)
    def _():
        fill_masks(mask_v, starts, window, info[1], level, HALO[level], rows)
        stack_inputs(
            lambda index: x_in[:, index * 128 : (index + 1) * 128], mask_v, stacked_v, rows
        )
        for index in range(C // 256):
            _, slope = gelu_and_slope(conv_columns(stacked_v, weight, index))
            cols = slice(index * 256, (index + 1) * 256)
            lines = slice(window * 16, window * 16 + 16)
            g = with_edges(
                cot[window, :, cols], near[lines, cols], far[lines, cols], info[1] % 2 == 1, 8, 8
            )
            du_v[:, cols] = (g * slope).astype(BF16).astype(F32)
        finish_backward(level, du_v, mask_v, stacked_v, turned, send_out, grad_out)
        own_grads(level, du_v, du_out)


def last_call(window, info, starts, weight, turned, token, x, cot, near, far, *held):
    rows = ROWS[3]
    return call(
        functools.partial(last_kernel, window),
        "last",
        4 * rows * C * C * TAPS,
        (info, starts),
        (x, cot, near, far, weight, turned, *held),
        (shape_of(rows, C), shape_of(256, C), shape_of(256, C)),
        token,
        [
            pltpu.VMEM((TAPS, rows, 128), F32),
            pltpu.VMEM((rows, TAPS * C), BF16),
            pltpu.VMEM((rows, C), F32),
        ],
        aliases=((6, 0),) if held else (),
    )


def spread_grads(arrived, wide_v, slope, du_v, rows):
    for index in range(C // 128):
        cols = slice(index * 128, (index + 1) * 128)
        half = 0.5 * arrived[:, cols].astype(F32)
        wide_v[index, pl.ds(0, rows // 2, stride=2), :] = half
        wide_v[index, pl.ds(1, rows // 2, stride=2), :] = half
        du_v[:, cols] = (wide_v[index] * slope[:, cols]).astype(BF16).astype(F32)


def backward_kernel(level, window, info, starts, arrived, slope, weight, _grad, _du, _token,
                    send_out, grad_out, du_out, _out, wide_v, mask_v, stacked_v, du_v):
    rows = BACK_ROWS[level]

    @pl.when(info[0] == level)
    def _():
        fill_masks(mask_v, starts, window, info[1], level, BACK_HALO[level], rows)
        spread_grads(arrived, wide_v, slope, du_v, rows)
        finish_backward(level, du_v, mask_v, stacked_v, weight, send_out, grad_out)
        own_grads(level, du_v, du_out)


def backward_call(level, window, info, starts, weight, token, arrived, slope, grad, du):
    rows = BACK_ROWS[level]
    return call(
        functools.partial(backward_kernel, level, window),
        f"backward{level}",
        2 * rows * C * C * TAPS,
        (info, starts),
        (arrived, slope, weight, grad, du),
        (shape_of(SEND_ROWS[level], C), shape_of(256, C), shape_of(256, C)),
        token,
        [
            pltpu.VMEM((C // 128, rows, 128), F32),
            pltpu.VMEM((TAPS, rows, 128), F32),
            pltpu.VMEM((rows, TAPS * C), BF16),
            pltpu.VMEM((rows, C), F32),
        ],
        aliases=((3, 1), (4, 2)),
    )


def first_du_kernel(info, arrived, slope, _du, _token, all_out, du_out, _out, wide_v, du_v):
    rows = BACK_ROWS[0]

    @pl.when(info[0] == 0)
    def _():
        spread_grads(arrived, wide_v, slope, du_v, rows)
        own_grads(0, du_v, du_out)
        all_out[...] = du_v[...].astype(BF16)


def first_du_call(info, token, arrived, slope, du):
    rows = BACK_ROWS[0]
    return call(
        first_du_kernel,
        "first_du",
        rows * C * 8,
        (info,),
        (arrived, slope, du),
        (shape_of(rows, C), shape_of(256, C)),
        token,
        [pltpu.VMEM((C // 128, rows, 128), F32), pltpu.VMEM((rows, C), F32)],
        aliases=((2, 1),),
    )


def first_grad_kernel(window, info, starts, du, weight, _grad, _token, grad_out, _out, mask_v,
                      stacked_v):
    rows = BACK_ROWS[0]

    @pl.when(info[0] == 0)
    def _():
        fill_masks(mask_v, starts, window, info[1], 0, BACK_HALO[0], rows)
        finish_backward(0, du, mask_v, stacked_v, weight, None, grad_out)


def first_grad_call(window, info, starts, weight, token, du, grad):
    rows = BACK_ROWS[0]
    return call(
        functools.partial(first_grad_kernel, window),
        "first_grad",
        2 * rows * C * C * TAPS,
        (info, starts),
        (du, weight, grad),
        (shape_of(256, C),),
        token,
        [pltpu.VMEM((TAPS, rows, 128), F32), pltpu.VMEM((rows, TAPS * C), BF16)],
        aliases=((2, 0),),
    )


def fill_order(seq, order_ref):
    row = lax.broadcasted_iota(jnp.int32, (C, 128), 0)
    place = (row * 2731) >> 16
    apart = ((place & 15) << 1) | (place >> 4)
    source = CHUNK * (seq ^ apart) + (row - CHUNK * place)
    lane = lax.broadcasted_iota(jnp.int32, (C, 128), 1)
    for index in range(C // 128):
        order_ref[:, index * 128 : (index + 1) * 128] = jnp.where(
            source == lane + index * 128, 1.0, 0.0
        ).astype(BF16)


def side_kernel(level, windows, info, starts, *refs):
    rows, halo, own = BACK_ROWS[level], BACK_HALO[level], OWN[level]
    inputs = 4 if level == 0 else windows
    xs = refs[:inputs]
    rest = refs[inputs + (1 if level == 0 else 2) :]
    side_out, _, mask_v, stacked_v, order_v = rest
    width = max(own, 128)
    skip = HALO[level] - halo

    @pl.when(info[0] == level)
    def _():
        fill_order(info[1], order_v)
        for window in range(windows):

            def read(index):
                cols = slice(index * 128, (index + 1) * 128)
                if level == 0:
                    x_in, near, far, rest = xs
                    first = max(window - 1, 0) * 64
                    far = rest if window else far
                    return with_edges(
                        x_in[window, :, cols],
                        near[window * 64 : window * 64 + 64, cols],
                        far[first : first + 64, cols],
                        info[1] % 2 == 1,
                        48,
                        16,
                    )
                return xs[window][skip : skip + rows, cols]

            fill_masks(mask_v, starts, window, info[1], level, halo, rows)
            stack_inputs(read, mask_v, stacked_v, rows)
            for tap in range(TAPS):
                part = stacked_v[halo : halo + own, tap * C : (tap + 1) * C]
                if own < width:
                    part = jnp.concatenate([part, jnp.zeros((width - own, C), BF16)], axis=0)
                found = lax.dot_general(
                    order_v[...], part, (((1,), (1,)), ((), ())), preferred_element_type=F32
                )
                lines = slice(tap * C, (tap + 1) * C)
                side_out[lines, window * 256 : window * 256 + width] = found.astype(BF16)
                if width < 256:
                    side_out[lines, window * 256 + width : (window + 1) * 256] = jnp.zeros(
                        (C, 256 - width), BF16
                    )


def side_call(level, windows, info, starts, token, side, *xs):
    rows = BACK_ROWS[level]
    held = () if side is None else (side,)
    return call(
        functools.partial(side_kernel, level, windows),
        f"side{level}",
        2 * windows * 256 * C * C * TAPS,
        (info, starts),
        (*xs, *held),
        (shape_of(TAPS * C, windows * 256),),
        token,
        [
            pltpu.VMEM((TAPS, rows, 128), F32),
            pltpu.VMEM((rows, TAPS * C), BF16),
            pltpu.VMEM((C, C), BF16),
        ],
        aliases=() if side is None else ((len(xs), 0),),
    )


def weight_kernel(quarter, side, *refs):
    dus = refs[:-4]
    _, send_out, keep_out, _ = refs[-4:]
    first = sum(PIECES[:quarter])
    for piece in range(PIECES[quarter]):
        tap, part = divmod(first + piece, 3)
        found = None
        for window, du in enumerate(dus):
            term = jnp.dot(
                side[tap * C : (tap + 1) * C, window * 256 : (window + 1) * 256],
                du[:, part * 256 : (part + 1) * 256],
                preferred_element_type=F32,
            )
            found = term if found is None else found + term
        found = found.reshape(2, 16, CHUNK, 256)
        cols = slice(piece * 256, (piece + 1) * 256)
        keep_out[:, :, cols] = found[0].astype(BF16)
        send_out[:, :, cols] = found[1].astype(BF16)


def weight_call(quarter, token, side, dus):
    width = PIECES[quarter] * 256
    shape = shape_of(16, CHUNK, width)
    return call(
        functools.partial(weight_kernel, quarter),
        f"weight{quarter}",
        2 * C * 768 * width,
        (),
        (side, *dus),
        (shape, shape),
        token,
        [],
    )


def quarter_plan(first_axis, *orders):
    held = [(y, z) for y in range(4) for z in range(4)]
    plan = []
    for axis, (one, two) in zip((first_axis, 1 - first_axis), orders):
        unit = (8, 2)[axis]
        for apart, gone in ((one, (one, 2)), (two, (two,))):
            leaving = [place for place in held if place[axis] in gone]
            leaving.sort(key=lambda place: (place[1 - axis], gone.index(place[axis])))
            staying = []
            for place in leaving:
                moved = list(place)
                moved[axis] ^= apart
                staying.append(tuple(moved))
            plan.append(
                (
                    apart * unit,
                    [held.index(place) for place in leaving],
                    [held.index(place) for place in staying],
                )
            )
            held = staying
    return plan


PLANS = (
    quarter_plan(1, (1, 3), (1, 3)),
    quarter_plan(1, (3, 1), (1, 3)),
    quarter_plan(0, (1, 3), (1, 3)),
    quarter_plan(0, (3, 1), (1, 3)),
)
GROUPS = ((0, 1), (2, 3))


def added(keep, arrived, source):
    return keep[source].astype(F32) + arrived[source].astype(F32)


def add_kernel(group, step, *refs):
    parts = GROUPS[group]
    keeps, arriveds = refs[0:2], refs[2:4]
    outs = refs[5:-1]
    first = 0
    for place, quarter in enumerate(parts):
        width = keeps[place].shape[-1]
        if step == 2:
            for apart in range(4):
                outs[apart][:, first : first + width] = added(
                    keeps[place], arriveds[place], apart
                ).astype(BF16)
        else:
            _, leaving, staying = PLANS[quarter][step]
            for target, sources in ((outs[place], staying), (outs[2 + place], leaving)):
                for row, source in enumerate(sources):
                    target[row] = added(keeps[place], arriveds[place], source).astype(BF16)
        first += width


def add_call(group, step, token, keeps, arriveds):
    widths = [keep.shape[-1] for keep in keeps]
    if step == 2:
        shapes = (shape_of(CHUNK, sum(widths)),) * 4
    else:
        half = len(PLANS[0][step][1])
        shapes = tuple(shape_of(half, CHUNK, width) for width in widths) * 2
    *outs, token = call(
        functools.partial(add_kernel, group, step),
        f"add{step}",
        4000000 // (1 << step),
        (),
        (*keeps, *arriveds),
        shapes,
        token,
        [],
    )
    return outs, token


def final_kernel(*refs):
    out = refs[9]
    for group, quarters in enumerate(GROUPS):
        total = None
        for ref in refs[group * 4 : group * 4 + 4]:
            term = ref[...].astype(F32)
            total = term if total is None else total + term
        piece = sum(PIECES[: quarters[0]])
        for place in range(total.shape[1] // 256):
            tap, part = divmod(piece + place, 3)
            out[tap, :, part * 256 : (part + 1) * 256] = total[:, place * 256 : (place + 1) * 256]


def section_pairs(source, target, shards):
    return [(source * shards + place, target * shards + place) for place in range(shards)]


def apart_pairs(sections, shards, apart):
    return [
        (section * shards + place, section * shards + (place ^ apart))
        for section in range(sections)
        for place in range(shards)
    ]


def body(dna_embed, conv_weight, interval_starts, cotangent):
    windows = dna_embed.shape[0]
    sections = lax.axis_size("section")
    shards = lax.axis_size("seq")
    section_index = lax.axis_index("section")
    seq_index = lax.axis_index("seq")
    info = jnp.stack([section_index, seq_index]).astype(jnp.int32)
    weight = jnp.transpose(conv_weight[0], (1, 0, 2)).reshape(TAPS * C, C)
    starts = interval_starts
    token = jnp.zeros((8, 128), F32)

    ends = (0, sections - 1)
    near_pairs = [
        pair for pair in apart_pairs(sections, shards, 1) if pair[0] // shards in ends
    ]
    far_pairs = [
        (section * shards + place, section * shards + place + by)
        for section in ends
        for place in range(shards)
        for by in (1 if place % 2 else -1,)
        if 0 <= place + by < shards
    ]
    near, far, rest, token = edges_call(info, token, dna_embed, cotangent)
    near = lax.ppermute(near, AXES, near_pairs)
    far = lax.ppermute(far, AXES, [pair for pair in far_pairs if pair[0] < shards])
    rest = lax.ppermute(rest, AXES, far_pairs)

    def relay(value, source, target):
        return lax.ppermute(value, AXES, section_pairs(source, target, shards))

    inputs = [[None] * windows for _ in range(4)]
    slopes = [[None] * windows for _ in range(4)]
    grads = [None] * windows
    dus = [None] * windows
    wide_du = [None] * windows
    arrived = [None] * windows
    side = None

    def forward(level, window, send=True):
        nonlocal token
        xs = (inputs[level][window],)
        if level == 0:
            xs = (dna_embed, near, rest if window else far)
        pooled, slopes[level][window], token = forward_call(
            level, window, info, starts, weight, token, *xs
        )
        if send:
            inputs[level + 1][window] = relay(pooled, level, level + 1)
        return pooled

    def turn(window, *held):
        nonlocal token
        send, grads[window], dus[window], token = last_call(
            window, info, starts, weight, turned, token, inputs[3][window], cotangent, near, rest,
            *held,
        )
        if held:
            pairs = section_pairs(2, 3, shards) + section_pairs(3, 2, shards)
            arrived[window] = lax.ppermute(send, AXES, pairs)
        else:
            arrived[window] = relay(send, 3, 2)
        return arrived[window]

    def backward(level, window):
        nonlocal token
        send, grads[window], dus[window], token = backward_call(
            level, window, info, starts, turned, token, arrived[window], slopes[level][window],
            grads[window], dus[window],
        )
        arrived[window] = relay(send, level, level - 1)

    def arrive(window):
        nonlocal token
        wide_du[window], dus[window], token = first_du_call(
            info, token, arrived[window], slopes[0][window], dus[window]
        )

    def first_grad(window):
        nonlocal token
        grads[window], token = first_grad_call(
            window, info, starts, weight, token, wide_du[window], grads[window]
        )

    def sideways(level):
        nonlocal side, token
        xs = (dna_embed, near, far, rest) if level == 0 else inputs[level]
        side, token = side_call(level, windows, info, starts, token, side, *xs)

    forward(0, 0)
    turned, token = turn_call(info, token, weight)
    forward(0, 1)
    forward(0, 2)
    sideways(0)
    forward(1, 0)
    forward(1, 1)
    forward(2, 0)
    forward(1, 2)
    sideways(1)
    inputs[3][1] = turn(0, forward(2, 1, send=False))
    forward(2, 2)
    turn(1)
    backward(2, 0)
    turn(2)
    sideways(3)
    backward(2, 1)
    backward(1, 0)
    backward(2, 2)
    sideways(2)
    backward(1, 1)
    backward(1, 2)
    arrive(0)
    first_grad(0)
    arrive(1)
    arrive(2)

    keeps, arriveds = [[], []], [[], []]

    def weigh(group):
        nonlocal token
        for quarter in GROUPS[group]:
            send, keep, token = weight_call(quarter, token, side, dus)
            keeps[group].append(keep)
            arriveds[group].append(lax.ppermute(send, AXES, apart_pairs(sections, shards, 1)))

    def trade(value, apart):
        return lax.ppermute(value, AXES, apart_pairs(sections, shards, apart))

    def pass_on(group, step):
        nonlocal token
        outs, token = add_call(group, step, token, keeps[group], arriveds[group])
        if step == 2:
            unit = 8 if group == 0 else 2
            keeps[group] = outs[:1]
            arriveds[group] = [trade(outs[apart], apart * unit) for apart in (1, 3, 2)]
        else:
            keeps[group] = outs[:2]
            arriveds[group] = [
                trade(leaving, PLANS[quarter][step][0])
                for quarter, leaving in zip(GROUPS[group], outs[2:])
            ]

    weigh(0)
    weigh(1)
    pass_on(0, 0)
    pass_on(1, 0)
    first_grad(1)
    first_grad(2)
    pass_on(0, 1)
    pass_on(1, 1)
    pass_on(0, 2)
    pass_on(1, 2)
    weight_grad, token = call(
        final_kernel, "final", 1000000, (), (*keeps[0], *arriveds[0], *keeps[1], *arriveds[1]),
        (shape_of(TAPS, CHUNK, C, dtype=F32),), token, [],
    )
    weight_grad = jnp.transpose(weight_grad, (1, 0, 2))[None]
    return (weight_grad, jnp.stack(grads)[None])


def solution(mesh):
    placed = (P(None, "seq", None), P("section", None, None, None), P(), P(None, "seq", None))
    return jax.shard_map(
        body,
        mesh=mesh,
        in_specs=placed,
        out_specs=(P("section", "seq", None, None), P("section", None, "seq", None)),
        check_vma=False,
    )
```

```python
import functools

import jax
import jax.numpy as jnp
from jax import lax
from jax.experimental import pallas as pl
from jax.experimental.pallas import tpu as pltpu
from jax.sharding import PartitionSpec as P

C = 768
TAPS = 5
AXES = ("section", "seq")
OWN = (256, 128, 64, 32)
HALO = (64, 32, 16, 8)
ROWS = (384, 192, 96, 48)
BACK_HALO = (16, 16, 16, 8)
BACK_ROWS = (288, 160, 96, 48)
SEND_ROWS = (0, 144, 80, 48)
CHUNK = 24
LIMIT = 24 * 1024 * 1024
F32 = jnp.float32
BF16 = jnp.bfloat16
ANY = pl.BlockSpec(memory_space=pl.ANY)
SMEM = pl.BlockSpec(memory_space=pltpu.SMEM)
VMEM = pl.BlockSpec(memory_space=pltpu.VMEM)
PIECES = (8, 7)


def shape_of(*dims, dtype=BF16):
    return jax.ShapeDtypeStruct(dims, dtype)


def call(kernel, name, flops, smem, vmem, outs, token, scratch, aliases=(), held=None, far_out=None):
    extra = () if held is None else (held,)
    operands = (*smem, *vmem, *extra, token)
    count = len(operands)
    pairs = {len(smem) + place: out for place, out in aliases}
    far_shape = held if held is not None else far_out
    far = () if far_shape is None else (shape_of(*far_shape.shape, dtype=far_shape.dtype),)
    if extra:
        pairs[count - 2] = len(outs)
    pairs[count - 1] = len(outs) + len(far)
    return pl.pallas_call(
        kernel,
        out_shape=(*outs, *far, jax.ShapeDtypeStruct(token.shape, token.dtype)),
        in_specs=[SMEM] * len(smem) + [VMEM] * len(vmem) + [ANY] * (len(extra) + 1),
        out_specs=(*[VMEM] * len(outs), *[ANY] * (len(far) + 1)),
        scratch_shapes=scratch,
        input_output_aliases=pairs,
        compiler_params=pltpu.CompilerParams(vmem_limit_bytes=LIMIT),
        cost_estimate=pl.CostEstimate(flops=int(flops), bytes_accessed=1000000, transcendentals=0),
        name=name,
    )(*operands)


def no_cut(starts, window, positions, level, length):
    cut = positions == length
    for entry in range(starts.shape[1]):
        first = (starts[window, entry] + ((1 << level) - 1)) >> level
        cut = cut | (positions == first)
    return jnp.where(cut, 0.0, 1.0)


def roll_rows(value, by):
    return pltpu.roll(value, by % value.shape[0], 0)


def fill_masks(mask_ref, starts, window, seq, level, halo, rows):
    own = OWN[level]
    length = own * 32
    row = lax.broadcasted_iota(jnp.int32, (rows, 128), 0)
    positions = row + (seq * own - halo)
    inside = jnp.where((positions >= 0) & (positions < length), 1.0, 0.0)
    free = no_cut(starts, window, positions, level, length)
    before = inside * free
    after = inside * roll_rows(free, -1)
    mask_ref[0, 0:rows] = before * roll_rows(free, 1)
    mask_ref[1, 0:rows] = before
    mask_ref[2, 0:rows] = inside
    mask_ref[3, 0:rows] = after
    mask_ref[4, 0:rows] = after * roll_rows(free, -2)


def stack_inputs(read, mask_ref, stacked_ref, rows):
    for index in range(C // 128):
        tile = read(index).astype(F32)
        for tap in range(TAPS):
            moved = roll_rows(tile, 2 - tap) if tap != 2 else tile
            first = tap * C + index * 128
            stacked_ref[0:rows, first : first + 128] = (moved * mask_ref[tap, 0:rows]).astype(BF16)


def stack_grads(value_ref, mask_ref, stacked_ref, rows):
    for index in range(C // 128):
        tile = value_ref[0:rows, index * 128 : (index + 1) * 128].astype(F32)
        for tap in range(TAPS):
            moved = tile * mask_ref[tap, 0:rows]
            moved = roll_rows(moved, tap - 2) if tap != 2 else moved
            first = tap * C + index * 128
            stacked_ref[0:rows, first : first + 128] = moved.astype(BF16)


def conv_columns(stacked_ref, weight_ref, index):
    return jnp.dot(
        stacked_ref[...], weight_ref[:, index * 256 : (index + 1) * 256], preferred_element_type=F32
    )


def back_columns(stacked_ref, weight_ref, index, turned):
    if turned:
        return conv_columns(stacked_ref, weight_ref, index)
    total = None
    for tap in range(TAPS):
        first = tap * C + index * 256
        part = lax.dot_general(
            stacked_ref[:, tap * C : (tap + 1) * C],
            weight_ref[first : first + 256, :],
            (((1,), (1,)), ((), ())),
            preferred_element_type=F32,
        )
        total = part if total is None else total + part
    return total


def turn_kernel(info, weight, _, turned_out, _out, unit_v):
    @pl.when(info[0] > 0)
    def _():
        row = lax.broadcasted_iota(jnp.int32, (C, 128), 0)
        lane = lax.broadcasted_iota(jnp.int32, (C, 128), 1)
        for index in range(C // 128):
            unit_v[:, index * 128 : (index + 1) * 128] = jnp.where(
                row == lane + index * 128, 1.0, 0.0
            ).astype(BF16)
        for tap in range(TAPS):
            lines = slice(tap * C, (tap + 1) * C)
            for index in range(C // 256):
                first = tap * C + index * 256
                turned_out[lines, index * 256 : (index + 1) * 256] = lax.dot_general(
                    unit_v[...],
                    weight[first : first + 256, :],
                    (((1,), (1,)), ((), ())),
                    preferred_element_type=F32,
                ).astype(BF16)


def turn_call(info, token, weight):
    return call(
        turn_kernel, "turn", 2 * C * C * C * TAPS, (info,), (weight,), (shape_of(TAPS * C, C),),
        token, [pltpu.VMEM((C, C), BF16)],
    )


def gelu_and_slope(u):
    scale = 0.7978845608028654
    square = u * u
    bend = jnp.tanh(scale * (u + 0.044715 * square * u))
    half = 0.5 * (1.0 + bend)
    slope = half + 0.5 * u * (1.0 - bend * bend) * (scale * (1.0 + 0.134145 * square))
    return u * half, slope


def edges_kernel(windows, info, dna, cot, _, near, first, rest, _out):
    own, part = OWN[0], cot.shape[1]
    odd = info[1] % 2 == 1

    def fill(leading_to_near):
        near_x, far_x = (0, own - 64) if leading_to_near else (own - 64, 0)
        near_c, far_c = (0, part - 16) if leading_to_near else (part - 16, 0)
        for window in range(windows):
            rows = slice(window * 64, window * 64 + 64)

            @pl.when(info[0] == 0)
            def _():
                near[rows, :] = dna[window, near_x : near_x + 64, :]
                if window == 0:
                    first[...] = dna[0, far_x : far_x + 64, :]
                else:
                    rest[(window - 1) * 64 : window * 64, :] = dna[window, far_x : far_x + 64, :]

            lines = slice(window * 16, window * 16 + 16)

            @pl.when(info[0] == 3)
            def _():
                near[lines, :] = cot[window, near_c : near_c + 16, :]
                rest[lines, :] = cot[window, far_c : far_c + 16, :]

    pl.when(odd)(functools.partial(fill, True))
    pl.when(jnp.logical_not(odd))(functools.partial(fill, False))


def edges_call(info, token, dna, cot):
    windows = dna.shape[0]
    return call(
        functools.partial(edges_kernel, windows),
        "edges",
        2e10,
        (info,),
        (dna, cot),
        (shape_of(windows * 64, C), shape_of(64, C), shape_of((windows - 1) * 64, C)),
        token,
        [],
    )


def sides(odd, near, far):
    near, far = near.astype(F32), far.astype(F32)
    return jnp.where(odd, near, far), jnp.where(odd, far, near)


def with_edges(own, near, far, odd, low, high):
    ahead, behind = sides(odd, near, far)
    return jnp.concatenate([ahead[low:], own.astype(F32), behind[:high]], axis=0)


def forward_kernel(level, window, info, starts, *refs):
    rows, back = ROWS[level], BACK_ROWS[level]
    skip = HALO[level] - BACK_HALO[level]
    inputs = 3 if level == 0 else 1
    xs = refs[:inputs]
    weight, _, pooled_out, slope_out, _, mask_v, stacked_v, act_v = refs[inputs:]

    def read(index):
        cols = slice(index * 128, (index + 1) * 128)
        if level == 0:
            x_in, near, far = xs
            first = max(window - 1, 0) * 64
            return with_edges(
                x_in[window, :, cols],
                near[window * 64 : window * 64 + 64, cols],
                far[first : first + 64, cols],
                info[1] % 2 == 1,
                0,
                64,
            )
        return xs[0][:, cols]

    @pl.when(info[0] == level)
    def _():
        fill_masks(mask_v, starts, window, info[1], level, HALO[level], rows)
        stack_inputs(read, mask_v, stacked_v, rows)
        for index in range(C // 256):
            act, slope = gelu_and_slope(conv_columns(stacked_v, weight, index))
            slope_out[:, index * 256 : (index + 1) * 256] = slope[skip : skip + back]
            for half in range(2):
                place = index * 2 + half
                act_v[place] = act[:, half * 128 : (half + 1) * 128]
                even = act_v[place, pl.ds(0, rows // 2, stride=2), :]
                odd = act_v[place, pl.ds(1, rows // 2, stride=2), :]
                pooled_out[:, place * 128 : (place + 1) * 128] = (0.5 * (even + odd)).astype(BF16)


def forward_call(level, window, info, starts, weight, token, *xs):
    rows, back = ROWS[level], BACK_ROWS[level]
    return call(
        functools.partial(forward_kernel, level, window),
        f"forward{level}",
        2 * rows * C * C * TAPS,
        (info, starts),
        (*xs, weight),
        (shape_of(rows // 2, C), shape_of(back, C, dtype=F32)),
        token,
        [
            pltpu.VMEM((TAPS, rows, 128), F32),
            pltpu.VMEM((rows, TAPS * C), BF16),
            pltpu.VMEM((C // 128, rows, 128), F32),
        ],
    )


def finish_backward(level, du_v, mask_v, stacked_v, weight, send_out, grad_out):
    rows, own, halo = BACK_ROWS[level], OWN[level], BACK_HALO[level]
    send = SEND_ROWS[level]
    trim = (rows - send) // 2
    stack_grads(du_v, mask_v, stacked_v, rows)
    for index in range(C // 256):
        found = back_columns(stacked_v, weight, index, level > 0)
        cols = slice(index * 256, (index + 1) * 256)
        if send:
            send_out[:, cols] = found[trim : trim + send].astype(BF16)
        grad_out[0:own, cols] = found[halo : halo + own].astype(BF16)
    if own < 256:
        grad_out[own:, :] = jnp.zeros((256 - own, C), BF16)


def own_grads(level, du_v, du_out):
    own, halo = OWN[level], BACK_HALO[level]
    du_out[0:own, :] = du_v[halo : halo + own, :].astype(BF16)
    if own < 256:
        du_out[own:, :] = jnp.zeros((256 - own, C), BF16)


def last_kernel(window, info, starts, x_in, cot, near, far, weight, turned, *refs):
    send_out, grad_out, du_out, _, mask_v, stacked_v, du_v = refs[-7:]
    level, rows = 3, ROWS[3]
    if len(refs) == 9:

        @pl.when(info[0] == 2)
        def _():
            send_out[...] = refs[0][...]

    @pl.when(info[0] == level)
    def _():
        fill_masks(mask_v, starts, window, info[1], level, HALO[level], rows)
        stack_inputs(
            lambda index: x_in[:, index * 128 : (index + 1) * 128], mask_v, stacked_v, rows
        )
        for index in range(C // 256):
            _, slope = gelu_and_slope(conv_columns(stacked_v, weight, index))
            cols = slice(index * 256, (index + 1) * 256)
            lines = slice(window * 16, window * 16 + 16)
            g = with_edges(
                cot[window, :, cols], near[lines, cols], far[lines, cols], info[1] % 2 == 1, 8, 8
            )
            du_v[:, cols] = (g * slope).astype(BF16).astype(F32)
        finish_backward(level, du_v, mask_v, stacked_v, turned, send_out, grad_out)
        own_grads(level, du_v, du_out)


def last_call(window, info, starts, weight, turned, token, x, cot, near, far, *held):
    rows = ROWS[3]
    return call(
        functools.partial(last_kernel, window),
        "last",
        4 * rows * C * C * TAPS,
        (info, starts),
        (x, cot, near, far, weight, turned, *held),
        (shape_of(rows, C), shape_of(256, C), shape_of(256, C)),
        token,
        [
            pltpu.VMEM((TAPS, rows, 128), F32),
            pltpu.VMEM((rows, TAPS * C), BF16),
            pltpu.VMEM((rows, C), F32),
        ],
        aliases=((6, 0),) if held else (),
    )


def spread_grads(arrived, wide_v, slope, du_v, rows):
    for index in range(C // 128):
        cols = slice(index * 128, (index + 1) * 128)
        half = 0.5 * arrived[:, cols].astype(F32)
        wide_v[index, pl.ds(0, rows // 2, stride=2), :] = half
        wide_v[index, pl.ds(1, rows // 2, stride=2), :] = half
        du_v[:, cols] = (wide_v[index] * slope[:, cols]).astype(BF16).astype(F32)


def keep_later(level, info, pairs):
    @pl.when(info[0] > level)
    def _():
        for source, target in pairs:
            target[...] = source[...]


def backward_kernel(level, window, info, starts, arrived, slope, weight, grad, du, _token,
                    send_out, grad_out, du_out, _out, wide_v, mask_v, stacked_v, du_v):
    rows = BACK_ROWS[level]
    keep_later(level, info, ((grad, grad_out), (du, du_out)))

    @pl.when(info[0] == level)
    def _():
        fill_masks(mask_v, starts, window, info[1], level, BACK_HALO[level], rows)
        spread_grads(arrived, wide_v, slope, du_v, rows)
        finish_backward(level, du_v, mask_v, stacked_v, weight, send_out, grad_out)
        own_grads(level, du_v, du_out)


def backward_call(level, window, info, starts, weight, token, arrived, slope, grad, du):
    rows = BACK_ROWS[level]
    return call(
        functools.partial(backward_kernel, level, window),
        f"backward{level}",
        2 * rows * C * C * TAPS,
        (info, starts),
        (arrived, slope, weight, grad, du),
        (shape_of(SEND_ROWS[level], C), shape_of(256, C), shape_of(256, C)),
        token,
        [
            pltpu.VMEM((C // 128, rows, 128), F32),
            pltpu.VMEM((TAPS, rows, 128), F32),
            pltpu.VMEM((rows, TAPS * C), BF16),
            pltpu.VMEM((rows, C), F32),
        ],
        aliases=((3, 1), (4, 2)),
    )


def first_du_kernel(info, arrived, slope, du, _token, all_out, du_out, _out, wide_v, du_v):
    rows = BACK_ROWS[0]
    keep_later(0, info, ((du, du_out),))

    @pl.when(info[0] == 0)
    def _():
        spread_grads(arrived, wide_v, slope, du_v, rows)
        own_grads(0, du_v, du_out)
        all_out[...] = du_v[...].astype(BF16)


def first_du_call(info, token, arrived, slope, du):
    rows = BACK_ROWS[0]
    return call(
        first_du_kernel,
        "first_du",
        rows * C * 8,
        (info,),
        (arrived, slope, du),
        (shape_of(rows, C), shape_of(256, C)),
        token,
        [pltpu.VMEM((C // 128, rows, 128), F32), pltpu.VMEM((rows, C), F32)],
        aliases=((2, 1),),
    )


def first_grad_kernel(window, info, starts, du, weight, grad, _token, grad_out, _out, mask_v,
                      stacked_v):
    rows = BACK_ROWS[0]
    keep_later(0, info, ((grad, grad_out),))

    @pl.when(info[0] == 0)
    def _():
        fill_masks(mask_v, starts, window, info[1], 0, BACK_HALO[0], rows)
        finish_backward(0, du, mask_v, stacked_v, weight, None, grad_out)


def first_grad_call(window, info, starts, weight, token, du, grad):
    rows = BACK_ROWS[0]
    return call(
        functools.partial(first_grad_kernel, window),
        "first_grad",
        2 * rows * C * C * TAPS,
        (info, starts),
        (du, weight, grad),
        (shape_of(256, C),),
        token,
        [pltpu.VMEM((TAPS, rows, 128), F32), pltpu.VMEM((rows, TAPS * C), BF16)],
        aliases=((2, 0),),
    )


def gather_kernel(windows, *refs):
    out = refs[-2]
    for window in range(windows):
        out[0, window] = refs[window][...]


def gather_call(token, grads):
    return call(
        functools.partial(gather_kernel, len(grads)), "gather", 1000000, (), tuple(grads),
        (shape_of(1, len(grads), 256, C),), token, [],
    )


def fill_order(seq, order_ref):
    row = lax.broadcasted_iota(jnp.int32, (C, 128), 0)
    place = (row * 2731) >> 16
    swap = (seq ^ (place >> 4)) & 1
    one, two = place & 3, (place >> 2) & 3
    along_z, along_y = jnp.where(swap == 1, two, one), jnp.where(swap == 1, one, two)
    apart = (along_y << 3) | (along_z << 1) | (place >> 4)
    source = CHUNK * (seq ^ apart) + (row - CHUNK * place)
    lane = lax.broadcasted_iota(jnp.int32, (C, 128), 1)
    for index in range(C // 128):
        order_ref[:, index * 128 : (index + 1) * 128] = jnp.where(
            source == lane + index * 128, 1.0, 0.0
        ).astype(BF16)


def side_kernel(level, windows, info, starts, *refs):
    rows, halo, own = BACK_ROWS[level], BACK_HALO[level], OWN[level]
    inputs = 4 if level == 0 else windows
    xs = refs[:inputs]
    side_out, _, mask_v, stacked_v, order_v, side_v, sems = refs[-7:]
    leaving = []
    width = max(own, 128)
    skip = HALO[level] - halo

    @pl.when(info[0] == level)
    def _():
        fill_order(info[1], order_v)
        for window in range(windows):

            def read(index):
                cols = slice(index * 128, (index + 1) * 128)
                if level == 0:
                    x_in, near, far, rest = xs
                    first = max(window - 1, 0) * 64
                    far = rest if window else far
                    return with_edges(
                        x_in[window, :, cols],
                        near[window * 64 : window * 64 + 64, cols],
                        far[first : first + 64, cols],
                        info[1] % 2 == 1,
                        48,
                        16,
                    )
                return xs[window][skip : skip + rows, cols]

            fill_masks(mask_v, starts, window, info[1], level, halo, rows)
            stack_inputs(read, mask_v, stacked_v, rows)
            for tap in range(TAPS):
                part = stacked_v[halo : halo + own, tap * C : (tap + 1) * C]
                if own < width:
                    part = jnp.concatenate([part, jnp.zeros((width - own, C), BF16)], axis=0)
                found = lax.dot_general(
                    order_v[...], part, (((1,), (1,)), ((), ())), preferred_element_type=F32
                )
                lines = slice(tap * C, (tap + 1) * C)
                side_v[lines, window * 256 : window * 256 + width] = found.astype(BF16)
                if width < 256:
                    side_v[lines, window * 256 + width : (window + 1) * 256] = jnp.zeros(
                        (C, 256 - width), BF16
                    )
            cols = pl.ds(window * 256, 256)
            leaving.append(
                pltpu.make_async_copy(side_v.at[:, cols], side_out.at[:, cols], sems.at[window])
            )
            leaving[-1].start()
        for copy in leaving:
            copy.wait()


def side_call(level, windows, info, starts, token, side, *xs):
    rows = BACK_ROWS[level]
    return call(
        functools.partial(side_kernel, level, windows),
        f"side{level}",
        2 * windows * 256 * C * C * TAPS,
        (info, starts),
        xs,
        (),
        token,
        [
            pltpu.VMEM((TAPS, rows, 128), F32),
            pltpu.VMEM((rows, TAPS * C), BF16),
            pltpu.VMEM((C, C), BF16),
            pltpu.VMEM((TAPS * C, windows * 256), BF16),
            pltpu.SemaphoreType.DMA((windows,)),
        ],
        held=side,
        far_out=shape_of(TAPS * C, windows * 256),
    )


def weight_kernel(quarter, side, *refs):
    dus = refs[:-4]
    _, send_out, keep_out, _ = refs[-4:]
    first = sum(PIECES[:quarter])
    for piece in range(PIECES[quarter]):
        tap, part = divmod(first + piece, 3)
        found = None
        for window, du in enumerate(dus):
            term = jnp.dot(
                side[tap * C : (tap + 1) * C, window * 256 : (window + 1) * 256],
                du[:, part * 256 : (part + 1) * 256],
                preferred_element_type=F32,
            )
            found = term if found is None else found + term
        found = found.reshape(2, 16, CHUNK, 256)
        cols = slice(piece * 256, (piece + 1) * 256)
        keep_out[:, :, cols] = found[0].astype(BF16)
        send_out[:, :, cols] = found[1].astype(BF16)


def weight_call(quarter, token, side, dus):
    width = PIECES[quarter] * 256
    shape = shape_of(16, CHUNK, width)
    return call(
        functools.partial(weight_kernel, quarter),
        f"weight{quarter}",
        2 * C * 768 * width,
        (),
        (side, *dus),
        (shape, shape),
        token,
        [],
    )


def half_plan(*orders):
    held = [(second, first) for second in range(4) for first in range(4)]
    plan = []
    for axis, (one, two) in zip((1, 0), orders):
        for apart, gone in ((one, (one, 2)), (two, (two,))):
            leaving = [place for place in held if place[axis] in gone]
            leaving.sort(key=lambda place: (place[1 - axis], gone.index(place[axis])))
            staying = []
            for place in leaving:
                moved = list(place)
                moved[axis] ^= apart
                staying.append(tuple(moved))
            plan.append(
                (
                    axis,
                    apart,
                    [held.index(place) for place in leaving],
                    [held.index(place) for place in staying],
                )
            )
            held = staying
    return plan


PLANS = (half_plan((1, 3), (1, 3)), half_plan((3, 1), (3, 1)))


def added(keep, arrived, source):
    return keep[source].astype(F32) + arrived[source].astype(F32)


def add_kernel(half, step, keep, arrived, _, stay_out, leave_out, _out):
    _, _, leaving, staying = PLANS[half][step]
    for target, sources in ((stay_out, staying), (leave_out, leaving)):
        for row, source in enumerate(sources):
            target[row] = added(keep, arrived, source).astype(BF16)


def add_call(half, step, token, keep, arrived):
    shape = shape_of(len(PLANS[half][step][2]), CHUNK, keep.shape[-1])
    return call(
        functools.partial(add_kernel, half, step),
        f"add{half}_{step}",
        4000000 // (1 << step),
        (),
        (keep, arrived),
        (shape, shape),
        token,
        [],
    )


def final_kernel(half, keep, arrived, *refs):
    out = refs[-2]
    total = added(keep, arrived, 0)
    piece = sum(PIECES[:half])
    for place in range(piece + PIECES[half]):
        tap, part = divmod(place, 3)
        cols = slice(part * 256, (part + 1) * 256)
        if place < piece:
            out[tap, :, cols] = refs[0][tap, :, cols]
        else:
            out[tap, :, cols] = total[:, (place - piece) * 256 : (place - piece + 1) * 256]


def final_call(half, token, keep, arrived, *held):
    return call(
        functools.partial(final_kernel, half),
        f"final{half}",
        1000000,
        (),
        (keep, arrived, *held),
        (shape_of(TAPS, CHUNK, C, dtype=F32),),
        token,
        [],
        aliases=((2, 0),) if held else (),
    )


def section_pairs(source, target, shards):
    return [(source * shards + place, target * shards + place) for place in range(shards)]


def apart_pairs(sections, shards, apart):
    return [
        (section * shards + place, section * shards + (place ^ apart))
        for section in range(sections)
        for place in range(shards)
    ]


def mixed_pairs(sections, shards, axis, apart):
    units = (8, 2) if axis == 0 else (2, 8)
    return [
        (section * shards + place, section * shards + (place ^ (apart * units[place % 2])))
        for section in range(sections)
        for place in range(shards)
    ]


def body(dna_embed, conv_weight, interval_starts, cotangent):
    windows = dna_embed.shape[0]
    sections = lax.axis_size("section")
    shards = lax.axis_size("seq")
    section_index = lax.axis_index("section")
    seq_index = lax.axis_index("seq")
    info = jnp.stack([section_index, seq_index]).astype(jnp.int32)
    weight = jnp.transpose(conv_weight[0], (1, 0, 2)).reshape(TAPS * C, C)
    starts = interval_starts
    token = jnp.zeros((8, 128), F32)

    ends = (0, sections - 1)
    near_pairs = [
        pair for pair in apart_pairs(sections, shards, 1) if pair[0] // shards in ends
    ]
    far_pairs = [
        (section * shards + place, section * shards + place + by)
        for section in ends
        for place in range(shards)
        for by in (1 if place % 2 else -1,)
        if 0 <= place + by < shards
    ]
    near, far, rest, token = edges_call(info, token, dna_embed, cotangent)
    near = lax.ppermute(near, AXES, near_pairs)
    far = lax.ppermute(far, AXES, [pair for pair in far_pairs if pair[0] < shards])
    rest = lax.ppermute(rest, AXES, far_pairs)

    def relay(value, source, target):
        return lax.ppermute(value, AXES, section_pairs(source, target, shards))

    inputs = [[None] * windows for _ in range(4)]
    slopes = [[None] * windows for _ in range(4)]
    grads = [None] * windows
    dus = [None] * windows
    wide_du = [None] * windows
    arrived = [None] * windows
    side = None

    def forward(level, window, send=True):
        nonlocal token
        xs = (inputs[level][window],)
        if level == 0:
            xs = (dna_embed, near, rest if window else far)
        pooled, slopes[level][window], token = forward_call(
            level, window, info, starts, weight, token, *xs
        )
        if send:
            inputs[level + 1][window] = relay(pooled, level, level + 1)
        return pooled

    def turn(window, *held):
        nonlocal token
        send, grads[window], dus[window], token = last_call(
            window, info, starts, weight, turned, token, inputs[3][window], cotangent, near, rest,
            *held,
        )
        if held:
            pairs = section_pairs(2, 3, shards) + section_pairs(3, 2, shards)
            arrived[window] = lax.ppermute(send, AXES, pairs)
        else:
            arrived[window] = relay(send, 3, 2)
        return arrived[window]

    def backward(level, window):
        nonlocal token
        send, grads[window], dus[window], token = backward_call(
            level, window, info, starts, turned, token, arrived[window], slopes[level][window],
            grads[window], dus[window],
        )
        arrived[window] = relay(send, level, level - 1)

    def arrive(window):
        nonlocal token
        wide_du[window], dus[window], token = first_du_call(
            info, token, arrived[window], slopes[0][window], dus[window]
        )

    def first_grad(window):
        nonlocal token
        grads[window], token = first_grad_call(
            window, info, starts, weight, token, wide_du[window], grads[window]
        )

    def sideways(level):
        nonlocal side, token
        xs = (dna_embed, near, far, rest) if level == 0 else inputs[level]
        side, token = side_call(level, windows, info, starts, token, side, *xs)

    forward(0, 0)
    turned, token = turn_call(info, token, weight)
    forward(0, 1)
    forward(0, 2)
    sideways(0)
    forward(1, 0)
    forward(1, 1)
    forward(2, 0)
    forward(1, 2)
    sideways(1)
    inputs[3][1] = turn(0, forward(2, 1, send=False))
    forward(2, 2)
    turn(1)
    turn(2)
    backward(2, 0)
    backward(2, 1)
    backward(2, 2)
    sideways(3)
    sideways(2)
    backward(1, 0)
    backward(1, 1)
    backward(1, 2)
    arrive(0)
    first_grad(0)
    arrive(1)
    arrive(2)

    keeps, arriveds = [None, None], [None, None]

    def weigh(half):
        nonlocal token
        send, keeps[half], token = weight_call(half, token, side, dus)
        arriveds[half] = lax.ppermute(send, AXES, apart_pairs(sections, shards, 1))

    def pass_on(half, step):
        nonlocal token
        keeps[half], leaving, token = add_call(half, step, token, keeps[half], arriveds[half])
        axis, apart = PLANS[half][step][:2]
        arriveds[half] = lax.ppermute(leaving, AXES, mixed_pairs(sections, shards, axis, apart))

    weigh(0)
    weigh(1)
    pass_on(0, 0)
    pass_on(1, 0)
    first_grad(1)
    first_grad(2)
    input_grads, token = gather_call(token, grads)
    for step in range(1, 4):
        pass_on(0, step)
        pass_on(1, step)
    weight_grad, token = final_call(0, token, keeps[0], arriveds[0])
    weight_grad, token = final_call(1, token, keeps[1], arriveds[1], weight_grad)
    weight_grad = jnp.transpose(weight_grad, (1, 0, 2))[None]
    return (weight_grad, input_grads)


def solution(mesh):
    placed = (P(None, "seq", None), P("section", None, None, None), P(), P(None, "seq", None))
    return jax.shard_map(
        body,
        mesh=mesh,
        in_specs=placed,
        out_specs=(P("section", "seq", None, None), P("section", None, "seq", None)),
        check_vma=False,
    )
```

```python
import functools

import jax
import jax.numpy as jnp
from jax import lax
from jax.experimental import pallas as pl
from jax.experimental.pallas import tpu as pltpu
from jax.sharding import PartitionSpec as P

C = 768
TAPS = 5
AXES = ("section", "seq")
OWN = (256, 128, 64, 32)
HALO = (64, 32, 16, 8)
ROWS = (384, 192, 96, 48)
BACK_HALO = (16, 16, 16, 8)
BACK_ROWS = (288, 160, 96, 48)
SEND_ROWS = (0, 144, 80, 48)
CHUNK = 24
LIMIT = 16 * 1024 * 1024
F32 = jnp.float32
BF16 = jnp.bfloat16
ANY = pl.BlockSpec(memory_space=pl.ANY)
SMEM = pl.BlockSpec(memory_space=pltpu.SMEM)
VMEM = pl.BlockSpec(memory_space=pltpu.VMEM)
PIECES = (8, 7)
BLOCKS_UNROLL = 3


def shape_of(*dims, dtype=BF16):
    return jax.ShapeDtypeStruct(dims, dtype)


def call(kernel, name, flops, smem, vmem, outs, token, scratch, aliases=(), held=None, far_out=None):
    extra = () if held is None else (held,)
    operands = (*smem, *vmem, *extra, token)
    count = len(operands)
    pairs = {len(smem) + place: out for place, out in aliases}
    far_shape = held if held is not None else far_out
    far = () if far_shape is None else (shape_of(*far_shape.shape, dtype=far_shape.dtype),)
    if extra:
        pairs[count - 2] = len(outs)
    pairs[count - 1] = len(outs) + len(far)
    return pl.pallas_call(
        kernel,
        out_shape=(*outs, *far, jax.ShapeDtypeStruct(token.shape, token.dtype)),
        in_specs=[SMEM] * len(smem) + [VMEM] * len(vmem) + [ANY] * (len(extra) + 1),
        out_specs=(*[VMEM] * len(outs), *[ANY] * (len(far) + 1)),
        scratch_shapes=scratch,
        input_output_aliases=pairs,
        compiler_params=pltpu.CompilerParams(vmem_limit_bytes=LIMIT),
        cost_estimate=pl.CostEstimate(flops=int(flops) if name in ("edges", "forward0", "turn") else 1, bytes_accessed=1000000 if name in ("edges", "forward0", "turn") else 1, transcendentals=0),
        name=name,
    )(*operands)


def no_cut(starts, window, positions, level, length):
    cut = positions == length
    for entry in range(starts.shape[1]):
        first = (starts[window, entry] + ((1 << level) - 1)) >> level
        cut = cut | (positions == first)
    return jnp.where(cut, 0.0, 1.0)


def lanes(index, width, first=0):
    if isinstance(index, int):
        return slice(first + index * width, first + (index + 1) * width)
    return pl.ds(pl.multiple_of(first + index * width, 128), width)


def loop(count, run, unroll=1):
    if unroll == count:
        for index in range(count):
            run(index)
        return

    def step(index, carry):
        run(index)
        return carry

    lax.fori_loop(0, count, step, 0, unroll=unroll)


def roll_rows(value, by):
    return pltpu.roll(value, by % value.shape[0], 0)


def fill_masks(mask_ref, starts, window, seq, level, halo, rows):
    own = OWN[level]
    length = own * 32
    row = lax.broadcasted_iota(jnp.int32, (rows, 128), 0)
    positions = row + (seq * own - halo)
    inside = jnp.where((positions >= 0) & (positions < length), 1.0, 0.0)
    free = no_cut(starts, window, positions, level, length)
    before = inside * free
    after = inside * roll_rows(free, -1)
    mask_ref[0, 0:rows] = before * roll_rows(free, 1)
    mask_ref[1, 0:rows] = before
    mask_ref[2, 0:rows] = inside
    mask_ref[3, 0:rows] = after
    mask_ref[4, 0:rows] = after * roll_rows(free, -2)


def stack_inputs(read, mask_ref, stacked_ref, rows, steps=1):
    part = C // 128 // steps

    def columns(first):
        for index in [first * part + place for place in range(part)]:
            tile = read(lanes(index, 128)).astype(F32)
            for tap in range(TAPS):
                moved = roll_rows(tile, 2 - tap) if tap != 2 else tile
                stacked_ref[0:rows, lanes(index, 128, tap * C)] = (
                    moved * mask_ref[tap, 0:rows]
                ).astype(BF16)

    columns(0) if steps == 1 else loop(steps, columns)


def stack_grads(value_ref, mask_ref, stacked_ref, rows, steps=1):
    part = C // 128 // steps

    def columns(first):
        for index in [first * part + place for place in range(part)]:
            tile = value_ref[0:rows, lanes(index, 128)].astype(F32)
            for tap in range(TAPS):
                moved = tile * mask_ref[tap, 0:rows]
                moved = roll_rows(moved, tap - 2) if tap != 2 else moved
                stacked_ref[0:rows, lanes(index, 128, tap * C)] = moved.astype(BF16)

    columns(0) if steps == 1 else loop(steps, columns)


def conv_columns(stacked_ref, weight_ref, index):
    return jnp.dot(
        stacked_ref[...], weight_ref[:, lanes(index, 256)], preferred_element_type=F32
    )


def back_columns(stacked_ref, weight_ref, index, turned):
    if turned:
        return conv_columns(stacked_ref, weight_ref, index)
    total = None
    for tap in range(TAPS):
        part = lax.dot_general(
            stacked_ref[:, tap * C : (tap + 1) * C],
            weight_ref[lanes(index, 256, tap * C), :],
            (((1,), (1,)), ((), ())),
            preferred_element_type=F32,
        )
        total = part if total is None else total + part
    return total


def turn_kernel(info, weight, _, turned_out, _out, unit_v):
    @pl.when(info[0] > 0)
    def _():
        row = lax.broadcasted_iota(jnp.int32, (C, 128), 0)
        lane = lax.broadcasted_iota(jnp.int32, (C, 128), 1)
        for index in range(C // 128):
            unit_v[:, index * 128 : (index + 1) * 128] = jnp.where(
                row == lane + index * 128, 1.0, 0.0
            ).astype(BF16)

        def block(place):
            tap, index = place // 3, place % 3
            turned_out[lanes(tap, C), lanes(index, 256)] = lax.dot_general(
                unit_v[...],
                weight[lanes(place, 256), :],
                (((1,), (1,)), ((), ())),
                preferred_element_type=F32,
            ).astype(BF16)

        loop(TAPS * 3, block)


def turn_call(info, token, weight):
    return call(
        turn_kernel, "turn", 2 * C * C * C * TAPS, (info,), (weight,), (shape_of(TAPS * C, C),),
        token, [pltpu.VMEM((C, C), BF16)],
    )


def gelu_and_slope(u):
    scale = 0.7978845608028654
    square = u * u
    bend = jnp.tanh(scale * (u + 0.044715 * square * u))
    half = 0.5 * (1.0 + bend)
    slope = half + 0.5 * u * (1.0 - bend * bend) * (scale * (1.0 + 0.134145 * square))
    return u * half, slope


def edges_kernel(windows, info, dna, cot, _, near, first, rest, _out):
    own, part = OWN[0], cot.shape[1]
    odd = info[1] % 2 == 1

    def fill(leading_to_near):
        near_x, far_x = (0, own - 64) if leading_to_near else (own - 64, 0)
        near_c, far_c = (0, part - 16) if leading_to_near else (part - 16, 0)
        for window in range(windows):
            rows = slice(window * 64, window * 64 + 64)

            @pl.when(info[0] == 0)
            def _():
                near[rows, :] = dna[window, near_x : near_x + 64, :]
                if window == 0:
                    first[...] = dna[0, far_x : far_x + 64, :]
                else:
                    rest[(window - 1) * 64 : window * 64, :] = dna[window, far_x : far_x + 64, :]

            lines = slice(window * 16, window * 16 + 16)

            @pl.when(info[0] == 3)
            def _():
                near[lines, :] = cot[window, near_c : near_c + 16, :]
                rest[lines, :] = cot[window, far_c : far_c + 16, :]

    pl.when(odd)(functools.partial(fill, True))
    pl.when(jnp.logical_not(odd))(functools.partial(fill, False))


def edges_call(info, token, dna, cot):
    windows = dna.shape[0]
    return call(
        functools.partial(edges_kernel, windows),
        "edges",
        2e10,
        (info,),
        (dna, cot),
        (shape_of(windows * 64, C), shape_of(64, C), shape_of((windows - 1) * 64, C)),
        token,
        [],
    )


def sides(odd, near, far):
    near, far = near.astype(F32), far.astype(F32)
    return jnp.where(odd, near, far), jnp.where(odd, far, near)


def with_edges(own, near, far, odd, low, high):
    ahead, behind = sides(odd, near, far)
    return jnp.concatenate([ahead[low:], own.astype(F32), behind[:high]], axis=0)


def forward_kernel(level, window, info, starts, *refs):
    rows, back = ROWS[level], BACK_ROWS[level]
    skip = HALO[level] - BACK_HALO[level]
    inputs = 3 if level == 0 else 1
    xs = refs[:inputs]
    weight, _, pooled_out, slope_out, stacked_v, _, mask_v, act_v = refs[inputs:]

    def read(cols):
        if level == 0:
            x_in, near, far = xs
            first = max(window - 1, 0) * 64
            return with_edges(
                x_in[window, :, cols],
                near[window * 64 : window * 64 + 64, cols],
                far[first : first + 64, cols],
                info[1] % 2 == 1,
                0,
                64,
            )
        return xs[0][:, cols]

    @pl.when(info[0] == level)
    def _():
        fill_masks(mask_v, starts, window, info[1], level, HALO[level], rows)
        stack_inputs(read, mask_v, stacked_v, rows)

        def block(index):
            act, slope = gelu_and_slope(conv_columns(stacked_v, weight, index))
            slope_out[:, lanes(index, 256)] = slope[skip : skip + back]
            for half in range(2):
                place = index * 2 + half
                act_v[place] = act[:, half * 128 : (half + 1) * 128]
                even = act_v[place, pl.ds(0, rows // 2, stride=2), :]
                odd = act_v[place, pl.ds(1, rows // 2, stride=2), :]
                pooled_out[:, lanes(place, 128)] = (0.5 * (even + odd)).astype(BF16)

        loop(C // 256, block, BLOCKS_UNROLL)


def forward_call(level, window, info, starts, weight, token, *xs):
    rows, back = ROWS[level], BACK_ROWS[level]
    return call(
        functools.partial(forward_kernel, level, window),
        f"forward{level}",
        2 * rows * C * C * TAPS,
        (info, starts),
        (*xs, weight),
        (shape_of(rows // 2, C), shape_of(back, C, dtype=F32), shape_of(rows, TAPS * C)),
        token,
        [
            pltpu.VMEM((TAPS, rows, 128), F32),
            pltpu.VMEM((C // 128, rows, 128), F32),
        ],
    )


def finish_backward(level, du_v, mask_v, stacked_v, weight, send_out, grad_out):
    rows, own, halo = BACK_ROWS[level], OWN[level], BACK_HALO[level]
    send = SEND_ROWS[level]
    trim = (rows - send) // 2
    stack_grads(du_v, mask_v, stacked_v, rows, 1 if level else 3)

    def block(index):
        found = back_columns(stacked_v, weight, index, level > 0)
        cols = lanes(index, 256)
        if send:
            send_out[:, cols] = found[trim : trim + send].astype(BF16)
        grad_out[0:own, cols] = found[halo : halo + own].astype(BF16)

    loop(C // 256, block, BLOCKS_UNROLL)
    if own < 256:
        grad_out[own:, :] = jnp.zeros((256 - own, C), BF16)


def own_grads(level, du_v, du_out):
    own, halo = OWN[level], BACK_HALO[level]
    du_out[0:own, :] = du_v[halo : halo + own, :].astype(BF16)
    if own < 256:
        du_out[own:, :] = jnp.zeros((256 - own, C), BF16)


def last_kernel(window, info, starts, x_in, cot, near, far, weight, turned, *refs):
    send_out, grad_out, du_out, inputs_v, _, mask_v, stacked_v, du_v = refs[-8:]
    level, rows = 3, ROWS[3]
    if len(refs) == 10:

        @pl.when(info[0] == 2)
        def _():
            send_out[...] = refs[0][...]

    @pl.when(info[0] == level)
    def _():
        fill_masks(mask_v, starts, window, info[1], level, HALO[level], rows)
        stack_inputs(
            lambda cols: x_in[:, cols], mask_v, inputs_v, rows
        )

        def block(index):
            _, slope = gelu_and_slope(conv_columns(inputs_v, weight, index))
            cols = lanes(index, 256)
            lines = slice(window * 16, window * 16 + 16)
            g = with_edges(
                cot[window, :, cols], near[lines, cols], far[lines, cols], info[1] % 2 == 1, 8, 8
            )
            du_v[:, cols] = (g * slope).astype(BF16).astype(F32)

        loop(C // 256, block, BLOCKS_UNROLL)
        finish_backward(level, du_v, mask_v, stacked_v, turned, send_out, grad_out)
        own_grads(level, du_v, du_out)


def last_call(window, info, starts, weight, turned, token, x, cot, near, far, *held):
    rows = ROWS[3]
    return call(
        functools.partial(last_kernel, window),
        "last",
        4 * rows * C * C * TAPS,
        (info, starts),
        (x, cot, near, far, weight, turned, *held),
        (shape_of(rows, C), shape_of(256, C), shape_of(256, C), shape_of(rows, TAPS * C)),
        token,
        [
            pltpu.VMEM((TAPS, rows, 128), F32),
            pltpu.VMEM((rows, TAPS * C), BF16),
            pltpu.VMEM((rows, C), F32),
        ],
        aliases=((6, 0),) if held else (),
    )


def spread_grads(arrived, wide_v, slope, du_v, rows):
    def column(index):
        cols = lanes(index, 128)
        half = 0.5 * arrived[:, cols].astype(F32)
        wide_v[index, pl.ds(0, rows // 2, stride=2), :] = half
        wide_v[index, pl.ds(1, rows // 2, stride=2), :] = half
        du_v[:, cols] = (wide_v[index] * slope[:, cols]).astype(BF16).astype(F32)

    loop(C // 128, column, C // 128)


def keep_later(level, info, pairs):
    @pl.when(info[0] > level)
    def _():
        for source, target in pairs:
            target[...] = source[...]


def backward_kernel(level, window, info, starts, arrived, slope, weight, grad, du, _token,
                    send_out, grad_out, du_out, _out, wide_v, mask_v, stacked_v, du_v):
    rows = BACK_ROWS[level]
    keep_later(level, info, ((grad, grad_out), (du, du_out)))

    @pl.when(info[0] == level)
    def _():
        fill_masks(mask_v, starts, window, info[1], level, BACK_HALO[level], rows)
        spread_grads(arrived, wide_v, slope, du_v, rows)
        finish_backward(level, du_v, mask_v, stacked_v, weight, send_out, grad_out)
        own_grads(level, du_v, du_out)


def backward_call(level, window, info, starts, weight, token, arrived, slope, grad, du):
    rows = BACK_ROWS[level]
    return call(
        functools.partial(backward_kernel, level, window),
        f"backward{level}",
        2 * rows * C * C * TAPS,
        (info, starts),
        (arrived, slope, weight, grad, du),
        (shape_of(SEND_ROWS[level], C), shape_of(256, C), shape_of(256, C)),
        token,
        [
            pltpu.VMEM((C // 128, rows, 128), F32),
            pltpu.VMEM((TAPS, rows, 128), F32),
            pltpu.VMEM((rows, TAPS * C), BF16),
            pltpu.VMEM((rows, C), F32),
        ],
        aliases=((3, 1), (4, 2)),
    )


def first_du_kernel(info, arrived, slope, du, _token, all_out, du_out, _out, wide_v, du_v):
    rows = BACK_ROWS[0]
    keep_later(0, info, ((du, du_out),))

    @pl.when(info[0] == 0)
    def _():
        spread_grads(arrived, wide_v, slope, du_v, rows)
        own_grads(0, du_v, du_out)
        all_out[...] = du_v[...].astype(BF16)


def first_du_call(info, token, arrived, slope, du):
    rows = BACK_ROWS[0]
    return call(
        first_du_kernel,
        "first_du",
        rows * C * 8,
        (info,),
        (arrived, slope, du),
        (shape_of(rows, C), shape_of(256, C)),
        token,
        [pltpu.VMEM((C // 128, rows, 128), F32), pltpu.VMEM((rows, C), F32)],
        aliases=((2, 1),),
    )


def first_grad_kernel(window, info, starts, du, weight, grad, _token, grad_out, _out, mask_v,
                      stacked_v):
    rows = BACK_ROWS[0]
    keep_later(0, info, ((grad, grad_out),))

    @pl.when(info[0] == 0)
    def _():
        fill_masks(mask_v, starts, window, info[1], 0, BACK_HALO[0], rows)
        finish_backward(0, du, mask_v, stacked_v, weight, None, grad_out)


def first_grad_call(window, info, starts, weight, token, du, grad):
    rows = BACK_ROWS[0]
    return call(
        functools.partial(first_grad_kernel, window),
        "first_grad",
        2 * rows * C * C * TAPS,
        (info, starts),
        (du, weight, grad),
        (shape_of(256, C),),
        token,
        [pltpu.VMEM((TAPS, rows, 128), F32), pltpu.VMEM((rows, TAPS * C), BF16)],
        aliases=((2, 0),),
    )


def gather_kernel(windows, *refs):
    out = refs[-2]
    for window in range(windows):
        out[0, window] = refs[window][...]


def gather_call(token, grads):
    return call(
        functools.partial(gather_kernel, len(grads)), "gather", 1000000, (), tuple(grads),
        (shape_of(1, len(grads), 256, C),), token, [],
    )


def fill_order(seq, order_ref):
    row = lax.broadcasted_iota(jnp.int32, (C, 128), 0)
    place = (row * 2731) >> 16
    swap = (seq ^ (place >> 4)) & 1
    one, two = place & 3, (place >> 2) & 3
    along_z, along_y = jnp.where(swap == 1, two, one), jnp.where(swap == 1, one, two)
    apart = (along_y << 3) | (along_z << 1) | (place >> 4)
    source = CHUNK * (seq ^ apart) + (row - CHUNK * place)
    lane = lax.broadcasted_iota(jnp.int32, (C, 128), 1)
    for index in range(C // 128):
        order_ref[:, index * 128 : (index + 1) * 128] = jnp.where(
            source == lane + index * 128, 1.0, 0.0
        ).astype(BF16)


def side_kernel(level, windows, info, *refs):
    halo, own = HALO[level], OWN[level]
    count = len(windows)
    xs = refs[:count]
    side_out, _, order_v, side_v, sems = refs[-5:]
    total = count * own
    padding = -total % 128

    def leave(place):
        return pltpu.make_async_copy(
            side_v.at[place], side_out.at[:, lanes(windows[place], 256)], sems.at[place]
        )

    @pl.when(info[0] == level)
    def _():
        fill_order(info[1], order_v)

        def one_tap(tap):
            parts = [x[halo : halo + own, lanes(tap, C)] for x in xs]
            if padding:
                parts.append(jnp.zeros((padding, C), BF16))
            found = lax.dot_general(
                order_v[...],
                jnp.concatenate(parts, axis=0),
                (((1,), (1,)), ((), ())),
                preferred_element_type=F32,
            )
            for place in range(count):
                part = found[:, place * own : (place + 1) * own]
                if own < 256:
                    part = jnp.concatenate([part, jnp.zeros((C, 256 - own), F32)], axis=1)
                side_v[place, lanes(tap, C), :] = part.astype(BF16)

        loop(TAPS, one_tap)
        for place in range(count):
            leave(place).start()
        for place in range(count):
            leave(place).wait()


def side_call(level, windows, info, token, side, *xs):
    return call(
        functools.partial(side_kernel, level, windows),
        f"side{level}",
        2 * len(windows) * 256 * C * C * TAPS,
        (info,),
        xs,
        (),
        token,
        [
            pltpu.VMEM((C, C), BF16),
            pltpu.VMEM((len(windows), TAPS * C, 256), BF16),
            pltpu.SemaphoreType.DMA((len(windows),)),
        ],
        held=side,
        far_out=shape_of(TAPS * C, 3 * 256),
    )


def weight_kernel(half, side, *refs):
    dus = refs[:-5]
    _, send_out, keep_out, _, du_v = refs[-5:]
    first = sum(PIECES[:half])
    for window, du in enumerate(dus):
        du_v[window * 256 : (window + 1) * 256, :] = du[...]

    def one_piece(piece):
        place = first + piece
        tap, part = place // 3, place % 3
        found = jnp.dot(
            side[lanes(tap, C), :], du_v[:, lanes(part, 256)], preferred_element_type=F32
        ).reshape(2, 16, CHUNK, 256)
        cols = lanes(piece, 256)
        keep_out[:, :, cols] = found[0].astype(BF16)
        send_out[:, :, cols] = found[1].astype(BF16)

    def two_pieces(pair):
        one_piece(2 * pair)
        one_piece(2 * pair + 1)

    loop(PIECES[half] // 2, two_pieces)
    if PIECES[half] % 2:
        one_piece(PIECES[half] - 1)


def weight_call(quarter, token, side, dus):
    width = PIECES[quarter] * 256
    shape = shape_of(16, CHUNK, width)
    return call(
        functools.partial(weight_kernel, quarter),
        f"weight{quarter}",
        2 * C * 768 * width,
        (),
        (side, *dus),
        (shape, shape),
        token,
        [pltpu.VMEM((len(dus) * 256, C), BF16)],
    )


def half_plan(*orders):
    held = [(second, first) for second in range(4) for first in range(4)]
    plan = []
    for axis, (one, two) in zip((1, 0), orders):
        for apart, gone in ((one, (one, 2)), (two, (two,))):
            leaving = [place for place in held if place[axis] in gone]
            leaving.sort(key=lambda place: (place[1 - axis], gone.index(place[axis])))
            staying = []
            for place in leaving:
                moved = list(place)
                moved[axis] ^= apart
                staying.append(tuple(moved))
            plan.append(
                (
                    axis,
                    apart,
                    [held.index(place) for place in leaving],
                    [held.index(place) for place in staying],
                )
            )
            held = staying
    return plan


PLANS = (half_plan((1, 3), (1, 3)), half_plan((3, 1), (3, 1)))


def added(keep, arrived, source):
    return keep[source].astype(F32) + arrived[source].astype(F32)


def add_kernel(half, step, keep, arrived, _, stay_out, leave_out, _out):
    _, _, leaving, staying = PLANS[half][step]
    for target, sources in ((stay_out, staying), (leave_out, leaving)):
        for row, source in enumerate(sources):
            target[row] = added(keep, arrived, source).astype(BF16)


def add_call(half, step, token, keep, arrived):
    shape = shape_of(len(PLANS[half][step][2]), CHUNK, keep.shape[-1])
    return call(
        functools.partial(add_kernel, half, step),
        f"add{half}_{step}",
        4000000 // (1 << step),
        (),
        (keep, arrived),
        (shape, shape),
        token,
        [],
    )


def final_kernel(half, keep, arrived, *refs):
    out = refs[-2]
    total = added(keep, arrived, 0)
    piece = sum(PIECES[:half])
    for place in range(piece + PIECES[half]):
        tap, part = divmod(place, 3)
        cols = slice(part * 256, (part + 1) * 256)
        if place < piece:
            out[tap, :, cols] = refs[0][tap, :, cols]
        else:
            out[tap, :, cols] = total[:, (place - piece) * 256 : (place - piece + 1) * 256]


def final_call(half, token, keep, arrived, *held):
    return call(
        functools.partial(final_kernel, half),
        f"final{half}",
        1000000,
        (),
        (keep, arrived, *held),
        (shape_of(TAPS, CHUNK, C, dtype=F32),),
        token,
        [],
        aliases=((2, 0),) if held else (),
    )


def section_pairs(source, target, shards):
    return [(source * shards + place, target * shards + place) for place in range(shards)]


def apart_pairs(sections, shards, apart):
    return [
        (section * shards + place, section * shards + (place ^ apart))
        for section in range(sections)
        for place in range(shards)
    ]


def mixed_pairs(sections, shards, axis, apart):
    units = (8, 2) if axis == 0 else (2, 8)
    return [
        (section * shards + place, section * shards + (place ^ (apart * units[place % 2])))
        for section in range(sections)
        for place in range(shards)
    ]


def body(dna_embed, conv_weight, interval_starts, cotangent):
    windows = dna_embed.shape[0]
    sections = lax.axis_size("section")
    shards = lax.axis_size("seq")
    section_index = lax.axis_index("section")
    seq_index = lax.axis_index("seq")
    info = jnp.stack([section_index, seq_index]).astype(jnp.int32)
    weight = jnp.transpose(conv_weight[0], (1, 0, 2)).reshape(TAPS * C, C)
    starts = interval_starts
    token = jnp.zeros((8, 128), F32)

    ends = (0, sections - 1)
    near_pairs = [
        pair for pair in apart_pairs(sections, shards, 1) if pair[0] // shards in ends
    ]
    far_pairs = [
        (section * shards + place, section * shards + place + by)
        for section in ends
        for place in range(shards)
        for by in (1 if place % 2 else -1,)
        if 0 <= place + by < shards
    ]
    near, far, rest, token = edges_call(info, token, dna_embed, cotangent)
    near = lax.ppermute(near, AXES, near_pairs)
    far = lax.ppermute(far, AXES, [pair for pair in far_pairs if pair[0] < shards])
    rest = lax.ppermute(rest, AXES, far_pairs)

    def relay(value, source, target):
        return lax.ppermute(value, AXES, section_pairs(source, target, shards))

    inputs = [[None] * windows for _ in range(4)]
    slopes = [[None] * windows for _ in range(4)]
    stacks = [[None] * windows for _ in range(4)]
    grads = [None] * windows
    dus = [None] * windows
    wide_du = [None] * windows
    arrived = [None] * windows
    side = None

    def forward(level, window, send=True):
        nonlocal token
        xs = (inputs[level][window],)
        if level == 0:
            xs = (dna_embed, near, rest if window else far)
        pooled, slopes[level][window], stacks[level][window], token = forward_call(
            level, window, info, starts, weight, token, *xs
        )
        if send:
            inputs[level + 1][window] = relay(pooled, level, level + 1)
        return pooled

    def turn(window, *held):
        nonlocal token
        send, grads[window], dus[window], stacks[3][window], token = last_call(
            window, info, starts, weight, turned, token, inputs[3][window], cotangent, near, rest,
            *held,
        )
        if held:
            pairs = section_pairs(2, 3, shards) + section_pairs(3, 2, shards)
            arrived[window] = lax.ppermute(send, AXES, pairs)
        else:
            arrived[window] = relay(send, 3, 2)
        return arrived[window]

    def backward(level, window):
        nonlocal token
        send, grads[window], dus[window], token = backward_call(
            level, window, info, starts, turned, token, arrived[window], slopes[level][window],
            grads[window], dus[window],
        )
        arrived[window] = relay(send, level, level - 1)

    def arrive(window):
        nonlocal token
        wide_du[window], dus[window], token = first_du_call(
            info, token, arrived[window], slopes[0][window], dus[window]
        )

    def first_grad(window):
        nonlocal token
        grads[window], token = first_grad_call(
            window, info, starts, weight, token, wide_du[window], grads[window]
        )

    def sideways(level, *chosen):
        nonlocal side, token
        chosen = chosen or tuple(range(windows))
        xs = [stacks[level][window] for window in chosen]
        side, token = side_call(level, chosen, info, token, side, *xs)

    forward(0, 0)
    turned, token = turn_call(info, token, weight)
    forward(0, 1)
    forward(0, 2)
    sideways(0)
    forward(1, 0)
    sideways(1, 0)
    forward(1, 1)
    forward(1, 2)
    sideways(1, 1, 2)
    forward(2, 0)
    inputs[3][1] = turn(0, forward(2, 1, send=False))
    forward(2, 2)
    backward(2, 0)
    turn(1)
    turn(2)
    backward(2, 1)
    backward(2, 2)
    sideways(3)
    sideways(2)
    backward(1, 0)
    backward(1, 1)
    backward(1, 2)
    arrive(0)
    first_grad(0)
    arrive(1)
    arrive(2)

    keeps, arriveds = [None, None], [None, None]

    def weigh(half):
        nonlocal token
        send, keeps[half], token = weight_call(half, token, side, dus)
        arriveds[half] = lax.ppermute(send, AXES, apart_pairs(sections, shards, 1))

    def pass_on(half, step):
        nonlocal token
        keeps[half], leaving, token = add_call(half, step, token, keeps[half], arriveds[half])
        axis, apart = PLANS[half][step][:2]
        arriveds[half] = lax.ppermute(leaving, AXES, mixed_pairs(sections, shards, axis, apart))

    weigh(0)
    weigh(1)
    pass_on(0, 0)
    pass_on(1, 0)
    first_grad(1)
    pass_on(0, 1)
    pass_on(1, 1)
    first_grad(2)
    pass_on(0, 2)
    pass_on(1, 2)
    input_grads, token = gather_call(token, grads)
    pass_on(0, 3)
    pass_on(1, 3)
    weight_grad, token = final_call(0, token, keeps[0], arriveds[0])
    weight_grad, token = final_call(1, token, keeps[1], arriveds[1], weight_grad)
    weight_grad = jnp.transpose(weight_grad, (1, 0, 2))[None]
    return (weight_grad, input_grads)


def solution(mesh):
    placed = (P(None, "seq", None), P("section", None, None, None), P(), P(None, "seq", None))
    return jax.shard_map(
        body,
        mesh=mesh,
        in_specs=placed,
        out_specs=(P("section", "seq", None, None), P("section", None, "seq", None)),
        check_vma=False,
    )
```

```python
import functools

import jax
import jax.numpy as jnp
from jax import lax
from jax.experimental import pallas as pl
from jax.experimental.pallas import tpu as pltpu
from jax.sharding import PartitionSpec as P

C = 768
TAPS = 5
AXES = ("section", "seq")
OWN = (256, 128, 64, 32)
HALO = (64, 32, 16, 8)
ROWS = (384, 192, 96, 48)
BACK_HALO = (16, 16, 16, 8)
BACK_ROWS = (288, 160, 96, 48)
SEND_ROWS = (0, 144, 80, 48)
CHUNK = 24
LIMIT = 16 * 1024 * 1024
F32 = jnp.float32
BF16 = jnp.bfloat16
ANY = pl.BlockSpec(memory_space=pl.ANY)
SMEM = pl.BlockSpec(memory_space=pltpu.SMEM)
VMEM = pl.BlockSpec(memory_space=pltpu.VMEM)
PIECES = (8, 7)
BLOCKS_UNROLL = 3


def shape_of(*dims, dtype=BF16):
    return jax.ShapeDtypeStruct(dims, dtype)


def call(kernel, name, flops, smem, vmem, outs, token, scratch, aliases=(), held=None, far_out=None):
    extra = () if held is None else (held,)
    operands = (*smem, *vmem, *extra, token)
    count = len(operands)
    pairs = {len(smem) + place: out for place, out in aliases}
    far_shape = held if held is not None else far_out
    far = () if far_shape is None else (shape_of(*far_shape.shape, dtype=far_shape.dtype),)
    if extra:
        pairs[count - 2] = len(outs)
    pairs[count - 1] = len(outs) + len(far)
    return pl.pallas_call(
        kernel,
        out_shape=(*outs, *far, jax.ShapeDtypeStruct(token.shape, token.dtype)),
        in_specs=[SMEM] * len(smem) + [VMEM] * len(vmem) + [ANY] * (len(extra) + 1),
        out_specs=(*[VMEM] * len(outs), *[ANY] * (len(far) + 1)),
        scratch_shapes=scratch,
        input_output_aliases=pairs,
        compiler_params=pltpu.CompilerParams(vmem_limit_bytes=LIMIT),
        cost_estimate=pl.CostEstimate(flops=int(flops) if name in ("edges", "forward0", "turn") else 1, bytes_accessed=1000000 if name in ("edges", "forward0", "turn") else 1, transcendentals=0),
        name=name,
    )(*operands)


def no_cut(starts, window, positions, level, length):
    cut = positions == length
    for entry in range(starts.shape[1]):
        first = (starts[window, entry] + ((1 << level) - 1)) >> level
        cut = cut | (positions == first)
    return jnp.where(cut, 0.0, 1.0)


def lanes(index, width, first=0):
    if isinstance(index, int):
        return slice(first + index * width, first + (index + 1) * width)
    return pl.ds(pl.multiple_of(first + index * width, 128), width)


def loop(count, run, unroll=1):
    if unroll == count:
        for index in range(count):
            run(index)
        return

    def step(index, carry):
        run(index)
        return carry

    lax.fori_loop(0, count, step, 0, unroll=unroll)


def roll_rows(value, by):
    return pltpu.roll(value, by % value.shape[0], 0)


def fill_masks(mask_ref, starts, window, seq, level, halo, rows):
    own = OWN[level]
    length = own * 32
    row = lax.broadcasted_iota(jnp.int32, (rows, 128), 0)
    positions = row + (seq * own - halo)
    inside = jnp.where((positions >= 0) & (positions < length), 1.0, 0.0)
    free = no_cut(starts, window, positions, level, length)
    before = inside * free
    after = inside * roll_rows(free, -1)
    mask_ref[0, 0:rows] = before * roll_rows(free, 1)
    mask_ref[1, 0:rows] = before
    mask_ref[2, 0:rows] = inside
    mask_ref[3, 0:rows] = after
    mask_ref[4, 0:rows] = after * roll_rows(free, -2)


def stack_inputs(read, mask_ref, stacked_ref, rows, steps=1):
    part = C // 128 // steps

    def columns(first):
        for index in [first * part + place for place in range(part)]:
            tile = read(lanes(index, 128)).astype(F32)
            for tap in range(TAPS):
                moved = roll_rows(tile, 2 - tap) if tap != 2 else tile
                stacked_ref[0:rows, lanes(index, 128, tap * C)] = (
                    moved * mask_ref[tap, 0:rows]
                ).astype(BF16)

    columns(0) if steps == 1 else loop(steps, columns)


def stack_grads(value_ref, mask_ref, stacked_ref, rows, steps=1):
    part = C // 128 // steps

    def columns(first):
        for index in [first * part + place for place in range(part)]:
            tile = value_ref[0:rows, lanes(index, 128)].astype(F32)
            for tap in range(TAPS):
                moved = tile * mask_ref[tap, 0:rows]
                moved = roll_rows(moved, tap - 2) if tap != 2 else moved
                stacked_ref[0:rows, lanes(index, 128, tap * C)] = moved.astype(BF16)

    columns(0) if steps == 1 else loop(steps, columns)


def conv_columns(stacked_ref, weight_ref, index):
    return jnp.dot(
        stacked_ref[...], weight_ref[:, lanes(index, 256)], preferred_element_type=F32
    )


def back_columns(stacked_ref, weight_ref, index, turned):
    if turned:
        return conv_columns(stacked_ref, weight_ref, index)
    total = None
    for tap in range(TAPS):
        part = lax.dot_general(
            stacked_ref[:, tap * C : (tap + 1) * C],
            weight_ref[lanes(index, 256, tap * C), :],
            (((1,), (1,)), ((), ())),
            preferred_element_type=F32,
        )
        total = part if total is None else total + part
    return total


def turn_kernel(info, weight, _, turned_out, _out, unit_v):
    @pl.when(info[0] > 0)
    def _():
        row = lax.broadcasted_iota(jnp.int32, (C, 128), 0)
        lane = lax.broadcasted_iota(jnp.int32, (C, 128), 1)
        for index in range(C // 128):
            unit_v[:, index * 128 : (index + 1) * 128] = jnp.where(
                row == lane + index * 128, 1.0, 0.0
            ).astype(BF16)

        def block(place):
            tap, index = place // 3, place % 3
            turned_out[lanes(tap, C), lanes(index, 256)] = lax.dot_general(
                unit_v[...],
                weight[lanes(place, 256), :],
                (((1,), (1,)), ((), ())),
                preferred_element_type=F32,
            ).astype(BF16)

        loop(TAPS * 3, block)


def turn_call(info, token, weight):
    return call(
        turn_kernel, "turn", 2 * C * C * C * TAPS, (info,), (weight,), (shape_of(TAPS * C, C),),
        token, [pltpu.VMEM((C, C), BF16)],
    )


def gelu_and_slope(u):
    scale = 0.7978845608028654
    square = u * u
    bend = jnp.tanh(scale * (u + 0.044715 * square * u))
    half = 0.5 * (1.0 + bend)
    slope = half + 0.5 * u * (1.0 - bend * bend) * (scale * (1.0 + 0.134145 * square))
    return u * half, slope


def edges_kernel(windows, info, dna, cot, _, near, first, rest, _out):
    own, part = OWN[0], cot.shape[1]
    odd = info[1] % 2 == 1

    def fill(leading_to_near):
        near_x, far_x = (0, own - 64) if leading_to_near else (own - 64, 0)
        near_c, far_c = (0, part - 16) if leading_to_near else (part - 16, 0)
        for window in range(windows):
            rows = slice(window * 64, window * 64 + 64)

            @pl.when(info[0] == 0)
            def _():
                near[rows, :] = dna[window, near_x : near_x + 64, :]
                if window == 0:
                    first[...] = dna[0, far_x : far_x + 64, :]
                else:
                    rest[(window - 1) * 64 : window * 64, :] = dna[window, far_x : far_x + 64, :]

            lines = slice(window * 16, window * 16 + 16)

            @pl.when(info[0] == 3)
            def _():
                near[lines, :] = cot[window, near_c : near_c + 16, :]
                rest[lines, :] = cot[window, far_c : far_c + 16, :]

    pl.when(odd)(functools.partial(fill, True))
    pl.when(jnp.logical_not(odd))(functools.partial(fill, False))


def edges_call(info, token, dna, cot):
    windows = dna.shape[0]
    return call(
        functools.partial(edges_kernel, windows),
        "edges",
        2e10,
        (info,),
        (dna, cot),
        (shape_of(windows * 64, C), shape_of(64, C), shape_of((windows - 1) * 64, C)),
        token,
        [],
    )


def sides(odd, near, far):
    near, far = near.astype(F32), far.astype(F32)
    return jnp.where(odd, near, far), jnp.where(odd, far, near)


def with_edges(own, near, far, odd, low, high):
    ahead, behind = sides(odd, near, far)
    return jnp.concatenate([ahead[low:], own.astype(F32), behind[:high]], axis=0)


def forward_kernel(level, window, info, starts, *refs):
    rows, back = ROWS[level], BACK_ROWS[level]
    skip = HALO[level] - BACK_HALO[level]
    inputs = 3 if level == 0 else 1
    xs = refs[:inputs]
    weight, _, pooled_out, slope_out, stacked_v, _, mask_v, act_v = refs[inputs:]

    def read(cols):
        if level == 0:
            x_in, near, far = xs
            first = max(window - 1, 0) * 64
            return with_edges(
                x_in[window, :, cols],
                near[window * 64 : window * 64 + 64, cols],
                far[first : first + 64, cols],
                info[1] % 2 == 1,
                0,
                64,
            )
        return xs[0][:, cols]

    @pl.when(info[0] == level)
    def _():
        fill_masks(mask_v, starts, window, info[1], level, HALO[level], rows)
        stack_inputs(read, mask_v, stacked_v, rows)

        def block(index):
            act, slope = gelu_and_slope(conv_columns(stacked_v, weight, index))
            slope_out[:, lanes(index, 256)] = slope[skip : skip + back]
            for half in range(2):
                place = index * 2 + half
                act_v[place] = act[:, half * 128 : (half + 1) * 128]
                even = act_v[place, pl.ds(0, rows // 2, stride=2), :]
                odd = act_v[place, pl.ds(1, rows // 2, stride=2), :]
                pooled_out[:, lanes(place, 128)] = (0.5 * (even + odd)).astype(BF16)

        loop(C // 256, block, BLOCKS_UNROLL)


def forward_call(level, window, info, starts, weight, token, *xs):
    rows, back = ROWS[level], BACK_ROWS[level]
    return call(
        functools.partial(forward_kernel, level, window),
        f"forward{level}",
        2 * rows * C * C * TAPS,
        (info, starts),
        (*xs, weight),
        (shape_of(rows // 2, C), shape_of(back, C, dtype=F32), shape_of(rows, TAPS * C)),
        token,
        [
            pltpu.VMEM((TAPS, rows, 128), F32),
            pltpu.VMEM((C // 128, rows, 128), F32),
        ],
    )


def finish_backward(level, du_v, mask_v, stacked_v, weight, send_out, grad_out):
    rows, own, halo = BACK_ROWS[level], OWN[level], BACK_HALO[level]
    send = SEND_ROWS[level]
    trim = (rows - send) // 2
    stack_grads(du_v, mask_v, stacked_v, rows, 1 if level else 3)

    def block(index):
        found = back_columns(stacked_v, weight, index, level > 0)
        cols = lanes(index, 256)
        if send:
            send_out[:, cols] = found[trim : trim + send].astype(BF16)
        grad_out[0:own, cols] = found[halo : halo + own].astype(BF16)

    loop(C // 256, block, BLOCKS_UNROLL)
    if own < 256:
        grad_out[own:, :] = jnp.zeros((256 - own, C), BF16)


def own_grads(level, du_v, du_out):
    own, halo = OWN[level], BACK_HALO[level]
    du_out[0:own, :] = du_v[halo : halo + own, :].astype(BF16)
    if own < 256:
        du_out[own:, :] = jnp.zeros((256 - own, C), BF16)


def last_kernel(window, info, starts, x_in, cot, near, far, weight, turned, *refs):
    send_out, grad_out, du_out, inputs_v, _, mask_v, stacked_v, du_v = refs[-8:]
    level, rows = 3, ROWS[3]
    if len(refs) == 10:

        @pl.when(info[0] == 2)
        def _():
            send_out[...] = refs[0][...]

    @pl.when(info[0] == level)
    def _():
        fill_masks(mask_v, starts, window, info[1], level, HALO[level], rows)
        stack_inputs(
            lambda cols: x_in[:, cols], mask_v, inputs_v, rows
        )

        def block(index):
            _, slope = gelu_and_slope(conv_columns(inputs_v, weight, index))
            cols = lanes(index, 256)
            lines = slice(window * 16, window * 16 + 16)
            g = with_edges(
                cot[window, :, cols], near[lines, cols], far[lines, cols], info[1] % 2 == 1, 8, 8
            )
            du_v[:, cols] = (g * slope).astype(BF16).astype(F32)

        loop(C // 256, block, BLOCKS_UNROLL)
        finish_backward(level, du_v, mask_v, stacked_v, turned, send_out, grad_out)
        own_grads(level, du_v, du_out)


def last_call(window, info, starts, weight, turned, token, x, cot, near, far, *held):
    rows = ROWS[3]
    return call(
        functools.partial(last_kernel, window),
        "last",
        4 * rows * C * C * TAPS,
        (info, starts),
        (x, cot, near, far, weight, turned, *held),
        (shape_of(rows, C), shape_of(256, C), shape_of(256, C), shape_of(rows, TAPS * C)),
        token,
        [
            pltpu.VMEM((TAPS, rows, 128), F32),
            pltpu.VMEM((rows, TAPS * C), BF16),
            pltpu.VMEM((rows, C), F32),
        ],
        aliases=((6, 0),) if held else (),
    )


def spread_grads(arrived, wide_v, slope, du_v, rows):
    def column(index):
        cols = lanes(index, 128)
        half = 0.5 * arrived[:, cols].astype(F32)
        wide_v[index, pl.ds(0, rows // 2, stride=2), :] = half
        wide_v[index, pl.ds(1, rows // 2, stride=2), :] = half
        du_v[:, cols] = (wide_v[index] * slope[:, cols]).astype(BF16).astype(F32)

    loop(C // 128, column, C // 128)


def keep_later(level, info, pairs):
    @pl.when(info[0] > level)
    def _():
        for source, target in pairs:
            target[...] = source[...]


def backward_kernel(level, window, info, starts, arrived, slope, weight, grad, du, _token,
                    send_out, grad_out, du_out, _out, wide_v, mask_v, stacked_v, du_v):
    rows = BACK_ROWS[level]
    keep_later(level, info, ((grad, grad_out), (du, du_out)))

    @pl.when(info[0] == level)
    def _():
        fill_masks(mask_v, starts, window, info[1], level, BACK_HALO[level], rows)
        spread_grads(arrived, wide_v, slope, du_v, rows)
        finish_backward(level, du_v, mask_v, stacked_v, weight, send_out, grad_out)
        own_grads(level, du_v, du_out)


def backward_call(level, window, info, starts, weight, token, arrived, slope, grad, du):
    rows = BACK_ROWS[level]
    return call(
        functools.partial(backward_kernel, level, window),
        f"backward{level}",
        2 * rows * C * C * TAPS,
        (info, starts),
        (arrived, slope, weight, grad, du),
        (shape_of(SEND_ROWS[level], C), shape_of(256, C), shape_of(256, C)),
        token,
        [
            pltpu.VMEM((C // 128, rows, 128), F32),
            pltpu.VMEM((TAPS, rows, 128), F32),
            pltpu.VMEM((rows, TAPS * C), BF16),
            pltpu.VMEM((rows, C), F32),
        ],
        aliases=((3, 1), (4, 2)),
    )


def first_du_kernel(info, arrived, slope, du, _token, all_out, du_out, _out, wide_v, du_v):
    rows = BACK_ROWS[0]
    keep_later(0, info, ((du, du_out),))

    @pl.when(info[0] == 0)
    def _():
        spread_grads(arrived, wide_v, slope, du_v, rows)
        own_grads(0, du_v, du_out)
        all_out[...] = du_v[...].astype(BF16)


def first_du_call(info, token, arrived, slope, du):
    rows = BACK_ROWS[0]
    return call(
        first_du_kernel,
        "first_du",
        rows * C * 8,
        (info,),
        (arrived, slope, du),
        (shape_of(rows, C), shape_of(256, C)),
        token,
        [pltpu.VMEM((C // 128, rows, 128), F32), pltpu.VMEM((rows, C), F32)],
        aliases=((2, 1),),
    )


def first_grad_kernel(window, info, starts, du, weight, grad, _token, grad_out, _out, mask_v,
                      stacked_v):
    rows = BACK_ROWS[0]
    keep_later(0, info, ((grad, grad_out),))

    @pl.when(info[0] == 0)
    def _():
        fill_masks(mask_v, starts, window, info[1], 0, BACK_HALO[0], rows)
        finish_backward(0, du, mask_v, stacked_v, weight, None, grad_out)


def first_grad_call(window, info, starts, weight, token, du, grad):
    rows = BACK_ROWS[0]
    return call(
        functools.partial(first_grad_kernel, window),
        "first_grad",
        2 * rows * C * C * TAPS,
        (info, starts),
        (du, weight, grad),
        (shape_of(256, C),),
        token,
        [pltpu.VMEM((TAPS, rows, 128), F32), pltpu.VMEM((rows, TAPS * C), BF16)],
        aliases=((2, 0),),
    )


def gather_kernel(windows, *refs):
    out = refs[-2]
    for window in range(windows):
        out[0, window] = refs[window][...]


def gather_call(token, grads):
    return call(
        functools.partial(gather_kernel, len(grads)), "gather", 1000000, (), tuple(grads),
        (shape_of(1, len(grads), 256, C),), token, [],
    )


def fill_order(seq, order_ref):
    row = lax.broadcasted_iota(jnp.int32, (C, 128), 0)
    place = (row * 2731) >> 16
    swap = (seq ^ (place >> 4)) & 1
    one, two = place & 3, (place >> 2) & 3
    along_z, along_y = jnp.where(swap == 1, two, one), jnp.where(swap == 1, one, two)
    apart = (along_y << 3) | (along_z << 1) | (place >> 4)
    source = CHUNK * (seq ^ apart) + (row - CHUNK * place)
    lane = lax.broadcasted_iota(jnp.int32, (C, 128), 1)
    for index in range(C // 128):
        order_ref[:, index * 128 : (index + 1) * 128] = jnp.where(
            source == lane + index * 128, 1.0, 0.0
        ).astype(BF16)


def side_kernel(level, windows, info, *refs):
    halo, own = HALO[level], OWN[level]
    count = len(windows)
    xs = refs[:count]
    side_out, _, order_v, side_v, sems = refs[-5:]
    total = count * own
    padding = -total % 128

    def leave(place):
        return pltpu.make_async_copy(
            side_v.at[place], side_out.at[:, lanes(windows[place], 256)], sems.at[place]
        )

    @pl.when(info[0] == level)
    def _():
        fill_order(info[1], order_v)

        def one_tap(tap):
            parts = [x[halo : halo + own, lanes(tap, C)] for x in xs]
            if padding:
                parts.append(jnp.zeros((padding, C), BF16))
            found = lax.dot_general(
                order_v[...],
                jnp.concatenate(parts, axis=0),
                (((1,), (1,)), ((), ())),
                preferred_element_type=F32,
            )
            for place in range(count):
                part = found[:, place * own : (place + 1) * own]
                if own < 256:
                    part = jnp.concatenate([part, jnp.zeros((C, 256 - own), F32)], axis=1)
                side_v[place, lanes(tap, C), :] = part.astype(BF16)

        loop(TAPS, one_tap)
        for place in range(count):
            leave(place).start()
        for place in range(count):
            leave(place).wait()


def side_call(level, windows, info, token, side, *xs):
    return call(
        functools.partial(side_kernel, level, windows),
        f"side{level}",
        2 * len(windows) * 256 * C * C * TAPS,
        (info,),
        xs,
        (),
        token,
        [
            pltpu.VMEM((C, C), BF16),
            pltpu.VMEM((len(windows), TAPS * C, 256), BF16),
            pltpu.SemaphoreType.DMA((len(windows),)),
        ],
        held=side,
        far_out=shape_of(TAPS * C, 3 * 256),
    )


def weight_kernel(half, side, *refs):
    dus = refs[:-5]
    _, send_out, keep_out, _, du_v = refs[-5:]
    first = sum(PIECES[:half])
    for window, du in enumerate(dus):
        du_v[window * 256 : (window + 1) * 256, :] = du[...]

    def one_piece(piece):
        place = first + piece
        tap, part = place // 3, place % 3
        found = jnp.dot(
            side[lanes(tap, C), :], du_v[:, lanes(part, 256)], preferred_element_type=F32
        ).reshape(2, 16, CHUNK, 256)
        cols = lanes(piece, 256)
        keep_out[:, :, cols] = found[0].astype(BF16)
        send_out[:, :, cols] = found[1].astype(BF16)

    loop(PIECES[half], one_piece, PIECES[half])


def weight_call(quarter, token, side, dus):
    width = PIECES[quarter] * 256
    shape = shape_of(16, CHUNK, width)
    return call(
        functools.partial(weight_kernel, quarter),
        f"weight{quarter}",
        2 * C * 768 * width,
        (),
        (side, *dus),
        (shape, shape),
        token,
        [pltpu.VMEM((len(dus) * 256, C), BF16)],
    )


def half_plan(one, two):
    held = [(second, first) for second in range(4) for first in range(4)]
    plan = []
    for axis, apart, gone in (
        (1, one, (one, 2)), (0, one, (one, 2)), (1, two, (two,)), (0, two, (two,))
    ):
        leaving = [place for place in held if place[axis] in gone]
        leaving.sort(key=lambda place: (place[1 - axis], gone.index(place[axis])))
        staying = []
        for place in leaving:
            moved = list(place)
            moved[axis] ^= apart
            staying.append(tuple(moved))
        plan.append(
            (
                axis,
                apart,
                [held.index(place) for place in leaving],
                [held.index(place) for place in staying],
            )
        )
        held = staying
    return plan


PLANS = (half_plan(1, 3), half_plan(3, 1))


def added(keep, arrived, source):
    return keep[source].astype(F32) + arrived[source].astype(F32)


def add_kernel(half, step, keep, arrived, _, stay_out, leave_out, _out):
    _, _, leaving, staying = PLANS[half][step]
    for target, sources in ((stay_out, staying), (leave_out, leaving)):
        for row, source in enumerate(sources):
            target[row] = added(keep, arrived, source).astype(BF16)


def add_call(half, step, token, keep, arrived):
    shape = shape_of(len(PLANS[half][step][2]), CHUNK, keep.shape[-1])
    return call(
        functools.partial(add_kernel, half, step),
        f"add{half}_{step}",
        4000000 // (1 << step),
        (),
        (keep, arrived),
        (shape, shape),
        token,
        [],
    )


def final_kernel(keep_a, arrived_a, keep_b, arrived_b, _, out, _out):
    for half, (keep, arrived) in enumerate(((keep_a, arrived_a), (keep_b, arrived_b))):
        total = added(keep, arrived, 0)
        piece = sum(PIECES[:half])
        for place in range(PIECES[half]):
            tap, part = divmod(piece + place, 3)
            out[tap, :, part * 256 : (part + 1) * 256] = total[:, place * 256 : (place + 1) * 256]


def final_call(token, *parts):
    return call(
        final_kernel, "final", 1, (), parts, (shape_of(TAPS, CHUNK, C, dtype=F32),), token, []
    )


def section_pairs(source, target, shards):
    return [(source * shards + place, target * shards + place) for place in range(shards)]


def apart_pairs(sections, shards, apart):
    return [
        (section * shards + place, section * shards + (place ^ apart))
        for section in range(sections)
        for place in range(shards)
    ]


def mixed_pairs(sections, shards, axis, apart):
    units = (8, 2) if axis == 0 else (2, 8)
    return [
        (section * shards + place, section * shards + (place ^ (apart * units[place % 2])))
        for section in range(sections)
        for place in range(shards)
    ]


def body(dna_embed, conv_weight, interval_starts, cotangent):
    windows = dna_embed.shape[0]
    sections = lax.axis_size("section")
    shards = lax.axis_size("seq")
    section_index = lax.axis_index("section")
    seq_index = lax.axis_index("seq")
    info = jnp.stack([section_index, seq_index]).astype(jnp.int32)
    weight = jnp.transpose(conv_weight[0], (1, 0, 2)).reshape(TAPS * C, C)
    starts = interval_starts
    token = jnp.zeros((8, 128), F32)

    ends = (0, sections - 1)
    near_pairs = [
        pair for pair in apart_pairs(sections, shards, 1) if pair[0] // shards in ends
    ]
    far_pairs = [
        (section * shards + place, section * shards + place + by)
        for section in ends
        for place in range(shards)
        for by in (1 if place % 2 else -1,)
        if 0 <= place + by < shards
    ]
    near, far, rest, token = edges_call(info, token, dna_embed, cotangent)
    near = lax.ppermute(near, AXES, near_pairs)
    far = lax.ppermute(far, AXES, [pair for pair in far_pairs if pair[0] < shards])
    rest = lax.ppermute(rest, AXES, far_pairs)

    def relay(value, source, target):
        return lax.ppermute(value, AXES, section_pairs(source, target, shards))

    inputs = [[None] * windows for _ in range(4)]
    slopes = [[None] * windows for _ in range(4)]
    stacks = [[None] * windows for _ in range(4)]
    grads = [None] * windows
    dus = [None] * windows
    wide_du = [None] * windows
    arrived = [None] * windows
    side = None

    def forward(level, window, send=True):
        nonlocal token
        xs = (inputs[level][window],)
        if level == 0:
            xs = (dna_embed, near, rest if window else far)
        pooled, slopes[level][window], stacks[level][window], token = forward_call(
            level, window, info, starts, weight, token, *xs
        )
        if send:
            inputs[level + 1][window] = relay(pooled, level, level + 1)
        return pooled

    def turn(window, *held):
        nonlocal token
        send, grads[window], dus[window], stacks[3][window], token = last_call(
            window, info, starts, weight, turned, token, inputs[3][window], cotangent, near, rest,
            *held,
        )
        if held:
            pairs = section_pairs(2, 3, shards) + section_pairs(3, 2, shards)
            arrived[window] = lax.ppermute(send, AXES, pairs)
        else:
            arrived[window] = relay(send, 3, 2)
        return arrived[window]

    def backward(level, window):
        nonlocal token
        send, grads[window], dus[window], token = backward_call(
            level, window, info, starts, turned, token, arrived[window], slopes[level][window],
            grads[window], dus[window],
        )
        arrived[window] = relay(send, level, level - 1)

    def arrive(window):
        nonlocal token
        wide_du[window], dus[window], token = first_du_call(
            info, token, arrived[window], slopes[0][window], dus[window]
        )

    def first_grad(window):
        nonlocal token
        grads[window], token = first_grad_call(
            window, info, starts, weight, token, wide_du[window], grads[window]
        )

    def sideways(level, *chosen):
        nonlocal side, token
        chosen = chosen or tuple(range(windows))
        xs = [stacks[level][window] for window in chosen]
        side, token = side_call(level, chosen, info, token, side, *xs)

    forward(0, 0)
    turned, token = turn_call(info, token, weight)
    forward(0, 1)
    forward(0, 2)
    sideways(0)
    forward(1, 0)
    sideways(1, 0)
    forward(1, 1)
    forward(1, 2)
    sideways(1, 1, 2)
    forward(2, 0)
    inputs[3][1] = turn(0, forward(2, 1, send=False))
    forward(2, 2)
    backward(2, 0)
    turn(1)
    turn(2)
    backward(2, 1)
    backward(2, 2)
    sideways(3)
    sideways(2)
    backward(1, 0)
    backward(1, 1)
    backward(1, 2)
    arrive(0)
    first_grad(0)
    arrive(1)
    arrive(2)

    keeps, arriveds = [None, None], [None, None]

    def weigh(half):
        nonlocal token
        send, keeps[half], token = weight_call(half, token, side, dus)
        arriveds[half] = lax.ppermute(send, AXES, apart_pairs(sections, shards, 1))

    def pass_on(half, step):
        nonlocal token
        keeps[half], leaving, token = add_call(half, step, token, keeps[half], arriveds[half])
        axis, apart = PLANS[half][step][:2]
        arriveds[half] = lax.ppermute(leaving, AXES, mixed_pairs(sections, shards, axis, apart))

    weigh(0)
    weigh(1)
    pass_on(0, 0)
    pass_on(1, 0)
    first_grad(1)
    pass_on(0, 1)
    pass_on(1, 1)
    first_grad(2)
    pass_on(0, 2)
    pass_on(1, 2)
    input_grads, token = gather_call(token, grads)
    pass_on(0, 3)
    pass_on(1, 3)
    weight_grad, token = final_call(token, keeps[0], arriveds[0], keeps[1], arriveds[1])
    weight_grad = jnp.transpose(weight_grad, (1, 0, 2))[None]
    return (weight_grad, input_grads)


def solution(mesh):
    placed = (P(None, "seq", None), P("section", None, None, None), P(), P(None, "seq", None))
    return jax.shard_map(
        body,
        mesh=mesh,
        in_specs=placed,
        out_specs=(P("section", "seq", None, None), P("section", None, "seq", None)),
        check_vma=False,
    )
```

```python
import functools

import jax
import jax.numpy as jnp
from jax import lax
from jax.experimental import pallas as pl
from jax.experimental.pallas import tpu as pltpu
from jax.sharding import PartitionSpec as P

C = 768
TAPS = 5
AXES = ("section", "seq")
OWN = (256, 128, 64, 32)
HALO = (64, 32, 16, 8)
ROWS = (384, 192, 96, 48)
BACK_HALO = (16, 16, 16, 8)
BACK_ROWS = (288, 160, 96, 48)
SEND_ROWS = (0, 144, 80, 48)
CHUNK = 24
LIMIT = 16 * 1024 * 1024
F32 = jnp.float32
BF16 = jnp.bfloat16
ANY = pl.BlockSpec(memory_space=pl.ANY)
SMEM = pl.BlockSpec(memory_space=pltpu.SMEM)
VMEM = pl.BlockSpec(memory_space=pltpu.VMEM)
PIECES = (8, 7)
BLOCKS_UNROLL = 3


def shape_of(*dims, dtype=BF16):
    return jax.ShapeDtypeStruct(dims, dtype)


def call(kernel, name, flops, smem, vmem, outs, token, scratch, aliases=(), held=None, far_out=None):
    extra = () if held is None else (held,)
    operands = (*smem, *vmem, *extra, token)
    count = len(operands)
    pairs = {len(smem) + place: out for place, out in aliases}
    far_shape = held if held is not None else far_out
    far = () if far_shape is None else (shape_of(*far_shape.shape, dtype=far_shape.dtype),)
    if extra:
        pairs[count - 2] = len(outs)
    pairs[count - 1] = len(outs) + len(far)
    return pl.pallas_call(
        kernel,
        out_shape=(*outs, *far, jax.ShapeDtypeStruct(token.shape, token.dtype)),
        in_specs=[SMEM] * len(smem) + [VMEM] * len(vmem) + [ANY] * (len(extra) + 1),
        out_specs=(*[VMEM] * len(outs), *[ANY] * (len(far) + 1)),
        scratch_shapes=scratch,
        input_output_aliases=pairs,
        compiler_params=pltpu.CompilerParams(vmem_limit_bytes=LIMIT),
        cost_estimate=pl.CostEstimate(flops=int(flops) if name in ("edges", "forward0", "turn", "backward1") else 1, bytes_accessed=1000000 if name in ("edges", "forward0", "turn", "backward1") else 1, transcendentals=0),
        name=name,
    )(*operands)


def no_cut(starts, window, positions, level, length):
    cut = positions == length
    for entry in range(starts.shape[1]):
        first = (starts[window, entry] + ((1 << level) - 1)) >> level
        cut = cut | (positions == first)
    return jnp.where(cut, 0.0, 1.0)


def lanes(index, width, first=0):
    if isinstance(index, int):
        return slice(first + index * width, first + (index + 1) * width)
    return pl.ds(pl.multiple_of(first + index * width, 128), width)


def loop(count, run, unroll=1):
    if unroll == count:
        for index in range(count):
            run(index)
        return

    def step(index, carry):
        run(index)
        return carry

    lax.fori_loop(0, count, step, 0, unroll=unroll)


def roll_rows(value, by):
    return pltpu.roll(value, by % value.shape[0], 0)


def fill_masks(mask_ref, starts, window, seq, level, halo, rows):
    own = OWN[level]
    length = own * 32
    row = lax.broadcasted_iota(jnp.int32, (rows, 128), 0)
    positions = row + (seq * own - halo)
    inside = jnp.where((positions >= 0) & (positions < length), 1.0, 0.0)
    free = no_cut(starts, window, positions, level, length)
    before = inside * free
    after = inside * roll_rows(free, -1)
    mask_ref[0, 0:rows] = before * roll_rows(free, 1)
    mask_ref[1, 0:rows] = before
    mask_ref[2, 0:rows] = inside
    mask_ref[3, 0:rows] = after
    mask_ref[4, 0:rows] = after * roll_rows(free, -2)


def stack_inputs(read, mask_ref, stacked_ref, rows, steps=1):
    part = C // 128 // steps

    def columns(first):
        for index in [first * part + place for place in range(part)]:
            tile = read(lanes(index, 128)).astype(F32)
            for tap in range(TAPS):
                moved = roll_rows(tile, 2 - tap) if tap != 2 else tile
                stacked_ref[0:rows, lanes(index, 128, tap * C)] = (
                    moved * mask_ref[tap, 0:rows]
                ).astype(BF16)

    columns(0) if steps == 1 else loop(steps, columns)


def stack_grads(value_ref, mask_ref, stacked_ref, rows, steps=1):
    part = C // 128 // steps

    def columns(first):
        for index in [first * part + place for place in range(part)]:
            tile = value_ref[0:rows, lanes(index, 128)].astype(F32)
            for tap in range(TAPS):
                moved = tile * mask_ref[tap, 0:rows]
                moved = roll_rows(moved, tap - 2) if tap != 2 else moved
                stacked_ref[0:rows, lanes(index, 128, tap * C)] = moved.astype(BF16)

    columns(0) if steps == 1 else loop(steps, columns)


def conv_columns(stacked_ref, weight_ref, index):
    return jnp.dot(
        stacked_ref[...], weight_ref[:, lanes(index, 256)], preferred_element_type=F32
    )


def back_columns(stacked_ref, weight_ref, index, turned):
    if turned:
        return conv_columns(stacked_ref, weight_ref, index)
    total = None
    for tap in range(TAPS):
        part = lax.dot_general(
            stacked_ref[:, tap * C : (tap + 1) * C],
            weight_ref[lanes(index, 256, tap * C), :],
            (((1,), (1,)), ((), ())),
            preferred_element_type=F32,
        )
        total = part if total is None else total + part
    return total


def turn_kernel(info, weight, _, turned_out, _out, unit_v):
    @pl.when(info[0] > 0)
    def _():
        row = lax.broadcasted_iota(jnp.int32, (C, 128), 0)
        lane = lax.broadcasted_iota(jnp.int32, (C, 128), 1)
        for index in range(C // 128):
            unit_v[:, index * 128 : (index + 1) * 128] = jnp.where(
                row == lane + index * 128, 1.0, 0.0
            ).astype(BF16)

        def block(place):
            tap, index = place // 3, place % 3
            turned_out[lanes(tap, C), lanes(index, 256)] = lax.dot_general(
                unit_v[...],
                weight[lanes(place, 256), :],
                (((1,), (1,)), ((), ())),
                preferred_element_type=F32,
            ).astype(BF16)

        loop(TAPS * 3, block)


def turn_call(info, token, weight):
    return call(
        turn_kernel, "turn", 2 * C * C * C * TAPS, (info,), (weight,), (shape_of(TAPS * C, C),),
        token, [pltpu.VMEM((C, C), BF16)],
    )


def gelu_and_slope(u):
    scale = 0.7978845608028654
    square = u * u
    bend = jnp.tanh(scale * (u + 0.044715 * square * u))
    half = 0.5 * (1.0 + bend)
    slope = half + 0.5 * u * (1.0 - bend * bend) * (scale * (1.0 + 0.134145 * square))
    return u * half, slope


def fill_edges(odd, fill):
    pl.when(odd)(functools.partial(fill, True))
    pl.when(jnp.logical_not(odd))(functools.partial(fill, False))


def edges_kernel(windows, info, dna, _, near, first, rest, _out):
    own = OWN[0]

    def fill(leading_to_near):
        near_x, far_x = (0, own - 64) if leading_to_near else (own - 64, 0)

        @pl.when(info[0] == 0)
        def _():
            for window in range(windows):
                near[window * 64 : window * 64 + 64, :] = dna[window, near_x : near_x + 64, :]
                edge = dna[window, far_x : far_x + 64, :]
                if window == 0:
                    first[...] = edge
                else:
                    rest[(window - 1) * 64 : window * 64, :] = edge

    fill_edges(info[1] % 2 == 1, fill)


def edges_call(info, token, dna):
    windows = dna.shape[0]
    return call(
        functools.partial(edges_kernel, windows),
        "edges",
        2e10,
        (info,),
        (dna,),
        (shape_of(windows * 64, C), shape_of(64, C), shape_of((windows - 1) * 64, C)),
        token,
        [],
    )


def cotangent_edges_kernel(windows, info, cot, _, near, far, _out):
    part = cot.shape[1]

    def fill(leading_to_near):
        near_c, far_c = (0, part - 16) if leading_to_near else (part - 16, 0)

        @pl.when(info[0] == 3)
        def _():
            for window in range(windows):
                lines = slice(window * 16, window * 16 + 16)
                near[lines, :] = cot[window, near_c : near_c + 16, :]
                far[lines, :] = cot[window, far_c : far_c + 16, :]

    fill_edges(info[1] % 2 == 1, fill)


def cotangent_edges_call(info, token, cot):
    windows = cot.shape[0]
    edge = shape_of(windows * 16, C)
    return call(
        functools.partial(cotangent_edges_kernel, windows), "cotangent_edges", 1, (info,), (cot,),
        (edge, edge), token, [],
    )


def sides(odd, near, far):
    near, far = near.astype(F32), far.astype(F32)
    return jnp.where(odd, near, far), jnp.where(odd, far, near)


def with_edges(own, near, far, odd, low, high):
    ahead, behind = sides(odd, near, far)
    return jnp.concatenate([ahead[low:], own.astype(F32), behind[:high]], axis=0)


def forward_kernel(level, window, info, starts, *refs):
    rows, back = ROWS[level], BACK_ROWS[level]
    skip = HALO[level] - BACK_HALO[level]
    inputs = 3 if level == 0 else 1
    xs = refs[:inputs]
    weight, _, pooled_out, slope_out, stacked_v, _, mask_v, act_v = refs[inputs:]

    def read(cols):
        if level == 0:
            x_in, near, far = xs
            first = max(window - 1, 0) * 64
            return with_edges(
                x_in[window, :, cols],
                near[window * 64 : window * 64 + 64, cols],
                far[first : first + 64, cols],
                info[1] % 2 == 1,
                0,
                64,
            )
        return xs[0][:, cols]

    @pl.when(info[0] == level)
    def _():
        fill_masks(mask_v, starts, window, info[1], level, HALO[level], rows)
        stack_inputs(read, mask_v, stacked_v, rows)

        def block(index):
            act, slope = gelu_and_slope(conv_columns(stacked_v, weight, index))
            slope_out[:, lanes(index, 256)] = slope[skip : skip + back]
            for half in range(2):
                place = index * 2 + half
                act_v[place] = act[:, half * 128 : (half + 1) * 128]
                even = act_v[place, pl.ds(0, rows // 2, stride=2), :]
                odd = act_v[place, pl.ds(1, rows // 2, stride=2), :]
                pooled_out[:, lanes(place, 128)] = (0.5 * (even + odd)).astype(BF16)

        loop(C // 256, block, BLOCKS_UNROLL)


def forward_call(level, window, info, starts, weight, token, *xs):
    rows, back = ROWS[level], BACK_ROWS[level]
    return call(
        functools.partial(forward_kernel, level, window),
        f"forward{level}",
        2 * rows * C * C * TAPS,
        (info, starts),
        (*xs, weight),
        (shape_of(rows // 2, C), shape_of(back, C, dtype=F32), shape_of(rows, TAPS * C)),
        token,
        [
            pltpu.VMEM((TAPS, rows, 128), F32),
            pltpu.VMEM((C // 128, rows, 128), F32),
        ],
    )


def finish_backward(level, du_v, mask_v, stacked_v, weight, send_out, grad_out):
    rows, own, halo = BACK_ROWS[level], OWN[level], BACK_HALO[level]
    send = SEND_ROWS[level]
    trim = (rows - send) // 2
    stack_grads(du_v, mask_v, stacked_v, rows)

    def block(index):
        found = back_columns(stacked_v, weight, index, level > 0)
        cols = lanes(index, 256)
        if send:
            send_out[:, cols] = found[trim : trim + send].astype(BF16)
        grad_out[0:own, cols] = found[halo : halo + own].astype(BF16)

    loop(C // 256, block, BLOCKS_UNROLL)
    if own < 256:
        grad_out[own:, :] = jnp.zeros((256 - own, C), BF16)


def own_grads(level, du_v, du_out):
    own, halo = OWN[level], BACK_HALO[level]
    du_out[0:own, :] = du_v[halo : halo + own, :].astype(BF16)
    if own < 256:
        du_out[own:, :] = jnp.zeros((256 - own, C), BF16)


def last_kernel(window, info, starts, x_in, cot, near, far, weight, turned, *refs):
    send_out, grad_out, du_out, inputs_v, _, mask_v, stacked_v, du_v = refs[-8:]
    level, rows = 3, ROWS[3]
    if len(refs) == 10:

        @pl.when(info[0] == 2)
        def _():
            send_out[...] = refs[0][...]

    @pl.when(info[0] == level)
    def _():
        fill_masks(mask_v, starts, window, info[1], level, HALO[level], rows)
        stack_inputs(
            lambda cols: x_in[:, cols], mask_v, inputs_v, rows
        )

        def block(index):
            _, slope = gelu_and_slope(conv_columns(inputs_v, weight, index))
            cols = lanes(index, 256)
            lines = slice(window * 16, window * 16 + 16)
            g = with_edges(
                cot[window, :, cols], near[lines, cols], far[lines, cols], info[1] % 2 == 1, 8, 8
            )
            du_v[:, cols] = (g * slope).astype(BF16).astype(F32)

        loop(C // 256, block, BLOCKS_UNROLL)
        finish_backward(level, du_v, mask_v, stacked_v, turned, send_out, grad_out)
        own_grads(level, du_v, du_out)


def last_call(window, info, starts, weight, turned, token, x, cot, near, far, *held):
    rows = ROWS[3]
    return call(
        functools.partial(last_kernel, window),
        "last",
        4 * rows * C * C * TAPS,
        (info, starts),
        (x, cot, near, far, weight, turned, *held),
        (shape_of(rows, C), shape_of(256, C), shape_of(256, C), shape_of(rows, TAPS * C)),
        token,
        [
            pltpu.VMEM((TAPS, rows, 128), F32),
            pltpu.VMEM((rows, TAPS * C), BF16),
            pltpu.VMEM((rows, C), F32),
        ],
        aliases=((6, 0),) if held else (),
    )


def spread_grads(arrived, wide_v, slope, du_v, rows):
    def column(index):
        cols = lanes(index, 128)
        half = 0.5 * arrived[:, cols].astype(F32)
        wide_v[index, pl.ds(0, rows // 2, stride=2), :] = half
        wide_v[index, pl.ds(1, rows // 2, stride=2), :] = half
        du_v[:, cols] = (wide_v[index] * slope[:, cols]).astype(BF16).astype(F32)

    loop(C // 128, column, C // 128)


def keep_later(level, info, pairs):
    @pl.when(info[0] > level)
    def _():
        for source, target in pairs:
            target[...] = source[...]


def backward_kernel(level, window, info, starts, arrived, slope, weight, grad, du, _token,
                    send_out, grad_out, du_out, _out, wide_v, mask_v, stacked_v, du_v):
    rows = BACK_ROWS[level]
    keep_later(level, info, ((grad, grad_out), (du, du_out)))

    @pl.when(info[0] == level)
    def _():
        fill_masks(mask_v, starts, window, info[1], level, BACK_HALO[level], rows)
        spread_grads(arrived, wide_v, slope, du_v, rows)
        finish_backward(level, du_v, mask_v, stacked_v, weight, send_out, grad_out)
        own_grads(level, du_v, du_out)


def backward_call(level, window, info, starts, weight, token, arrived, slope, grad, du):
    rows = BACK_ROWS[level]
    return call(
        functools.partial(backward_kernel, level, window),
        f"backward{level}",
        2 * rows * C * C * TAPS,
        (info, starts),
        (arrived, slope, weight, grad, du),
        (shape_of(SEND_ROWS[level], C), shape_of(256, C), shape_of(256, C)),
        token,
        [
            pltpu.VMEM((C // 128, rows, 128), F32),
            pltpu.VMEM((TAPS, rows, 128), F32),
            pltpu.VMEM((rows, TAPS * C), BF16),
            pltpu.VMEM((rows, C), F32),
        ],
        aliases=((3, 1), (4, 2)),
    )


def first_du_kernel(info, arrived, slope, du, _token, all_out, du_out, _out, wide_v, du_v):
    rows = BACK_ROWS[0]
    keep_later(0, info, ((du, du_out),))

    @pl.when(info[0] == 0)
    def _():
        spread_grads(arrived, wide_v, slope, du_v, rows)
        own_grads(0, du_v, du_out)
        all_out[...] = du_v[...].astype(BF16)


def first_du_call(info, token, arrived, slope, du):
    rows = BACK_ROWS[0]
    return call(
        first_du_kernel,
        "first_du",
        rows * C * 8,
        (info,),
        (arrived, slope, du),
        (shape_of(rows, C), shape_of(256, C)),
        token,
        [pltpu.VMEM((C // 128, rows, 128), F32), pltpu.VMEM((rows, C), F32)],
        aliases=((2, 1),),
    )


def first_grad_kernel(window, info, starts, du, weight, grad, _token, grad_out, _out, mask_v,
                      stacked_v):
    rows = BACK_ROWS[0]
    keep_later(0, info, ((grad, grad_out),))

    @pl.when(info[0] == 0)
    def _():
        fill_masks(mask_v, starts, window, info[1], 0, BACK_HALO[0], rows)
        finish_backward(0, du, mask_v, stacked_v, weight, None, grad_out)


def first_grad_call(window, info, starts, weight, token, du, grad):
    rows = BACK_ROWS[0]
    return call(
        functools.partial(first_grad_kernel, window),
        "first_grad",
        2 * rows * C * C * TAPS,
        (info, starts),
        (du, weight, grad),
        (shape_of(256, C),),
        token,
        [pltpu.VMEM((TAPS, rows, 128), F32), pltpu.VMEM((rows, TAPS * C), BF16)],
        aliases=((2, 0),),
    )


def gather_kernel(windows, *refs):
    out = refs[-2]
    for window in range(windows):
        out[0, window] = refs[window][...]


def gather_call(token, grads):
    return call(
        functools.partial(gather_kernel, len(grads)), "gather", 1000000, (), tuple(grads),
        (shape_of(1, len(grads), 256, C),), token, [],
    )


def fill_order(seq, order_ref):
    row = lax.broadcasted_iota(jnp.int32, (C, 128), 0)
    place = (row * 2731) >> 16
    swap = (seq ^ (place >> 4)) & 1
    one, two = place & 3, (place >> 2) & 3
    along_z, along_y = jnp.where(swap == 1, two, one), jnp.where(swap == 1, one, two)
    apart = (along_y << 3) | (along_z << 1) | (place >> 4)
    source = CHUNK * (seq ^ apart) + (row - CHUNK * place)
    lane = lax.broadcasted_iota(jnp.int32, (C, 128), 1)
    for index in range(C // 128):
        order_ref[:, index * 128 : (index + 1) * 128] = jnp.where(
            source == lane + index * 128, 1.0, 0.0
        ).astype(BF16)


def side_kernel(level, windows, info, *refs):
    halo, own = HALO[level], OWN[level]
    count = len(windows)
    xs = refs[:count]
    side_out, _, order_v, side_v, sems = refs[-5:]
    total = count * own
    padding = -total % 128

    def leave(place):
        return pltpu.make_async_copy(
            side_v.at[place], side_out.at[:, lanes(windows[place], 256)], sems.at[place]
        )

    @pl.when(info[0] == level)
    def _():
        fill_order(info[1], order_v)

        def one_tap(tap):
            parts = [x[halo : halo + own, lanes(tap, C)] for x in xs]
            if padding:
                parts.append(jnp.zeros((padding, C), BF16))
            found = lax.dot_general(
                order_v[...],
                jnp.concatenate(parts, axis=0),
                (((1,), (1,)), ((), ())),
                preferred_element_type=F32,
            )
            for place in range(count):
                part = found[:, place * own : (place + 1) * own]
                if own < 256:
                    part = jnp.concatenate([part, jnp.zeros((C, 256 - own), F32)], axis=1)
                side_v[place, lanes(tap, C), :] = part.astype(BF16)

        loop(TAPS, one_tap)
        for place in range(count):
            leave(place).start()
        for place in range(count):
            leave(place).wait()


def side_call(level, windows, info, token, side, *xs):
    return call(
        functools.partial(side_kernel, level, windows),
        f"side{level}",
        2 * len(windows) * 256 * C * C * TAPS,
        (info,),
        xs,
        (),
        token,
        [
            pltpu.VMEM((C, C), BF16),
            pltpu.VMEM((len(windows), TAPS * C, 256), BF16),
            pltpu.SemaphoreType.DMA((len(windows),)),
        ],
        held=side,
        far_out=shape_of(TAPS * C, 3 * 256),
    )


def weight_kernel(half, side, *refs):
    dus = refs[:-5]
    _, send_out, keep_out, _, du_v = refs[-5:]
    first = sum(PIECES[:half])
    for window, du in enumerate(dus):
        du_v[window * 256 : (window + 1) * 256, :] = du[...]

    def one_piece(piece):
        place = first + piece
        tap, part = place // 3, place % 3
        found = jnp.dot(
            side[lanes(tap, C), :], du_v[:, lanes(part, 256)], preferred_element_type=F32
        ).reshape(2, 16, CHUNK, 256)
        cols = lanes(piece, 256)
        keep_out[:, :, cols] = found[0].astype(BF16)
        send_out[:, :, cols] = found[1].astype(BF16)

    loop(PIECES[half], one_piece, PIECES[half])


def weight_call(quarter, token, side, dus):
    width = PIECES[quarter] * 256
    shape = shape_of(16, CHUNK, width)
    return call(
        functools.partial(weight_kernel, quarter),
        f"weight{quarter}",
        2 * C * 768 * width,
        (),
        (side, *dus),
        (shape, shape),
        token,
        [pltpu.VMEM((len(dus) * 256, C), BF16)],
    )


def half_plan(one, two):
    held = [(second, first) for second in range(4) for first in range(4)]
    plan = []
    for axis, apart, gone in (
        (1, one, (one, 2)), (0, one, (one, 2)), (1, two, (two,)), (0, two, (two,))
    ):
        leaving = [place for place in held if place[axis] in gone]
        leaving.sort(key=lambda place: (place[1 - axis], gone.index(place[axis])))
        staying = []
        for place in leaving:
            moved = list(place)
            moved[axis] ^= apart
            staying.append(tuple(moved))
        plan.append(
            (
                axis,
                apart,
                [held.index(place) for place in leaving],
                [held.index(place) for place in staying],
            )
        )
        held = staying
    return plan


PLANS = (half_plan(1, 3), half_plan(3, 1))


def added(keep, arrived, source):
    return keep[source].astype(F32) + arrived[source].astype(F32)


def add_kernel(half, step, keep, arrived, _, stay_out, leave_out, _out):
    _, _, leaving, staying = PLANS[half][step]
    for target, sources in ((stay_out, staying), (leave_out, leaving)):
        for row, source in enumerate(sources):
            target[row] = added(keep, arrived, source).astype(BF16)


def add_call(half, step, token, keep, arrived):
    shape = shape_of(len(PLANS[half][step][2]), CHUNK, keep.shape[-1])
    return call(
        functools.partial(add_kernel, half, step),
        f"add{half}_{step}",
        4000000 // (1 << step),
        (),
        (keep, arrived),
        (shape, shape),
        token,
        [],
    )


def final_kernel(keep_a, arrived_a, keep_b, arrived_b, _, out, _out):
    for half, (keep, arrived) in enumerate(((keep_a, arrived_a), (keep_b, arrived_b))):
        total = added(keep, arrived, 0)
        piece = sum(PIECES[:half])
        for place in range(PIECES[half]):
            tap, part = divmod(piece + place, 3)
            out[tap, :, part * 256 : (part + 1) * 256] = total[:, place * 256 : (place + 1) * 256]


def final_call(token, *parts):
    return call(
        final_kernel, "final", 1, (), parts, (shape_of(TAPS, CHUNK, C, dtype=F32),), token, []
    )


def section_pairs(source, target, shards):
    return [(source * shards + place, target * shards + place) for place in range(shards)]


def apart_pairs(sections, shards, apart):
    return [
        (section * shards + place, section * shards + (place ^ apart))
        for section in range(sections)
        for place in range(shards)
    ]


def mixed_pairs(sections, shards, axis, apart):
    units = (8, 2) if axis == 0 else (2, 8)
    return [
        (section * shards + place, section * shards + (place ^ (apart * units[place % 2])))
        for section in range(sections)
        for place in range(shards)
    ]


def body(dna_embed, conv_weight, interval_starts, cotangent):
    windows = dna_embed.shape[0]
    sections = lax.axis_size("section")
    shards = lax.axis_size("seq")
    section_index = lax.axis_index("section")
    seq_index = lax.axis_index("seq")
    info = jnp.stack([section_index, seq_index]).astype(jnp.int32)
    weight = jnp.transpose(conv_weight[0], (1, 0, 2)).reshape(TAPS * C, C)
    starts = interval_starts
    token = jnp.zeros((8, 128), F32)

    ends = (0, sections - 1)
    near_pairs = [
        pair for pair in apart_pairs(sections, shards, 1) if pair[0] // shards in ends
    ]
    far_pairs = [
        (section * shards + place, section * shards + place + by)
        for section in ends
        for place in range(shards)
        for by in (1 if place % 2 else -1,)
        if 0 <= place + by < shards
    ]
    near, far, rest, token = edges_call(info, token, dna_embed)
    near = lax.ppermute(near, AXES, [pair for pair in near_pairs if pair[0] < shards])
    far = lax.ppermute(far, AXES, [pair for pair in far_pairs if pair[0] < shards])
    rest = lax.ppermute(rest, AXES, [pair for pair in far_pairs if pair[0] < shards])

    def relay(value, source, target):
        return lax.ppermute(value, AXES, section_pairs(source, target, shards))

    inputs = [[None] * windows for _ in range(4)]
    slopes = [[None] * windows for _ in range(4)]
    stacks = [[None] * windows for _ in range(4)]
    grads = [None] * windows
    dus = [None] * windows
    wide_du = [None] * windows
    arrived = [None] * windows
    side = None

    def forward(level, window, send=True):
        nonlocal token
        xs = (inputs[level][window],)
        if level == 0:
            xs = (dna_embed, near, rest if window else far)
        pooled, slopes[level][window], stacks[level][window], token = forward_call(
            level, window, info, starts, weight, token, *xs
        )
        if send:
            inputs[level + 1][window] = relay(pooled, level, level + 1)
        return pooled

    def turn(window, *held):
        nonlocal token
        send, grads[window], dus[window], stacks[3][window], token = last_call(
            window, info, starts, weight, turned, token, inputs[3][window], cotangent, near_cot, far_cot,
            *held,
        )
        if held:
            pairs = section_pairs(2, 3, shards) + section_pairs(3, 2, shards)
            arrived[window] = lax.ppermute(send, AXES, pairs)
        else:
            arrived[window] = relay(send, 3, 2)
        return arrived[window]

    def backward(level, window):
        nonlocal token
        send, grads[window], dus[window], token = backward_call(
            level, window, info, starts, turned, token, arrived[window], slopes[level][window],
            grads[window], dus[window],
        )
        arrived[window] = relay(send, level, level - 1)

    def arrive(window):
        nonlocal token
        wide_du[window], dus[window], token = first_du_call(
            info, token, arrived[window], slopes[0][window], dus[window]
        )

    def first_grad(window):
        nonlocal token
        grads[window], token = first_grad_call(
            window, info, starts, weight, token, wide_du[window], grads[window]
        )

    def sideways(level, *chosen):
        nonlocal side, token
        chosen = chosen or tuple(range(windows))
        xs = [stacks[level][window] for window in chosen]
        side, token = side_call(level, chosen, info, token, side, *xs)

    forward(0, 0)
    forward(0, 1)
    forward(0, 2)
    turned, token = turn_call(info, token, weight)
    near_cot, far_cot, token = cotangent_edges_call(info, token, cotangent)
    near_cot = lax.ppermute(near_cot, AXES, [pair for pair in near_pairs if pair[0] >= shards])
    far_cot = lax.ppermute(far_cot, AXES, [pair for pair in far_pairs if pair[0] >= shards])
    sideways(0)
    forward(1, 0)
    sideways(1, 0)
    forward(1, 1)
    forward(1, 2)
    sideways(1, 1, 2)
    forward(2, 0)
    inputs[3][1] = turn(0, forward(2, 1, send=False))
    forward(2, 2)
    backward(2, 0)
    turn(1)
    turn(2)
    backward(2, 1)
    backward(2, 2)
    sideways(3)
    sideways(2)
    backward(1, 0)
    backward(1, 1)
    backward(1, 2)
    arrive(0)
    first_grad(0)
    arrive(1)
    arrive(2)

    keeps, arriveds = [None, None], [None, None]

    def weigh(half):
        nonlocal token
        send, keeps[half], token = weight_call(half, token, side, dus)
        arriveds[half] = lax.ppermute(send, AXES, apart_pairs(sections, shards, 1))

    def pass_on(half, step):
        nonlocal token
        keeps[half], leaving, token = add_call(half, step, token, keeps[half], arriveds[half])
        axis, apart = PLANS[half][step][:2]
        arriveds[half] = lax.ppermute(leaving, AXES, mixed_pairs(sections, shards, axis, apart))

    weigh(0)
    weigh(1)
    pass_on(0, 0)
    pass_on(1, 0)
    first_grad(1)
    pass_on(0, 1)
    pass_on(1, 1)
    first_grad(2)
    pass_on(0, 2)
    pass_on(1, 2)
    input_grads, token = gather_call(token, grads)
    pass_on(0, 3)
    pass_on(1, 3)
    weight_grad, token = final_call(token, keeps[0], arriveds[0], keeps[1], arriveds[1])
    weight_grad = jnp.transpose(weight_grad, (1, 0, 2))[None]
    return (weight_grad, input_grads)


def solution(mesh):
    placed = (P(None, "seq", None), P("section", None, None, None), P(), P(None, "seq", None))
    return jax.shard_map(
        body,
        mesh=mesh,
        in_specs=placed,
        out_specs=(P("section", "seq", None, None), P("section", None, "seq", None)),
        check_vma=False,
    )
```

```python
import functools

import jax
import jax.numpy as jnp
from jax import lax
from jax.experimental import pallas as pl
from jax.experimental.pallas import tpu as pltpu
from jax.sharding import PartitionSpec as P

C = 768
TAPS = 5
AXES = ("section", "seq")
OWN = (256, 128, 64, 32)
HALO = (64, 32, 16, 8)
ROWS = (384, 192, 96, 48)
BACK_HALO = (16, 16, 16, 8)
BACK_ROWS = (288, 160, 96, 48)
SEND_ROWS = (0, 144, 80, 48)
CHUNK = 24
LIMIT = 16 * 1024 * 1024
F32 = jnp.float32
BF16 = jnp.bfloat16
ANY = pl.BlockSpec(memory_space=pl.ANY)
SMEM = pl.BlockSpec(memory_space=pltpu.SMEM)
VMEM = pl.BlockSpec(memory_space=pltpu.VMEM)
PIECES = (8, 7)
BLOCKS_UNROLL = 3


def shape_of(*dims, dtype=BF16):
    return jax.ShapeDtypeStruct(dims, dtype)


def call(kernel, name, flops, smem, vmem, outs, token, scratch, aliases=(), held=None, far_out=None):
    extra = () if held is None else (held,)
    operands = (*smem, *vmem, *extra, token)
    count = len(operands)
    pairs = {len(smem) + place: out for place, out in aliases}
    far_shape = held if held is not None else far_out
    far = () if far_shape is None else (shape_of(*far_shape.shape, dtype=far_shape.dtype),)
    if extra:
        pairs[count - 2] = len(outs)
    pairs[count - 1] = len(outs) + len(far)
    return pl.pallas_call(
        kernel,
        out_shape=(*outs, *far, jax.ShapeDtypeStruct(token.shape, token.dtype)),
        in_specs=[SMEM] * len(smem) + [VMEM] * len(vmem) + [ANY] * (len(extra) + 1),
        out_specs=(*[VMEM] * len(outs), *[ANY] * (len(far) + 1)),
        scratch_shapes=scratch,
        input_output_aliases=pairs,
        compiler_params=pltpu.CompilerParams(vmem_limit_bytes=LIMIT),
        cost_estimate=pl.CostEstimate(flops=int(flops) if name in ("edges", "forward0", "turn") else 1, bytes_accessed=1000000 if name in ("edges", "forward0", "turn") else 1, transcendentals=0),
        name=name,
    )(*operands)


def no_cut(starts, window, positions, level, length):
    cut = positions == length
    for entry in range(starts.shape[1]):
        first = (starts[window, entry] + ((1 << level) - 1)) >> level
        cut = cut | (positions == first)
    return jnp.where(cut, 0.0, 1.0)


def lanes(index, width, first=0):
    if isinstance(index, int):
        return slice(first + index * width, first + (index + 1) * width)
    return pl.ds(pl.multiple_of(first + index * width, 128), width)


def loop(count, run, unroll=1):
    if unroll == count:
        for index in range(count):
            run(index)
        return

    def step(index, carry):
        run(index)
        return carry

    lax.fori_loop(0, count, step, 0, unroll=unroll)


def roll_rows(value, by):
    return pltpu.roll(value, by % value.shape[0], 0)


def fill_masks(mask_ref, starts, window, seq, level, halo, rows):
    own = OWN[level]
    length = own * 32
    row = lax.broadcasted_iota(jnp.int32, (rows, 128), 0)
    positions = row + (seq * own - halo)
    inside = jnp.where((positions >= 0) & (positions < length), 1.0, 0.0)
    free = no_cut(starts, window, positions, level, length)
    before = inside * free
    after = inside * roll_rows(free, -1)
    mask_ref[0, 0:rows] = before * roll_rows(free, 1)
    mask_ref[1, 0:rows] = before
    mask_ref[2, 0:rows] = inside
    mask_ref[3, 0:rows] = after
    mask_ref[4, 0:rows] = after * roll_rows(free, -2)


def stack_inputs(read, mask_ref, stacked_ref, rows, steps=1):
    part = C // 128 // steps

    def columns(first):
        for index in [first * part + place for place in range(part)]:
            tile = read(lanes(index, 128)).astype(F32)
            for tap in range(TAPS):
                moved = roll_rows(tile, 2 - tap) if tap != 2 else tile
                stacked_ref[0:rows, lanes(index, 128, tap * C)] = (
                    moved * mask_ref[tap, 0:rows]
                ).astype(BF16)

    columns(0) if steps == 1 else loop(steps, columns)


def stack_grads(value_ref, mask_ref, stacked_ref, rows, steps=1):
    part = C // 128 // steps

    def columns(first):
        for index in [first * part + place for place in range(part)]:
            tile = value_ref[0:rows, lanes(index, 128)].astype(F32)
            for tap in range(TAPS):
                moved = tile * mask_ref[tap, 0:rows]
                moved = roll_rows(moved, tap - 2) if tap != 2 else moved
                stacked_ref[0:rows, lanes(index, 128, tap * C)] = moved.astype(BF16)

    columns(0) if steps == 1 else loop(steps, columns)


def conv_columns(stacked_ref, weight_ref, index):
    return jnp.dot(
        stacked_ref[...], weight_ref[:, lanes(index, 256)], preferred_element_type=F32
    )


def back_columns(stacked_ref, weight_ref, index, turned):
    if turned:
        return conv_columns(stacked_ref, weight_ref, index)
    total = None
    for tap in range(TAPS):
        part = lax.dot_general(
            stacked_ref[:, tap * C : (tap + 1) * C],
            weight_ref[lanes(index, 256, tap * C), :],
            (((1,), (1,)), ((), ())),
            preferred_element_type=F32,
        )
        total = part if total is None else total + part
    return total


def turn_kernel(info, weight, _, turned_out, _out, unit_v):
    @pl.when(info[0] > 0)
    def _():
        row = lax.broadcasted_iota(jnp.int32, (C, 128), 0)
        lane = lax.broadcasted_iota(jnp.int32, (C, 128), 1)
        for index in range(C // 128):
            unit_v[:, index * 128 : (index + 1) * 128] = jnp.where(
                row == lane + index * 128, 1.0, 0.0
            ).astype(BF16)

        def block(place):
            tap, index = place // 3, place % 3
            turned_out[lanes(tap, C), lanes(index, 256)] = lax.dot_general(
                unit_v[...],
                weight[lanes(place, 256), :],
                (((1,), (1,)), ((), ())),
                preferred_element_type=F32,
            ).astype(BF16)

        loop(TAPS * 3, block)


def turn_call(info, token, weight):
    return call(
        turn_kernel, "turn", 2 * C * C * C * TAPS, (info,), (weight,), (shape_of(TAPS * C, C),),
        token, [pltpu.VMEM((C, C), BF16)],
    )


def gelu_and_slope(u):
    scale = 0.7978845608028654
    square = u * u
    bend = jnp.tanh(scale * (u + 0.044715 * square * u))
    half = 0.5 * (1.0 + bend)
    slope = half + 0.5 * u * (1.0 - bend * bend) * (scale * (1.0 + 0.134145 * square))
    return u * half, slope


def fill_edges(odd, fill):
    pl.when(odd)(functools.partial(fill, True))
    pl.when(jnp.logical_not(odd))(functools.partial(fill, False))


def edges_kernel(windows, info, dna, _, near, first, rest, _out):
    own = OWN[0]

    def fill(leading_to_near):
        near_x, far_x = (0, own - 64) if leading_to_near else (own - 64, 0)

        @pl.when(info[0] == 0)
        def _():
            for window in range(windows):
                near[window * 64 : window * 64 + 64, :] = dna[window, near_x : near_x + 64, :]
                edge = dna[window, far_x : far_x + 64, :]
                if window == 0:
                    first[...] = edge
                else:
                    rest[(window - 1) * 64 : window * 64, :] = edge

    fill_edges(info[1] % 2 == 1, fill)


def edges_call(info, token, dna):
    windows = dna.shape[0]
    return call(
        functools.partial(edges_kernel, windows),
        "edges",
        2e10,
        (info,),
        (dna,),
        (shape_of(windows * 64, C), shape_of(64, C), shape_of((windows - 1) * 64, C)),
        token,
        [],
    )


def cotangent_edges_kernel(windows, info, cot, _, near, far, _out):
    part = cot.shape[1]

    def fill(leading_to_near):
        near_c, far_c = (0, part - 16) if leading_to_near else (part - 16, 0)

        @pl.when(info[0] == 3)
        def _():
            for window in range(windows):
                lines = slice(window * 16, window * 16 + 16)
                near[lines, :] = cot[window, near_c : near_c + 16, :]
                far[lines, :] = cot[window, far_c : far_c + 16, :]

    fill_edges(info[1] % 2 == 1, fill)


def cotangent_edges_call(info, token, cot):
    windows = cot.shape[0]
    edge = shape_of(windows * 16, C)
    return call(
        functools.partial(cotangent_edges_kernel, windows), "cotangent_edges", 1, (info,), (cot,),
        (edge, edge), token, [],
    )


def sides(odd, near, far):
    near, far = near.astype(F32), far.astype(F32)
    return jnp.where(odd, near, far), jnp.where(odd, far, near)


def with_edges(own, near, far, odd, low, high):
    ahead, behind = sides(odd, near, far)
    return jnp.concatenate([ahead[low:], own.astype(F32), behind[:high]], axis=0)


def forward_kernel(level, window, info, starts, *refs):
    rows, back = ROWS[level], BACK_ROWS[level]
    skip = HALO[level] - BACK_HALO[level]
    inputs = 3 if level == 0 else 1
    xs = refs[:inputs]
    weight, _, pooled_out, slope_out, stacked_v, _, mask_v, act_v = refs[inputs:]

    def read(cols):
        if level == 0:
            x_in, near, far = xs
            first = max(window - 1, 0) * 64
            return with_edges(
                x_in[window, :, cols],
                near[window * 64 : window * 64 + 64, cols],
                far[first : first + 64, cols],
                info[1] % 2 == 1,
                0,
                64,
            )
        return xs[0][:, cols]

    @pl.when(info[0] == level)
    def _():
        fill_masks(mask_v, starts, window, info[1], level, HALO[level], rows)
        stack_inputs(read, mask_v, stacked_v, rows)

        def block(index):
            act, slope = gelu_and_slope(conv_columns(stacked_v, weight, index))
            slope_out[:, lanes(index, 256)] = slope[skip : skip + back]
            for half in range(2):
                place = index * 2 + half
                act_v[place] = act[:, half * 128 : (half + 1) * 128]
                even = act_v[place, pl.ds(0, rows // 2, stride=2), :]
                odd = act_v[place, pl.ds(1, rows // 2, stride=2), :]
                pooled_out[:, lanes(place, 128)] = (0.5 * (even + odd)).astype(BF16)

        loop(C // 256, block, BLOCKS_UNROLL)


def forward_call(level, window, info, starts, weight, token, *xs):
    rows, back = ROWS[level], BACK_ROWS[level]
    return call(
        functools.partial(forward_kernel, level, window),
        f"forward{level}",
        2 * rows * C * C * TAPS,
        (info, starts),
        (*xs, weight),
        (shape_of(rows // 2, C), shape_of(back, C, dtype=F32), shape_of(rows, TAPS * C)),
        token,
        [
            pltpu.VMEM((TAPS, rows, 128), F32),
            pltpu.VMEM((C // 128, rows, 128), F32),
        ],
    )


def finish_backward(level, du_v, mask_v, stacked_v, weight, send_out, grad_out):
    rows, own, halo = BACK_ROWS[level], OWN[level], BACK_HALO[level]
    send = SEND_ROWS[level]
    trim = (rows - send) // 2
    stack_grads(du_v, mask_v, stacked_v, rows)

    def block(index):
        found = back_columns(stacked_v, weight, index, level > 0)
        cols = lanes(index, 256)
        if send:
            send_out[:, cols] = found[trim : trim + send].astype(BF16)
        grad_out[0:own, cols] = found[halo : halo + own].astype(BF16)

    loop(C // 256, block, BLOCKS_UNROLL)
    if own < 256:
        grad_out[own:, :] = jnp.zeros((256 - own, C), BF16)


def own_grads(level, du_v, du_out):
    own, halo = OWN[level], BACK_HALO[level]
    du_out[0:own, :] = du_v[halo : halo + own, :].astype(BF16)
    if own < 256:
        du_out[own:, :] = jnp.zeros((256 - own, C), BF16)


def last_kernel(window, info, starts, x_in, cot, near, far, weight, turned, *refs):
    send_out, grad_out, du_out, inputs_v, _, mask_v, stacked_v, du_v = refs[-8:]
    level, rows = 3, ROWS[3]
    if len(refs) == 10:

        @pl.when(info[0] == 2)
        def _():
            send_out[...] = refs[0][...]

    @pl.when(info[0] == level)
    def _():
        fill_masks(mask_v, starts, window, info[1], level, HALO[level], rows)
        stack_inputs(
            lambda cols: x_in[:, cols], mask_v, inputs_v, rows
        )

        def block(index):
            _, slope = gelu_and_slope(conv_columns(inputs_v, weight, index))
            cols = lanes(index, 256)
            lines = slice(window * 16, window * 16 + 16)
            g = with_edges(
                cot[window, :, cols], near[lines, cols], far[lines, cols], info[1] % 2 == 1, 8, 8
            )
            du_v[:, cols] = (g * slope).astype(BF16).astype(F32)

        loop(C // 256, block, BLOCKS_UNROLL)
        finish_backward(level, du_v, mask_v, stacked_v, turned, send_out, grad_out)
        own_grads(level, du_v, du_out)


def last_call(window, info, starts, weight, turned, token, x, cot, near, far, *held):
    rows = ROWS[3]
    return call(
        functools.partial(last_kernel, window),
        "last",
        4 * rows * C * C * TAPS,
        (info, starts),
        (x, cot, near, far, weight, turned, *held),
        (shape_of(rows, C), shape_of(256, C), shape_of(256, C), shape_of(rows, TAPS * C)),
        token,
        [
            pltpu.VMEM((TAPS, rows, 128), F32),
            pltpu.VMEM((rows, TAPS * C), BF16),
            pltpu.VMEM((rows, C), F32),
        ],
        aliases=((6, 0),) if held else (),
    )


def spread_grads(arrived, wide_v, slope, du_v, rows):
    def column(index):
        cols = lanes(index, 128)
        half = 0.5 * arrived[:, cols].astype(F32)
        wide_v[index, pl.ds(0, rows // 2, stride=2), :] = half
        wide_v[index, pl.ds(1, rows // 2, stride=2), :] = half
        du_v[:, cols] = (wide_v[index] * slope[:, cols]).astype(BF16).astype(F32)

    loop(C // 128, column, C // 128)


def keep_later(level, info, pairs):
    @pl.when(info[0] > level)
    def _():
        for source, target in pairs:
            target[...] = source[...]


def backward_kernel(level, window, info, starts, arrived, slope, weight, grad, du, _token,
                    send_out, grad_out, du_out, _out, wide_v, mask_v, stacked_v, du_v):
    rows = BACK_ROWS[level]
    keep_later(level, info, ((grad, grad_out), (du, du_out)))

    @pl.when(info[0] == level)
    def _():
        fill_masks(mask_v, starts, window, info[1], level, BACK_HALO[level], rows)
        spread_grads(arrived, wide_v, slope, du_v, rows)
        finish_backward(level, du_v, mask_v, stacked_v, weight, send_out, grad_out)
        own_grads(level, du_v, du_out)


def backward_call(level, window, info, starts, weight, token, arrived, slope, grad, du):
    rows = BACK_ROWS[level]
    return call(
        functools.partial(backward_kernel, level, window),
        f"backward{level}",
        2 * rows * C * C * TAPS,
        (info, starts),
        (arrived, slope, weight, grad, du),
        (shape_of(SEND_ROWS[level], C), shape_of(256, C), shape_of(256, C)),
        token,
        [
            pltpu.VMEM((C // 128, rows, 128), F32),
            pltpu.VMEM((TAPS, rows, 128), F32),
            pltpu.VMEM((rows, TAPS * C), BF16),
            pltpu.VMEM((rows, C), F32),
        ],
        aliases=((3, 1), (4, 2)),
    )


def first_du_kernel(info, arrived, slope, du, _token, all_out, du_out, _out, wide_v, du_v):
    rows = BACK_ROWS[0]
    keep_later(0, info, ((du, du_out),))

    @pl.when(info[0] == 0)
    def _():
        spread_grads(arrived, wide_v, slope, du_v, rows)
        own_grads(0, du_v, du_out)
        all_out[...] = du_v[...].astype(BF16)


def first_du_call(info, token, arrived, slope, du):
    rows = BACK_ROWS[0]
    return call(
        first_du_kernel,
        "first_du",
        rows * C * 8,
        (info,),
        (arrived, slope, du),
        (shape_of(rows, C), shape_of(256, C)),
        token,
        [pltpu.VMEM((C // 128, rows, 128), F32), pltpu.VMEM((rows, C), F32)],
        aliases=((2, 1),),
    )


def first_grad_kernel(window, info, starts, du, weight, grad, _token, grad_out, _out, mask_v,
                      stacked_v):
    rows = BACK_ROWS[0]
    keep_later(0, info, ((grad, grad_out),))

    @pl.when(info[0] == 0)
    def _():
        fill_masks(mask_v, starts, window, info[1], 0, BACK_HALO[0], rows)
        finish_backward(0, du, mask_v, stacked_v, weight, None, grad_out)


def first_grad_call(window, info, starts, weight, token, du, grad):
    rows = BACK_ROWS[0]
    return call(
        functools.partial(first_grad_kernel, window),
        "first_grad",
        2 * rows * C * C * TAPS,
        (info, starts),
        (du, weight, grad),
        (shape_of(256, C),),
        token,
        [pltpu.VMEM((TAPS, rows, 128), F32), pltpu.VMEM((rows, TAPS * C), BF16)],
        aliases=((2, 0),),
    )


def gather_kernel(windows, *refs):
    out = refs[-2]
    for window in range(windows):
        out[0, window] = refs[window][...]


def gather_call(token, grads):
    return call(
        functools.partial(gather_kernel, len(grads)), "gather", 1000000, (), tuple(grads),
        (shape_of(1, len(grads), 256, C),), token, [],
    )


def fill_order(seq, order_ref):
    row = lax.broadcasted_iota(jnp.int32, (C, 128), 0)
    place = (row * 2731) >> 16
    swap = (seq ^ (place >> 4)) & 1
    one, two = place & 3, (place >> 2) & 3
    along_z, along_y = jnp.where(swap == 1, two, one), jnp.where(swap == 1, one, two)
    apart = (along_y << 3) | (along_z << 1) | (place >> 4)
    source = CHUNK * (seq ^ apart) + (row - CHUNK * place)
    lane = lax.broadcasted_iota(jnp.int32, (C, 128), 1)
    for index in range(C // 128):
        order_ref[:, index * 128 : (index + 1) * 128] = jnp.where(
            source == lane + index * 128, 1.0, 0.0
        ).astype(BF16)


def side_kernel(level, windows, info, *refs):
    halo, own = HALO[level], OWN[level]
    count = len(windows)
    xs = refs[:count]
    side_out, _, order_v, side_v, sems = refs[-5:]
    total = count * own
    padding = -total % 128

    def leave(place):
        return pltpu.make_async_copy(
            side_v.at[place], side_out.at[:, lanes(windows[place], 256)], sems.at[place]
        )

    @pl.when(info[0] == level)
    def _():
        fill_order(info[1], order_v)

        def one_tap(tap):
            parts = [x[halo : halo + own, lanes(tap, C)] for x in xs]
            if padding:
                parts.append(jnp.zeros((padding, C), BF16))
            found = lax.dot_general(
                order_v[...],
                jnp.concatenate(parts, axis=0),
                (((1,), (1,)), ((), ())),
                preferred_element_type=F32,
            )
            for place in range(count):
                part = found[:, place * own : (place + 1) * own]
                if own < 256:
                    part = jnp.concatenate([part, jnp.zeros((C, 256 - own), F32)], axis=1)
                side_v[place, lanes(tap, C), :] = part.astype(BF16)

        loop(TAPS, one_tap)
        for place in range(count):
            leave(place).start()
        for place in range(count):
            leave(place).wait()


def side_call(level, windows, info, token, side, *xs):
    return call(
        functools.partial(side_kernel, level, windows),
        f"side{level}",
        2 * len(windows) * 256 * C * C * TAPS,
        (info,),
        xs,
        (),
        token,
        [
            pltpu.VMEM((C, C), BF16),
            pltpu.VMEM((len(windows), TAPS * C, 256), BF16),
            pltpu.SemaphoreType.DMA((len(windows),)),
        ],
        held=side,
        far_out=shape_of(TAPS * C, 3 * 256),
    )


def weight_kernel(half, side, *refs):
    dus = refs[:-5]
    _, send_out, keep_out, _, du_v = refs[-5:]
    first = sum(PIECES[:half])
    for window, du in enumerate(dus):
        du_v[window * 256 : (window + 1) * 256, :] = du[...]

    def one_piece(piece):
        place = first + piece
        tap, part = place // 3, place % 3
        found = jnp.dot(
            side[lanes(tap, C), :], du_v[:, lanes(part, 256)], preferred_element_type=F32
        ).reshape(2, 16, CHUNK, 256)
        cols = lanes(piece, 256)
        keep_out[:, :, cols] = found[0].astype(BF16)
        send_out[:, :, cols] = found[1].astype(BF16)

    loop(PIECES[half], one_piece, PIECES[half])


def weight_call(quarter, token, side, dus):
    width = PIECES[quarter] * 256
    shape = shape_of(16, CHUNK, width)
    return call(
        functools.partial(weight_kernel, quarter),
        f"weight{quarter}",
        2 * C * 768 * width,
        (),
        (side, *dus),
        (shape, shape),
        token,
        [pltpu.VMEM((len(dus) * 256, C), BF16)],
    )


def half_plan(one, two):
    held = [(second, first) for second in range(4) for first in range(4)]
    plan = []
    for axis, apart, gone in (
        (1, one, (one, 2)), (0, one, (one, 2)), (1, two, (two,)), (0, two, (two,))
    ):
        leaving = [place for place in held if place[axis] in gone]
        leaving.sort(key=lambda place: (place[1 - axis], gone.index(place[axis])))
        staying = []
        for place in leaving:
            moved = list(place)
            moved[axis] ^= apart
            staying.append(tuple(moved))
        plan.append(
            (
                axis,
                apart,
                [held.index(place) for place in leaving],
                [held.index(place) for place in staying],
            )
        )
        held = staying
    return plan


PLANS = (half_plan(1, 3), half_plan(3, 1))


def added(keep, arrived, source):
    return keep[source].astype(F32) + arrived[source].astype(F32)


def add_kernel(half, step, keep, arrived, _, stay_out, leave_out, _out):
    _, _, leaving, staying = PLANS[half][step]
    for target, sources in ((stay_out, staying), (leave_out, leaving)):
        for row, source in enumerate(sources):
            target[row] = added(keep, arrived, source).astype(BF16)


def add_call(half, step, token, keep, arrived):
    shape = shape_of(len(PLANS[half][step][2]), CHUNK, keep.shape[-1])
    return call(
        functools.partial(add_kernel, half, step),
        f"add{half}_{step}",
        4000000 // (1 << step),
        (),
        (keep, arrived),
        (shape, shape),
        token,
        [],
    )


def final_kernel(keep_a, arrived_a, keep_b, arrived_b, _, out, _out):
    for half, (keep, arrived) in enumerate(((keep_a, arrived_a), (keep_b, arrived_b))):
        total = added(keep, arrived, 0)
        piece = sum(PIECES[:half])
        for place in range(PIECES[half]):
            tap, part = divmod(piece + place, 3)
            out[tap, :, part * 256 : (part + 1) * 256] = total[:, place * 256 : (place + 1) * 256]


def final_call(token, *parts):
    return call(
        final_kernel, "final", 1, (), parts, (shape_of(TAPS, CHUNK, C, dtype=F32),), token, []
    )


def section_pairs(source, target, shards):
    return [(source * shards + place, target * shards + place) for place in range(shards)]


def apart_pairs(sections, shards, apart):
    return [
        (section * shards + place, section * shards + (place ^ apart))
        for section in range(sections)
        for place in range(shards)
    ]


def mixed_pairs(sections, shards, axis, apart):
    units = (8, 2) if axis == 0 else (2, 8)
    return [
        (section * shards + place, section * shards + (place ^ (apart * units[place % 2])))
        for section in range(sections)
        for place in range(shards)
    ]


def body(dna_embed, conv_weight, interval_starts, cotangent):
    windows = dna_embed.shape[0]
    sections = lax.axis_size("section")
    shards = lax.axis_size("seq")
    section_index = lax.axis_index("section")
    seq_index = lax.axis_index("seq")
    info = jnp.stack([section_index, seq_index]).astype(jnp.int32)
    weight = jnp.transpose(conv_weight[0], (1, 0, 2)).reshape(TAPS * C, C)
    starts = interval_starts
    token = jnp.zeros((8, 128), F32)

    ends = (0, sections - 1)
    near_pairs = [
        pair for pair in apart_pairs(sections, shards, 1) if pair[0] // shards in ends
    ]
    far_pairs = [
        (section * shards + place, section * shards + place + by)
        for section in ends
        for place in range(shards)
        for by in (1 if place % 2 else -1,)
        if 0 <= place + by < shards
    ]
    near, far, rest, token = edges_call(info, token, dna_embed)
    near = lax.ppermute(near, AXES, [pair for pair in near_pairs if pair[0] < shards])
    far = lax.ppermute(far, AXES, [pair for pair in far_pairs if pair[0] < shards])
    rest = lax.ppermute(rest, AXES, [pair for pair in far_pairs if pair[0] < shards])

    def relay(value, source, target):
        return lax.ppermute(value, AXES, section_pairs(source, target, shards))

    inputs = [[None] * windows for _ in range(4)]
    slopes = [[None] * windows for _ in range(4)]
    stacks = [[None] * windows for _ in range(4)]
    grads = [None] * windows
    dus = [None] * windows
    wide_du = [None] * windows
    arrived = [None] * windows
    side = None

    def forward(level, window, send=True):
        nonlocal token
        xs = (inputs[level][window],)
        if level == 0:
            xs = (dna_embed, near, rest if window else far)
        pooled, slopes[level][window], stacks[level][window], token = forward_call(
            level, window, info, starts, weight, token, *xs
        )
        if send:
            inputs[level + 1][window] = relay(pooled, level, level + 1)
        return pooled

    def turn(window, *held):
        nonlocal token
        send, grads[window], dus[window], stacks[3][window], token = last_call(
            window, info, starts, weight, turned, token, inputs[3][window], cotangent, near_cot, far_cot,
            *held,
        )
        if held:
            pairs = section_pairs(2, 3, shards) + section_pairs(3, 2, shards)
            arrived[window] = lax.ppermute(send, AXES, pairs)
        else:
            arrived[window] = relay(send, 3, 2)
        return arrived[window]

    def backward(level, window):
        nonlocal token
        send, grads[window], dus[window], token = backward_call(
            level, window, info, starts, turned, token, arrived[window], slopes[level][window],
            grads[window], dus[window],
        )
        arrived[window] = relay(send, level, level - 1)

    def arrive(window):
        nonlocal token
        wide_du[window], dus[window], token = first_du_call(
            info, token, arrived[window], slopes[0][window], dus[window]
        )

    def first_grad(window):
        nonlocal token
        grads[window], token = first_grad_call(
            window, info, starts, weight, token, wide_du[window], grads[window]
        )

    def sideways(level, *chosen):
        nonlocal side, token
        chosen = chosen or tuple(range(windows))
        xs = [stacks[level][window] for window in chosen]
        side, token = side_call(level, chosen, info, token, side, *xs)

    forward(0, 0)
    forward(0, 1)
    forward(0, 2)
    turned, token = turn_call(info, token, weight)
    near_cot, far_cot, token = cotangent_edges_call(info, token, cotangent)
    near_cot = lax.ppermute(near_cot, AXES, [pair for pair in near_pairs if pair[0] >= shards])
    far_cot = lax.ppermute(far_cot, AXES, [pair for pair in far_pairs if pair[0] >= shards])
    sideways(0)
    forward(1, 0)
    sideways(1, 0)
    forward(1, 1)
    forward(1, 2)
    sideways(1, 1, 2)
    forward(2, 0)
    inputs[3][1] = turn(0, forward(2, 1, send=False))
    forward(2, 2)
    turn(1)
    backward(2, 0)
    turn(2)
    backward(2, 1)
    backward(2, 2)
    sideways(3)
    sideways(2)
    backward(1, 0)
    backward(1, 1)
    backward(1, 2)
    arrive(0)
    first_grad(0)
    arrive(1)
    arrive(2)

    keeps, arriveds = [None, None], [None, None]

    def weigh(half):
        nonlocal token
        send, keeps[half], token = weight_call(half, token, side, dus)
        arriveds[half] = lax.ppermute(send, AXES, apart_pairs(sections, shards, 1))

    def pass_on(half, step):
        nonlocal token
        keeps[half], leaving, token = add_call(half, step, token, keeps[half], arriveds[half])
        axis, apart = PLANS[half][step][:2]
        arriveds[half] = lax.ppermute(leaving, AXES, mixed_pairs(sections, shards, axis, apart))

    weigh(0)
    weigh(1)
    pass_on(0, 0)
    pass_on(1, 0)
    first_grad(1)
    pass_on(0, 1)
    pass_on(1, 1)
    first_grad(2)
    pass_on(0, 2)
    pass_on(1, 2)
    input_grads, token = gather_call(token, grads)
    pass_on(0, 3)
    pass_on(1, 3)
    weight_grad, token = final_call(token, keeps[0], arriveds[0], keeps[1], arriveds[1])
    weight_grad = jnp.transpose(weight_grad, (1, 0, 2))[None]
    return (weight_grad, input_grads)


def solution(mesh):
    placed = (P(None, "seq", None), P("section", None, None, None), P(), P(None, "seq", None))
    return jax.shard_map(
        body,
        mesh=mesh,
        in_specs=placed,
        out_specs=(P("section", "seq", None, None), P("section", None, "seq", None)),
        check_vma=False,
    )
```
